32 devices in a mesh: section: 2 (over y), batch: 16 (over z, x, core).
Axes of the slice: x: 2, y: 2, z: 4, core: 2. Of those that a mesh axis runs over, the one named last changes fastest.
Arguments:
- tokens: bfloat16 [256, 128, 512], P('batch'), may hold values from -6 to 6
- start_steps: int32 [256], P('batch'), may hold values from 0 to 20
- cond_counts: int32 [256], P('batch'), may hold values from 1 to 8
- valid_steps: int32 [256], P('batch'), may hold values from 4 to 21
- qkv_weight: bfloat16 [2, 512, 1536], P('section'), may hold values from -0.25 to 0.25
- out_weight: bfloat16 [2, 512, 512], P('section'), may hold values from -1 to 1
- up_weight: bfloat16 [2, 512, 2048], P('section'), may hold values from -0.25 to 0.25
- down_weight: bfloat16 [2, 2048, 512], P('section'), may hold values from -0.125 to 0.125
- norm_gains: float32 [2, 2, 512], P('section'), may hold values from 0.1 to 1.9
- cotangent: bfloat16 [256, 128, 512], P('batch'), may hold values from -6 to 6
Outputs:
- layer_outputs: bfloat16 [2, 256, 128, 512], P('section', 'batch')
- input_grads: bfloat16 [2, 256, 128, 512], P('section', 'batch')
- qkv_grad: float32 [2, 512, 1536], P('section')
- out_grad: float32 [2, 512, 512], P('section')
- up_grad: float32 [2, 512, 2048], P('section')
- down_grad: float32 [2, 2048, 512], P('section')
- gain_grad: float32 [2, 2, 512], P('section')
The draws below stay inside these ranges and needn't reach their ends.
All inputs are finite; a program needn't handle non-finite values.
Results may differ from the reference program's by a relative error of at most 0.015.
Values may be sent and summed in bfloat16 or wider, within the bound.
A program may use at most 192 MiB of HBM per device.

```python
import math
import jax
import jax.numpy as jnp
from jax import lax

HEADS = 8
HEAD_DIM = 64
D = 512
FF = 2048
SLOTS = 128
STEPS = 21
STEP_TOKENS = 6
SEQS = 256


def set_ends(drawn, rng, low, largest):
    longest = drawn.shape.index(max(drawn.shape))
    spots = []
    for shift in (0, 1):
        where = [jax.random.randint(jax.random.fold_in(rng, axis), (), 0, length) for axis, length in enumerate(drawn.shape)]
        where[longest] = (where[longest] + shift) % drawn.shape[longest]
        spots.append(tuple(where))
    return drawn.at[spots[0]].set(low).at[spots[1]].set(largest)


def levels(key, extent, split, low, top_value):
    loudness = 1.0
    for dim, shards_of in split:
        steps = jax.random.uniform(jax.random.fold_in(jax.random.fold_in(key, 6), dim), (shards_of,), jnp.float32, low / len(split), top_value / len(split))
        loudness = loudness * jnp.repeat(jnp.exp(steps), extent[dim] // shards_of).reshape((-1,) + (1,) * (len(extent) - 1 - dim))
    return loudness


def bell_draw(own_key, extent, deviation, limit, shards=(), kind=jnp.bfloat16):
    entries = deviation * jax.random.normal(own_key, extent, jnp.float32)
    if shards:
        entries = entries * levels(own_key, extent, shards, -0.22, 0.18)
    return jnp.clip(entries, -limit, limit).astype(kind)


def setup_inputs(seed: int = 0) -> dict:
    seeds = jax.random.split(jax.random.key(seed), 11)
    tokens = bell_draw(seeds[0], (SEQS, SLOTS, D), 1.0, 6.0, ((0, 16),))
    start_steps = set_ends(jax.random.randint(seeds[1], (SEQS,), 0, STEPS), jax.random.fold_in(seeds[1], 1), 0, STEPS - 1).astype(jnp.int32)
    cond_counts = set_ends(jax.random.randint(seeds[2], (SEQS,), 1, 9), jax.random.fold_in(seeds[2], 1), 1, 8).astype(jnp.int32)
    valid_steps = set_ends(jax.random.randint(seeds[3], (SEQS,), 4, STEPS + 1), jax.random.fold_in(seeds[3], 1), 4, STEPS).astype(jnp.int32)
    qkv_weight = bell_draw(seeds[4], (2, D, 3 * D), D ** -0.5, 0.25, ((0, 2),))
    out_weight = bell_draw(seeds[5], (2, D, D), (D // 16) ** -0.5, 1.0, ((0, 2),))
    up_weight = bell_draw(seeds[6], (2, D, FF), D ** -0.5, 0.25, ((0, 2),))
    down_weight = bell_draw(seeds[7], (2, FF, D), FF ** -0.5, 0.125, ((0, 2),))
    norm_gains = jnp.clip(1.0 + 0.18 * jax.random.normal(seeds[8], (2, 2, D), jnp.float32), 0.1, 1.9)
    cotangent = bell_draw(seeds[9], (SEQS, SLOTS, D), 1.0, 6.0, ((0, 16),))
    return {"tokens": tokens, "start_steps": start_steps, "cond_counts": cond_counts, "valid_steps": valid_steps, "qkv_weight": qkv_weight, "out_weight": out_weight, "up_weight": up_weight, "down_weight": down_weight, "norm_gains": norm_gains, "cotangent": cotangent}


@jax.custom_vjp
def low(v):
    return lax.optimization_barrier(v.astype(jnp.bfloat16)).astype(jnp.float32)

@jax.custom_vjp
def low_back(v):
    return v

def low_keep(v):
    return (low(v), None)

def low_pass(kept, grad):
    return (grad,)

def back_keep(v):
    return (v, None)

def back_low(kept, grad):
    return (low(grad),)
low.defvjp(low_keep, low_pass)
low_back.defvjp(back_keep, back_low)
HIGHEST = lax.Precision.HIGHEST
NEGATIVE = -1e+30

def normalize(values, gain):
    row_mean = lax.optimization_barrier(jnp.mean(values, axis=-1, keepdims=True))
    centered = values - row_mean
    spread = lax.optimization_barrier(jnp.mean(centered * centered, axis=-1, keepdims=True))
    return centered * lax.rsqrt(spread + 1e-05) * gain

def allowed_mask(rollout, context, filled):
    slot_ids = jnp.arange(SLOTS, dtype=jnp.int32)
    step_of = slot_ids // STEP_TOKENS
    causal = step_of[None, :] <= step_of[:, None]
    live_keys = slot_ids[None, None, :] < (filled * STEP_TOKENS)[:, None, None]
    recent = step_of[None, None, :] >= (rollout - context)[:, None, None]
    diagonal = slot_ids[:, None] == slot_ids[None, :]
    return causal[None] & live_keys & recent | diagonal[None]

def block_forward(inputs_f, qkv_w, out_w, up_w, down_w, gain_pair, allowed):
    group_size = inputs_f.shape[0]
    normed_one = low(normalize(inputs_f, gain_pair[0]))
    projected = low(low_back(jnp.einsum('gsd,de->gse', normed_one, qkv_w, precision=HIGHEST)))
    query_rows = projected[..., :D].reshape(group_size, SLOTS, HEADS, HEAD_DIM)
    key_rows = projected[..., D:2 * D].reshape(group_size, SLOTS, HEADS, HEAD_DIM)
    value_rows = projected[..., 2 * D:].reshape(group_size, SLOTS, HEADS, HEAD_DIM)
    raw_scores = jnp.einsum('gqhd,gkhd->ghqk', query_rows, key_rows, precision=HIGHEST) * HEAD_DIM ** (-0.5)
    scores = low_back(jnp.where(allowed[:, None], raw_scores, NEGATIVE))
    row_max = lax.optimization_barrier(jnp.max(scores, axis=-1, keepdims=True))
    exponent = jnp.exp(scores - row_max)
    weights_p = exponent / lax.optimization_barrier(jnp.sum(exponent, axis=-1, keepdims=True))
    mixed_rows = jnp.einsum('ghqk,gkhd->gqhd', low(weights_p), value_rows, precision=HIGHEST)
    mixed_rows = low(low_back(mixed_rows.reshape(group_size, SLOTS, D)))
    residual = inputs_f + low_back(jnp.einsum('gsd,de->gse', mixed_rows, out_w, precision=HIGHEST))
    normed_two = low(normalize(residual, gain_pair[1]))
    pre_act = low_back(jnp.einsum('gsd,df->gsf', normed_two, up_w, precision=HIGHEST))
    activated = low(jax.nn.gelu(pre_act, approximate=True))
    return residual + low_back(jnp.einsum('gsf,fd->gsd', activated, down_w, precision=HIGHEST))

def reference(tokens, start_steps, cond_counts, valid_steps, qkv_weight, out_weight, up_weight, down_weight, norm_gains, cotangent):
    params = (qkv_weight.astype(jnp.float32), out_weight.astype(jnp.float32), up_weight.astype(jnp.float32), down_weight.astype(jnp.float32), norm_gains.astype(jnp.float32))
    group_size = math.gcd(SEQS, 32)
    group_count = SEQS // group_size
    pieces = (tokens.reshape(group_count, group_size, SLOTS, D), cotangent.reshape(group_count, group_size, SLOTS, D), start_steps.reshape(group_count, group_size), cond_counts.reshape(group_count, group_size), valid_steps.reshape(group_count, group_size))

    def one_group(totals, piece_set):
        token_rows, cot_rows, rollout, context, filled = piece_set
        allowed = allowed_mask(rollout, context, filled)

        def both_layers(inputs_f, boundary, weights):
            first_out = block_forward(inputs_f, *[w[0] for w in weights], allowed)
            second_in = low(low_back(first_out)) + boundary
            second_out = block_forward(second_in, *[w[1] for w in weights], allowed)
            return (second_out, first_out)
        inputs_f = token_rows.astype(jnp.float32)
        boundary = jnp.zeros_like(inputs_f)
        (second_out, first_out), pullback = jax.vjp(both_layers, inputs_f, boundary, params)
        grad_in, grad_boundary, grad_params = pullback((cot_rows.astype(jnp.float32), jnp.zeros_like(first_out)))
        totals = jax.tree.map(lambda a, b: a + b, totals, grad_params)
        outputs = (first_out.astype(jnp.bfloat16), second_out.astype(jnp.bfloat16), grad_in.astype(jnp.bfloat16), grad_boundary.astype(jnp.bfloat16))
        return (totals, outputs)
    start_totals = jax.tree.map(jnp.zeros_like, params)
    totals, outputs = lax.scan(one_group, start_totals, pieces)
    first_out, second_out, grad_in, grad_boundary = [o.reshape(SEQS, SLOTS, D) for o in outputs]
    layer_outputs = jnp.stack([first_out, second_out])
    input_grads = jnp.stack([grad_in, grad_boundary])
    return (layer_outputs, input_grads, totals[0], totals[1], totals[2], totals[3], totals[4])
```

```python
import functools

import jax
import jax.numpy as jnp
from jax import lax
from jax.experimental import pallas as pl
from jax.experimental.pallas import tpu as pltpu
from jax.sharding import PartitionSpec as P

HEADS = 8
HEAD_DIM = 64
SLOTS = 128
STEP_TOKENS = 6
PAIR = 2 * HEAD_DIM
NEGATIVE = -1e30
EPS = 1e-05
SCALE = HEAD_DIM ** (-0.5)
GELU_A = 0.7978845608028654
GELU_B = 0.7978845608028654 * 0.044715
CHUNK = 2
MESH = pl.DeviceIdType.MESH
BF = jnp.bfloat16
F32 = jnp.float32


def dot(a, b):
    return jnp.dot(a, b, preferred_element_type=F32)


def dot_t(a, b):
    return lax.dot_general(a, b, (((1,), (1,)), ((), ())), preferred_element_type=F32)


def t_dot(a, b):
    return lax.dot_general(a, b, (((0,), (0,)), ((), ())), preferred_element_type=F32)


def layer_kernel(
    seqs,
    start_ref,
    cond_ref,
    valid_ref,
    tok_ref,
    cot_ref,
    qkv_w,
    out_w,
    up_w,
    down_w,
    gain_ref,
    y_out,
    dx_out,
    grad_out,
    gain_out,
    x_buf,
    d_buf,
    y_buf,
    g_buf,
    n1_buf,
    z_buf,
    p_buf,
    o_buf,
    n2_buf,
    act_buf,
    der_buf,
    da_buf,
    rs_buf,
    lhs_t,
    stage,
    gain_acc,
    in_sem,
    send_sem,
    recv_sem,
    yo_sem,
    xo_sem,
    go_sem,
):
    section = lax.axis_index("section")
    batch = lax.axis_index("batch")
    first = section == 0
    second = section == 1
    partner = (1 - section, batch)
    d = x_buf.shape[1]
    ff = act_buf.shape[1]
    rows = CHUNK * SLOTS
    chunks = seqs // CHUNK
    total = seqs * SLOTS

    load_x = pltpu.make_async_copy(tok_ref, x_buf, in_sem)
    load_d = pltpu.make_async_copy(cot_ref, d_buf, in_sem)

    @pl.when(first)
    def _():
        load_x.start()

    @pl.when(second)
    def _():
        load_d.start()

    barrier = pltpu.get_barrier_semaphore()
    pl.semaphore_signal(barrier, inc=1, device_id=partner, device_id_type=MESH)

    gain_acc[...] = jnp.zeros_like(gain_acc)

    @pl.when(first)
    def _():
        load_x.wait()

    @pl.when(second)
    def _():
        load_d.wait()

    pl.semaphore_wait(barrier, 1)

    lane = lax.broadcasted_iota(jnp.int32, (1, PAIR), 1)
    low = jnp.where(lane < HEAD_DIM, 1.0, 0.0).astype(BF)
    high = jnp.where(lane < HEAD_DIM, 0.0, 1.0).astype(BF)
    scale = jnp.asarray(SCALE, BF)
    key_id = lax.broadcasted_iota(jnp.int32, (SLOTS, SLOTS), 1)
    row_id = lax.broadcasted_iota(jnp.int32, (SLOTS, SLOTS), 0)
    key_step = (key_id * 43) >> 8
    row_step = (row_id * 43) >> 8
    causal = key_step <= row_step
    diagonal = key_id == row_id
    gain0 = gain_ref[0:1, :]
    gain1 = gain_ref[1:2, :]

    def chunk_rows(i):
        return pl.ds(pl.multiple_of(i * rows, rows), rows)

    def to_second(i):
        r = chunk_rows(i)
        return pltpu.make_async_remote_copy(
            src_ref=y_buf.at[r],
            dst_ref=x_buf.at[r],
            send_sem=send_sem.at[i],
            recv_sem=recv_sem.at[i],
            device_id=partner,
            device_id_type=MESH,
        )

    def to_first(i):
        r = chunk_rows(i)
        return pltpu.make_async_remote_copy(
            src_ref=g_buf.at[r],
            dst_ref=d_buf.at[r],
            send_sem=send_sem.at[i],
            recv_sem=recv_sem.at[i],
            device_id=partner,
            device_id_type=MESH,
        )

    def store_y(i):
        r = chunk_rows(i)
        return pltpu.make_async_copy(y_buf.at[r], y_out.at[r], yo_sem.at[i])

    def store_dx(i):
        r = chunk_rows(i)
        return pltpu.make_async_copy(g_buf.at[r], dx_out.at[r], xo_sem.at[i])

    def norm(v, gain):
        mean = jnp.mean(v, axis=-1, keepdims=True)
        c = v - mean
        var = jnp.mean(c * c, axis=-1, keepdims=True)
        rs = lax.rsqrt(var + EPS)
        return (c * rs * gain).astype(BF), rs

    def norm_back(dn, n, gain, rs):
        xhat = n.astype(F32) * (1.0 / gain)
        w = dn * gain
        dgain = jnp.sum((dn * xhat).reshape(rows // 8, 8, d), axis=0)
        m1 = jnp.mean(w, axis=-1, keepdims=True)
        m2 = jnp.mean(w * xhat, axis=-1, keepdims=True)
        return rs * (w - m1 - xhat * m2), dgain

    def halves(v):
        return jnp.concatenate([v * low, v * high], axis=0)

    def forward(i):
        r = chunk_rows(i)
        x = x_buf[r, :].astype(F32)
        n1, rs1 = norm(x, gain0)
        n1_buf[r, :] = n1
        rs_buf[r, 0:1] = rs1
        for c in range(3):
            z_buf[r, c * d : (c + 1) * d] = dot(n1, qkv_w[:, c * d : (c + 1) * d]).astype(BF)
        for s in range(CHUNK):
            seq = i * CHUNK + s
            rs = pl.ds(pl.multiple_of(seq * SLOTS, SLOTS), SLOTS)
            live = key_id < valid_ref[seq] * STEP_TOKENS
            recent = key_step >= start_ref[seq] - cond_ref[seq]
            allowed = (causal & live & recent) | diagonal
            for p in range(HEADS // 2):
                cq = pl.ds(p * PAIR, PAIR)
                ck = pl.ds(d + p * PAIR, PAIR)
                cv = pl.ds(2 * d + p * PAIR, PAIR)
                q = z_buf[rs, cq] * scale
                sc = dot_t(q, halves(z_buf[rs, ck]))
                parts = []
                for h in range(2):
                    sh = jnp.where(allowed, sc[:, h * SLOTS : (h + 1) * SLOTS], NEGATIVE)
                    e = jnp.exp(sh - jnp.max(sh, axis=-1, keepdims=True))
                    parts.append((e / jnp.sum(e, axis=-1, keepdims=True)).astype(BF))
                pr = jnp.concatenate(parts, axis=1)
                p_buf[rs, p * 2 * SLOTS : (p + 1) * 2 * SLOTS] = pr
                o_buf[rs, cq] = dot(pr, halves(z_buf[rs, cv])).astype(BF)
        h = x + dot(o_buf[r, :], out_w[...])
        n2, rs2 = norm(h, gain1)
        n2_buf[r, :] = n2
        rs_buf[r, 1:2] = rs2
        for f in range(0, ff, d):
            u = dot(n2, up_w[:, f : f + d])
            sq = u * u
            t = jnp.tanh(u * (GELU_A + GELU_B * sq))
            hs = 0.5 + 0.5 * t
            act_buf[r, f : f + d] = (u * hs).astype(BF)
            der_buf[r, f : f + d] = (
                hs + (u * (2.0 * GELU_A + 6.0 * GELU_B * sq)) * (hs * (1.0 - hs))
            ).astype(BF)
        y_buf[r, :] = (h + dot(act_buf[r, :], down_w[...])).astype(BF)

    def backward(i):
        r = chunk_rows(i)
        dm = d_buf[r, :]
        for f in range(0, ff, d):
            dg = dot_t(dm, down_w[f : f + d, :])
            der_buf[r, f : f + d] = (der_buf[r, f : f + d].astype(F32) * dg).astype(BF)
        dn2 = dot_t(der_buf[r, :], up_w[...])
        dh_norm, dgain1 = norm_back(dn2, n2_buf[r, :], gain1, rs_buf[r, 1:2])
        gain_acc[1] += dgain1
        dh = dm.astype(F32) + dh_norm
        da = dh.astype(BF)
        da_buf[r, :] = da
        dout = dot_t(da, out_w[...]).astype(BF)
        for s in range(CHUNK):
            seq = i * CHUNK + s
            rs = pl.ds(pl.multiple_of(seq * SLOTS, SLOTS), SLOTS)
            for p in range(HEADS // 2):
                cq = pl.ds(p * PAIR, PAIR)
                ck = pl.ds(d + p * PAIR, PAIR)
                cv = pl.ds(2 * d + p * PAIR, PAIR)
                do = dout[s * SLOTS : (s + 1) * SLOTS, p * PAIR : (p + 1) * PAIR]
                pr = p_buf[rs, p * 2 * SLOTS : (p + 1) * 2 * SLOTS]
                dp = dot_t(do, halves(z_buf[rs, cv]))
                parts = []
                for h in range(2):
                    dph = dp[:, h * SLOTS : (h + 1) * SLOTS]
                    ph = pr[:, h * SLOTS : (h + 1) * SLOTS].astype(F32)
                    inner = jnp.sum(ph * dph, axis=-1, keepdims=True)
                    parts.append((ph * (dph - inner)).astype(BF))
                ds = jnp.concatenate(parts, axis=1)
                ds_rows = jnp.concatenate(parts, axis=0)
                pr_rows = jnp.concatenate([pr[:, :SLOTS], pr[:, SLOTS:]], axis=0)
                q = z_buf[rs, cq] * scale
                k = z_buf[rs, ck] * scale
                dq = dot(ds, halves(k))
                dk = t_dot(ds_rows, halves(q))
                dv = t_dot(pr_rows, halves(do))
                z_buf[rs, cq] = dq.astype(BF)
                z_buf[rs, ck] = dk.astype(BF)
                z_buf[rs, cv] = dv.astype(BF)
        dn1 = dot_t(z_buf[r, :], qkv_w[...])
        dx_norm, dgain0 = norm_back(dn1, n1_buf[r, :], gain0, rs_buf[r, 0:1])
        gain_acc[0] += dgain0
        g_buf[r, :] = (dh + dx_norm).astype(BF)

    def step(t, carry):
        forth = jnp.where(first, t < chunks, t % 2 == 0)
        i = jnp.where(first, t % chunks, t // 2)

        @pl.when(forth)
        def _():
            @pl.when(second)
            def _():
                to_second(i).wait_recv()

            forward(i)

            @pl.when(first)
            def _():
                to_second(i).start()

            store_y(i).start()

        @pl.when(jnp.logical_not(forth))
        def _():
            @pl.when(first)
            def _():
                to_first(i).wait_recv()

            backward(i)

            @pl.when(second)
            def _():
                to_first(i).start()

            store_dx(i).start()

        return carry

    lax.fori_loop(0, 2 * chunks, step, 0)

    def block_copy(slot, b):
        return pltpu.make_async_copy(
            stage.at[slot], grad_out.at[pl.ds(pl.multiple_of(b * d, d), d)], go_sem.at[slot]
        )

    def emit(b, value):
        slot = b % 2
        if not isinstance(b, int) or b >= 2:
            block_copy(slot, b - 2).wait()
        stage[slot] = value.astype(BF)
        block_copy(slot, b).start()

    lhs_t[...] = n1_buf[...].T
    for c in range(3):
        emit(c, dot(lhs_t[...], z_buf[:, c * d : (c + 1) * d]))
    lhs_t[...] = o_buf[...].T
    emit(3, dot(lhs_t[...], da_buf[...]))
    lhs_t[...] = n2_buf[...].T
    for c in range(ff // d):
        emit(4 + c, dot(lhs_t[...], der_buf[:, c * d : (c + 1) * d]))

    base = 4 + ff // d
    for c in range(ff // d):
        lhs_t[...] = act_buf[:, c * d : (c + 1) * d].T
        emit(base + c, dot(lhs_t[...], d_buf[...]))
    gain_out[...] = jnp.sum(gain_acc[...], axis=1)
    for b in (base + ff // d - 2, base + ff // d - 1):
        block_copy(b % 2, b).wait()

    def finish(i, carry):
        @pl.when(first)
        def _():
            to_second(i).wait_send()

        @pl.when(second)
        def _():
            to_first(i).wait_send()

        store_y(i).wait()
        store_dx(i).wait()
        return carry

    lax.fori_loop(0, chunks, finish, 0)


def local(
    tokens,
    start_steps,
    cond_counts,
    valid_steps,
    qkv_weight,
    out_weight,
    up_weight,
    down_weight,
    norm_gains,
    cotangent,
):
    seqs, slots, d = tokens.shape
    ff = up_weight.shape[2]
    rows = seqs * slots
    chunks = seqs // CHUNK
    vmem = pl.BlockSpec(memory_space=pltpu.VMEM)
    smem = pl.BlockSpec(memory_space=pltpu.SMEM)
    hbm = pl.BlockSpec(memory_space=pl.ANY)
    blocks = 4 + 2 * (ff // d)
    y, dx, grads, gains = pl.pallas_call(
        functools.partial(layer_kernel, seqs),
        out_shape=(
            jax.ShapeDtypeStruct((rows, d), BF),
            jax.ShapeDtypeStruct((rows, d), BF),
            jax.ShapeDtypeStruct((blocks * d, d), BF),
            jax.ShapeDtypeStruct((2, d), F32),
        ),
        in_specs=[smem] * 3 + [hbm] * 2 + [vmem] * 5,
        out_specs=(hbm, hbm, hbm, vmem),
        scratch_shapes=[
            pltpu.VMEM((rows, d), BF),
            pltpu.VMEM((rows, d), BF),
            pltpu.VMEM((rows, d), BF),
            pltpu.VMEM((rows, d), BF),
            pltpu.VMEM((rows, d), BF),
            pltpu.VMEM((rows, 3 * d), BF),
            pltpu.VMEM((rows, HEADS * SLOTS), BF),
            pltpu.VMEM((rows, d), BF),
            pltpu.VMEM((rows, d), BF),
            pltpu.VMEM((rows, ff), BF),
            pltpu.VMEM((rows, ff), BF),
            pltpu.VMEM((rows, d), BF),
            pltpu.VMEM((rows, 2), F32),
            pltpu.VMEM((d, rows), BF),
            pltpu.VMEM((2, d, d), BF),
            pltpu.VMEM((2, 8, d), F32),
            pltpu.SemaphoreType.DMA,
            pltpu.SemaphoreType.DMA((chunks,)),
            pltpu.SemaphoreType.DMA((chunks,)),
            pltpu.SemaphoreType.DMA((chunks,)),
            pltpu.SemaphoreType.DMA((chunks,)),
            pltpu.SemaphoreType.DMA((2,)),
        ],
        compiler_params=pltpu.CompilerParams(
            collective_id=0, has_side_effects=True, vmem_limit_bytes=60 * 2**20
        ),
        name="layer",
    )(
        start_steps,
        cond_counts,
        valid_steps,
        tokens.reshape(rows, d),
        cotangent.reshape(rows, d),
        qkv_weight[0],
        out_weight[0],
        up_weight[0],
        down_weight[0],
        norm_gains[0],
    )
    grads, gains = lax.psum((grads.astype(F32), gains), "batch")
    parts = [grads[b * d : (b + 1) * d] for b in range(blocks)]
    qkv_grad = jnp.concatenate(parts[:3], axis=1)
    up_grad = jnp.concatenate(parts[4 : 4 + ff // d], axis=1)
    down_grad = grads[(4 + ff // d) * d :]
    shape = (1, seqs, slots, d)
    return (
        y.reshape(shape),
        dx.reshape(shape),
        qkv_grad[None],
        parts[3][None],
        up_grad[None],
        down_grad[None],
        gains[None],
    )


def solution(mesh):
    rows = P("batch", None, None)
    flat = P("batch")
    layer = P("section", None, None)
    in_specs = (rows, flat, flat, flat, layer, layer, layer, layer, layer, rows)
    both = P("section", "batch", None, None)
    out_specs = (both, both, layer, layer, layer, layer, layer)
    return jax.shard_map(local, mesh=mesh, in_specs=in_specs, out_specs=out_specs, check_vma=False)
```

```python
import functools

import jax
import jax.numpy as jnp
from jax import lax
from jax.experimental import pallas as pl
from jax.experimental.pallas import tpu as pltpu
from jax.sharding import PartitionSpec as P

HEADS = 8
HEAD_DIM = 64
SLOTS = 128
STEP_TOKENS = 6
PAIR = 2 * HEAD_DIM
NEGATIVE = -1e30
EPS = 1e-05
SCALE = HEAD_DIM ** (-0.5)
GELU_A = 0.7978845608028654
GELU_B = 0.7978845608028654 * 0.044715
CHUNK = 2
MESH = pl.DeviceIdType.MESH
BF = jnp.bfloat16
F32 = jnp.float32


def dot(a, b):
    return jnp.dot(a, b, preferred_element_type=F32)


def dot_t(a, b):
    return lax.dot_general(a, b, (((1,), (1,)), ((), ())), preferred_element_type=F32)


def t_dot(a, b):
    return lax.dot_general(a, b, (((0,), (0,)), ((), ())), preferred_element_type=F32)


def layer_kernel(
    seqs,
    chips,
    start_ref,
    cond_ref,
    valid_ref,
    tok_ref,
    cot_ref,
    qkv_w,
    out_w,
    up_w,
    down_w,
    gain_ref,
    y_out,
    dx_out,
    qkv_out,
    out_out,
    up_out,
    down_out,
    gain_out,
    x_buf,
    d_buf,
    y_buf,
    n1_buf,
    z_buf,
    p_buf,
    o_buf,
    n2_buf,
    act_buf,
    der_buf,
    da_buf,
    rs_buf,
    lhs_t,
    grads,
    sib,
    gain_acc,
    gain_own,
    gain_sib,
    gain_all,
    in_sem,
    send_sem,
    recv_sem,
    yo_sem,
    xo_sem,
    sib_send,
    sib_recv,
    ring_send,
    rs_recv,
    ag_recv,
    fwd_send,
    fwd_recv,
    gain_send,
    gain_recv,
    gsib_sem,
    go_sem,
    ready,
    freed,
):
    section = lax.axis_index("section")
    batch = lax.axis_index("batch")
    first = section == 0
    second = section == 1
    partner = (1 - section, batch)
    core = lax.rem(batch, 2)
    chip = batch // 2
    half_ring = chips // 2
    place = jnp.where(chip % 2 == 0, chip // 2, chips - 1 - chip // 2)

    def at_place(p):
        c = jnp.where(p < half_ring, 2 * p, 2 * (chips - 1 - p) + 1)
        return (section, 2 * c + core)

    right = at_place(lax.rem(place + 1, chips))
    left = at_place(lax.rem(place + chips - 1, chips))
    ahead = (right, left)
    sibling = (section, batch + 1 - 2 * core)
    segments = grads.shape[0]
    prow = grads.shape[3]
    d = x_buf.shape[1]
    ff = act_buf.shape[1]
    rows = CHUNK * SLOTS
    chunks = seqs // CHUNK
    total = seqs * SLOTS

    load_x = pltpu.make_async_copy(tok_ref, x_buf, in_sem)
    load_d = pltpu.make_async_copy(cot_ref, d_buf, in_sem)

    @pl.when(first)
    def _():
        load_x.start()

    @pl.when(second)
    def _():
        load_d.start()

    barrier = pltpu.get_barrier_semaphore()
    for other in (partner, sibling, left, right):
        pl.semaphore_signal(barrier, inc=1, device_id=other, device_id_type=MESH)

    gain_acc[...] = jnp.zeros_like(gain_acc)

    @pl.when(first)
    def _():
        load_x.wait()

    @pl.when(second)
    def _():
        load_d.wait()

    pl.semaphore_wait(barrier, 4)

    lane = lax.broadcasted_iota(jnp.int32, (1, PAIR), 1)
    low = jnp.where(lane < HEAD_DIM, 1.0, 0.0).astype(BF)
    high = jnp.where(lane < HEAD_DIM, 0.0, 1.0).astype(BF)
    scale = jnp.asarray(SCALE, BF)
    key_id = lax.broadcasted_iota(jnp.int32, (SLOTS, SLOTS), 1)
    row_id = lax.broadcasted_iota(jnp.int32, (SLOTS, SLOTS), 0)
    key_step = (key_id * 43) >> 8
    row_step = (row_id * 43) >> 8
    causal = key_step <= row_step
    diagonal = key_id == row_id
    gain0 = gain_ref[0:1, :]
    gain1 = gain_ref[1:2, :]

    def chunk_rows(i):
        return pl.ds(pl.multiple_of(i * rows, rows), rows)

    def to_second(i):
        r = chunk_rows(i)
        return pltpu.make_async_remote_copy(
            src_ref=y_buf.at[r],
            dst_ref=x_buf.at[r],
            send_sem=send_sem.at[i],
            recv_sem=recv_sem.at[i],
            device_id=partner,
            device_id_type=MESH,
        )

    def to_first(i):
        r = chunk_rows(i)
        return pltpu.make_async_remote_copy(
            src_ref=x_buf.at[r],
            dst_ref=d_buf.at[r],
            send_sem=send_sem.at[i],
            recv_sem=recv_sem.at[i],
            device_id=partner,
            device_id_type=MESH,
        )

    def store_y(i):
        r = chunk_rows(i)
        return pltpu.make_async_copy(y_buf.at[r], y_out.at[r], yo_sem.at[i])

    def store_dx(i):
        r = chunk_rows(i)
        return pltpu.make_async_copy(x_buf.at[r], dx_out.at[r], xo_sem.at[i])

    def norm(v, gain):
        mean = jnp.mean(v, axis=-1, keepdims=True)
        c = v - mean
        var = jnp.mean(c * c, axis=-1, keepdims=True)
        rs = lax.rsqrt(var + EPS)
        return (c * rs * gain).astype(BF), rs

    def norm_back(dn, n, gain, rs):
        xhat = n.astype(F32) * (1.0 / gain)
        w = dn * gain
        dgain = jnp.sum((dn * xhat).reshape(rows // 8, 8, d), axis=0)
        m1 = jnp.mean(w, axis=-1, keepdims=True)
        m2 = jnp.mean(w * xhat, axis=-1, keepdims=True)
        return rs * (w - m1 - xhat * m2), dgain

    def halves(v):
        return jnp.concatenate([v * low, v * high], axis=0)

    def forward(i):
        r = chunk_rows(i)
        x = x_buf[r, :].astype(F32)
        n1, rs1 = norm(x, gain0)
        n1_buf[r, :] = n1
        rs_buf[r, 0:1] = rs1
        for c in range(3):
            z_buf[r, c * d : (c + 1) * d] = dot(n1, qkv_w[:, c * d : (c + 1) * d]).astype(BF)
        for s in range(CHUNK):
            seq = i * CHUNK + s
            rs = pl.ds(pl.multiple_of(seq * SLOTS, SLOTS), SLOTS)
            live = key_id < valid_ref[seq] * STEP_TOKENS
            recent = key_step >= start_ref[seq] - cond_ref[seq]
            allowed = (causal & live & recent) | diagonal
            for p in range(HEADS // 2):
                cq = pl.ds(p * PAIR, PAIR)
                ck = pl.ds(d + p * PAIR, PAIR)
                cv = pl.ds(2 * d + p * PAIR, PAIR)
                q = z_buf[rs, cq] * scale
                sc = dot_t(q, halves(z_buf[rs, ck]))
                parts = []
                for h in range(2):
                    sh = jnp.where(allowed, sc[:, h * SLOTS : (h + 1) * SLOTS], NEGATIVE)
                    e = jnp.exp(sh - jnp.max(sh, axis=-1, keepdims=True))
                    parts.append((e / jnp.sum(e, axis=-1, keepdims=True)).astype(BF))
                pr = jnp.concatenate(parts, axis=1)
                p_buf[seq * (HEADS // 2) + p] = pr
                o_buf[rs, cq] = dot(pr, halves(z_buf[rs, cv])).astype(BF)
        h = x + dot(o_buf[r, :], out_w[...])
        n2, rs2 = norm(h, gain1)
        n2_buf[r, :] = n2
        rs_buf[r, 1:2] = rs2
        for f in range(0, ff, d):
            u = dot(n2, up_w[:, f : f + d])
            sq = u * u
            t = jnp.tanh(u * (GELU_A + GELU_B * sq))
            hs = 0.5 + 0.5 * t
            act_buf[r, f : f + d] = (u * hs).astype(BF)
            der_buf[r, f : f + d] = (
                hs + (u * (2.0 * GELU_A + 6.0 * GELU_B * sq)) * (hs * (1.0 - hs))
            ).astype(BF)
        y_buf[r, :] = (h + dot(act_buf[r, :], down_w[...])).astype(BF)

    def backward(i):
        r = chunk_rows(i)
        dm = d_buf[r, :]
        for f in range(0, ff, d):
            dg = dot_t(dm, down_w[f : f + d, :])
            der_buf[r, f : f + d] = (der_buf[r, f : f + d].astype(F32) * dg).astype(BF)
        dn2 = dot_t(der_buf[r, :], up_w[...])
        dh_norm, dgain1 = norm_back(dn2, n2_buf[r, :], gain1, rs_buf[r, 1:2])
        gain_acc[1] += dgain1
        dh = dm.astype(F32) + dh_norm
        da = dh.astype(BF)
        da_buf[r, :] = da
        dout = dot_t(da, out_w[...]).astype(BF)
        for s in range(CHUNK):
            seq = i * CHUNK + s
            rs = pl.ds(pl.multiple_of(seq * SLOTS, SLOTS), SLOTS)
            for p in range(HEADS // 2):
                cq = pl.ds(p * PAIR, PAIR)
                ck = pl.ds(d + p * PAIR, PAIR)
                cv = pl.ds(2 * d + p * PAIR, PAIR)
                do = dout[s * SLOTS : (s + 1) * SLOTS, p * PAIR : (p + 1) * PAIR]
                pr = p_buf[seq * (HEADS // 2) + p]
                dp = dot_t(do, halves(z_buf[rs, cv]))
                parts = []
                for h in range(2):
                    dph = dp[:, h * SLOTS : (h + 1) * SLOTS]
                    ph = pr[:, h * SLOTS : (h + 1) * SLOTS].astype(F32)
                    inner = jnp.sum(ph * dph, axis=-1, keepdims=True)
                    parts.append((ph * (dph - inner)).astype(BF))
                ds = jnp.concatenate(parts, axis=1)
                ds_rows = jnp.concatenate(parts, axis=0)
                pr_rows = jnp.concatenate([pr[:, :SLOTS], pr[:, SLOTS:]], axis=0)
                q = z_buf[rs, cq] * scale
                k = z_buf[rs, ck] * scale
                dq = dot(ds, halves(k))
                dk = t_dot(ds_rows, halves(q))
                dv = t_dot(pr_rows, halves(do))
                z_buf[rs, cq] = dq.astype(BF)
                z_buf[rs, ck] = dk.astype(BF)
                z_buf[rs, cv] = dv.astype(BF)
        dn1 = dot_t(z_buf[r, :], qkv_w[...])
        dx_norm, dgain0 = norm_back(dn1, n1_buf[r, :], gain0, rs_buf[r, 0:1])
        gain_acc[0] += dgain0
        x_buf[r, :] = (dh + dx_norm).astype(BF)

    half = total // 2
    blocks = ff // d
    per = d // (2 * prow)

    def put(seg, c, value, h):
        where = pl.ds(c * per, per)
        value = value.reshape(per, 2, prow, d)
        if h is not None:
            value = value + jnp.where(h == 0, 0.0, 1.0) * grads[seg, where].astype(F32)
        grads[seg, where] = value.astype(BF)

    def weight_grads(h, r, between):
        for c in range(blocks):
            lhs_t[...] = act_buf[r, c * d : (c + 1) * d].T
            put(0, c, dot(lhs_t[...], d_buf[r, :]), h)
            between(0, c)
        lhs_t[...] = n2_buf[r, :].T
        for c in range(blocks):
            put(1, c, dot(lhs_t[...], der_buf[r, c * d : (c + 1) * d]), h)
            between(1, c)
        lhs_t[...] = n1_buf[r, :].T
        for c in range(3):
            put(2, c, dot(lhs_t[...], z_buf[r, c * d : (c + 1) * d]), h)
            between(2, c)
        lhs_t[...] = o_buf[r, :].T
        put(2, 3, dot(lhs_t[...], da_buf[r, :]), h)
        between(2, 3)

    def step(t, carry):
        mid = chunks + chunks // 2
        kind0 = jnp.where(t < chunks, 0, jnp.where((t == mid) | (t == 2 * chunks + 1), 2, 1))
        i0 = jnp.where(t < chunks, t, jnp.where(t < mid, t - chunks, t - chunks - 1))
        kind1 = jnp.where(t < 2 * chunks, t % 2, 2)
        kind = jnp.where(first, kind0, kind1)
        i = jnp.where(first, i0, t // 2)
        h = jnp.where(t == 2 * chunks + 1, 1, 0)

        @pl.when(kind == 0)
        def _():
            @pl.when(second)
            def _():
                to_second(i).wait_recv()

            forward(i)

            @pl.when(first)
            def _():
                to_second(i).start()

            store_y(i).start()

        @pl.when(kind == 1)
        def _():
            @pl.when(first)
            def _():
                to_first(i).wait_recv()
                to_second(i).wait_send()

            backward(i)

            @pl.when(second)
            def _():
                to_first(i).start()

            store_dx(i).start()

        @pl.when(kind == 2)
        def _():
            r = pl.ds(pl.multiple_of(h * half, half), half)
            weight_grads(h, r, lambda seg, c: None)

        return carry

    lax.fori_loop(0, 2 * chunks + 2, step, 0)
    for other in (left, right):
        pl.semaphore_signal(ready, inc=1, device_id=other, device_id_type=MESH)

    width = d // 2
    per_block = SLOTS // prow

    def columns(way):
        return pl.ds(way * width, width)

    def exchange(seg):
        return pltpu.make_async_remote_copy(
            src_ref=grads.at[seg, :, 1 - core],
            dst_ref=sib.at[seg],
            send_sem=sib_send.at[seg],
            recv_sem=sib_recv.at[seg],
            device_id=sibling,
            device_id_type=MESH,
        )

    def landing(seg, way, s):
        q = (seg * 2 + way) * (chips - 1) + s
        row = pl.multiple_of((q % per_block) * prow, prow)
        return p_buf.at[q // per_block, pl.ds(row, prow)]

    def ring(src, dst, seg, way, recv):
        return pltpu.make_async_remote_copy(
            src_ref=src,
            dst_ref=dst,
            send_sem=ring_send.at[seg, way],
            recv_sem=recv,
            device_id=ahead[way],
            device_id_type=MESH,
        )

    def gather_copy(seg, way, k, s):
        spot = grads.at[seg, k, core, :, columns(way)]
        return ring(spot, spot, seg, way, ag_recv.at[seg, way, s])

    def forward_copy(seg, way, k, f):
        spot = grads.at[seg, k, core, :, columns(way)]
        return pltpu.make_async_remote_copy(
            src_ref=spot,
            dst_ref=spot,
            send_sem=fwd_send.at[seg, way],
            recv_sem=fwd_recv.at[seg, way, f],
            device_id=sibling,
            device_id_type=MESH,
        )

    def first_copy(seg, way):
        return ring(
            sib.at[seg, place, :, columns(way)],
            landing(seg, way, 0),
            seg,
            way,
            rs_recv.at[seg, way, 0],
        )

    def ring_start(seg):
        exchange(seg).wait()
        mine = grads[seg, place, core].astype(F32) + sib[seg, place].astype(F32)
        sib[seg, place] = mine.astype(BF)
        for way in range(2):
            first_copy(seg, way).start()

    def reduce_tick(seg, s, last):
        for way in range(2):
            if way == 0:
                k = lax.rem(place + 2 * chips - 1 - s, chips)
            else:
                k = lax.rem(place + 1 + s, chips)
            here = landing(seg, way, s)
            ring(here, here, seg, way, rs_recv.at[seg, way, s]).wait()
            value = (
                here[...].astype(F32)
                + grads[seg, k, core, :, columns(way)].astype(F32)
                + sib[seg, k, :, columns(way)].astype(F32)
            ).astype(BF)
            if last:
                grads[seg, k, core, :, columns(way)] = value
                gather_copy(seg, way, k, 0).start()
                forward_copy(seg, way, k, 0).start()
            else:
                here[...] = value
                ring(
                    here, landing(seg, way, s + 1), seg, way, rs_recv.at[seg, way, s + 1]
                ).start()

    def gather_tick(seg, s, last):
        for way in range(2):
            k = lax.rem(place + chips - s, chips) if way == 0 else lax.rem(place + s, chips)
            gather_copy(seg, way, k, s).wait()
            if not last:
                gather_copy(seg, way, k, s + 1).start()
            forward_copy(seg, way, k, 0).wait_send()
            forward_copy(seg, way, k, s + 1).start()

    def gain_copy(s):
        spot = gain_all.at[lax.rem(place + chips - s, chips)]
        return pltpu.make_async_remote_copy(
            src_ref=spot,
            dst_ref=spot,
            send_sem=gain_send,
            recv_sem=gain_recv.at[s],
            device_id=right,
            device_id_type=MESH,
        )

    gain_swap = pltpu.make_async_remote_copy(
        src_ref=gain_own,
        dst_ref=gain_sib,
        send_sem=gsib_sem.at[0],
        recv_sem=gsib_sem.at[1],
        device_id=sibling,
        device_id_type=MESH,
    )
    gain_own[...] = jnp.zeros_like(gain_own)
    gain_own[0:2, :] = jnp.sum(gain_acc[...], axis=1)
    gain_swap.start()
    for seg in range(segments):
        exchange(seg).start()
    gain_swap.wait()
    gain_all[place] = gain_own[...] + gain_sib[...]
    pl.semaphore_wait(ready, 2)
    gain_copy(0).start()
    for seg in range(segments):
        ring_start(seg)
    pl.semaphore_signal(freed, inc=1, device_id=sibling, device_id_type=MESH)

    def reduce_step(s, carry):
        for seg in range(segments):
            reduce_tick(seg, s, False)
        gain_copy(s).wait()
        gain_copy(s + 1).start()
        return carry

    lax.fori_loop(0, chips - 2, reduce_step, 0)
    pl.semaphore_wait(freed, 1)
    for seg in range(segments):
        reduce_tick(seg, chips - 2, True)
    gain_copy(chips - 2).wait()

    def gather_step(s, carry):
        for seg in range(segments):
            gather_tick(seg, s, False)
        return carry

    lax.fori_loop(0, chips - 2, gather_step, 0)
    for seg in range(segments):
        gather_tick(seg, chips - 2, True)

    gains = gain_all[0]
    for k in range(1, chips):
        gains = gains + gain_all[k]
    gain_out[...] = gains[0:2, :]

    def results(seg):
        if seg == 0:
            return [pltpu.make_async_copy(grads.at[0], down_out, go_sem.at[0])]
        copies = []
        for c in range(blocks):
            if seg == 1:
                dst = up_out.at[:, :, :, c * d : (c + 1) * d]
            elif c < 3:
                dst = qkv_out.at[:, :, :, c * d : (c + 1) * d]
            else:
                dst = out_out
            src = grads.at[seg, pl.ds(c * per, per)]
            copies.append(pltpu.make_async_copy(src, dst, go_sem.at[blocks * seg + c]))
        return copies

    for seg in range(segments):
        for way in range(2):
            forward_copy(seg, way, 0, 0).wait_send()

        def arrived(f, carry, seg=seg):
            for way in range(2):
                forward_copy(seg, way, 0, f).wait_recv()
            return carry

        lax.fori_loop(0, chips, arrived, 0)
        for copy in results(seg):
            copy.start()
    for seg in range(segments):
        for copy in results(seg):
            copy.wait()

    def finish(i, carry):
        @pl.when(second)
        def _():
            to_first(i).wait_send()

        store_y(i).wait()
        store_dx(i).wait()
        return carry

    lax.fori_loop(0, chunks, finish, 0)


def local(
    tokens,
    start_steps,
    cond_counts,
    valid_steps,
    qkv_weight,
    out_weight,
    up_weight,
    down_weight,
    norm_gains,
    cotangent,
):
    seqs, slots, d = tokens.shape
    ff = up_weight.shape[2]
    rows = seqs * slots
    chunks = seqs // CHUNK
    chips = lax.axis_size("batch") // 2
    segments = 3
    prow = ff // (2 * chips)
    per = d // (2 * prow)
    vmem = pl.BlockSpec(memory_space=pltpu.VMEM)
    smem = pl.BlockSpec(memory_space=pltpu.SMEM)
    hbm = pl.BlockSpec(memory_space=pl.ANY)
    y, dx, qkv_grad, out_grad, up_grad, down_grad, gains = pl.pallas_call(
        functools.partial(layer_kernel, seqs, chips),
        out_shape=(
            jax.ShapeDtypeStruct((rows, d), BF),
            jax.ShapeDtypeStruct((rows, d), BF),
            jax.ShapeDtypeStruct((per, 2, prow, 3 * d), BF),
            jax.ShapeDtypeStruct((per, 2, prow, d), BF),
            jax.ShapeDtypeStruct((per, 2, prow, ff), BF),
            jax.ShapeDtypeStruct((chips, 2, prow, d), BF),
            jax.ShapeDtypeStruct((2, d), F32),
        ),
        in_specs=[smem] * 3 + [hbm] * 2 + [vmem] * 5,
        out_specs=(hbm, hbm, hbm, hbm, hbm, hbm, vmem),
        scratch_shapes=[
            pltpu.VMEM((rows, d), BF),
            pltpu.VMEM((rows, d), BF),
            pltpu.VMEM((rows, d), BF),
            pltpu.VMEM((rows, d), BF),
            pltpu.VMEM((rows, 3 * d), BF),
            pltpu.VMEM((seqs * HEADS // 2, SLOTS, 2 * SLOTS), BF),
            pltpu.VMEM((rows, d), BF),
            pltpu.VMEM((rows, d), BF),
            pltpu.VMEM((rows, ff), BF),
            pltpu.VMEM((rows, ff), BF),
            pltpu.VMEM((rows, d), BF),
            pltpu.VMEM((rows, 2), F32),
            pltpu.VMEM((d, rows // 2), BF),
            pltpu.VMEM((segments, chips, 2, prow, d), BF),
            pltpu.VMEM((segments, chips, prow, d), BF),
            pltpu.VMEM((2, 8, d), F32),
            pltpu.VMEM((8, d), F32),
            pltpu.VMEM((8, d), F32),
            pltpu.VMEM((chips, 8, d), F32),
            pltpu.SemaphoreType.DMA,
            pltpu.SemaphoreType.DMA((chunks,)),
            pltpu.SemaphoreType.DMA((chunks,)),
            pltpu.SemaphoreType.DMA((chunks,)),
            pltpu.SemaphoreType.DMA((chunks,)),
            pltpu.SemaphoreType.DMA((segments,)),
            pltpu.SemaphoreType.DMA((segments,)),
            pltpu.SemaphoreType.DMA((segments, 2)),
            pltpu.SemaphoreType.DMA((segments, 2, chips - 1)),
            pltpu.SemaphoreType.DMA((segments, 2, chips - 1)),
            pltpu.SemaphoreType.DMA((segments, 2)),
            pltpu.SemaphoreType.DMA((segments, 2, chips)),
            pltpu.SemaphoreType.DMA,
            pltpu.SemaphoreType.DMA((chips - 1,)),
            pltpu.SemaphoreType.DMA((2,)),
            pltpu.SemaphoreType.DMA((segments * ff // d,)),
            pltpu.SemaphoreType.REGULAR,
            pltpu.SemaphoreType.REGULAR,
        ],
        compiler_params=pltpu.CompilerParams(
            collective_id=0, has_side_effects=True, vmem_limit_bytes=63 * 2**20
        ),
        name="layer",
    )(
        start_steps,
        cond_counts,
        valid_steps,
        tokens.reshape(rows, d),
        cotangent.reshape(rows, d),
        qkv_weight[0],
        out_weight[0],
        up_weight[0],
        down_weight[0],
        norm_gains[0],
    )
    shape = (1, seqs, slots, d)
    return (
        y.reshape(shape),
        dx.reshape(shape),
        qkv_grad.reshape(qkv_weight.shape).astype(F32),
        out_grad.reshape(out_weight.shape).astype(F32),
        up_grad.reshape(up_weight.shape).astype(F32),
        down_grad.reshape(down_weight.shape).astype(F32),
        gains[None],
    )


def solution(mesh):
    rows = P("batch", None, None)
    flat = P("batch")
    layer = P("section", None, None)
    in_specs = (rows, flat, flat, flat, layer, layer, layer, layer, layer, rows)
    both = P("section", "batch", None, None)
    out_specs = (both, both, layer, layer, layer, layer, layer)
    return jax.shard_map(local, mesh=mesh, in_specs=in_specs, out_specs=out_specs, check_vma=False)
```

```python
import functools

import jax
import jax.numpy as jnp
from jax import lax
from jax.experimental import pallas as pl
from jax.experimental.pallas import tpu as pltpu
from jax.sharding import PartitionSpec as P

HEADS = 8
HEAD_DIM = 64
SLOTS = 128
STEP_TOKENS = 6
PAIR = 2 * HEAD_DIM
NEGATIVE = -1e30
EPS = 1e-05
SCALE = HEAD_DIM ** (-0.5)
GELU_A = 0.7978845608028654
GELU_B = 0.7978845608028654 * 0.044715
CHUNK = 2
MESH = pl.DeviceIdType.MESH
BF = jnp.bfloat16
F32 = jnp.float32


def dot(a, b):
    return jnp.dot(a, b, preferred_element_type=F32)


def dot_t(a, b):
    return lax.dot_general(a, b, (((1,), (1,)), ((), ())), preferred_element_type=F32)


def t_dot(a, b):
    return lax.dot_general(a, b, (((0,), (0,)), ((), ())), preferred_element_type=F32)


def layer_kernel(
    seqs,
    chips,
    start_ref,
    cond_ref,
    valid_ref,
    tok_ref,
    cot_ref,
    qkv_w,
    out_w,
    up_w,
    down_w,
    gain_ref,
    y_out,
    dx_out,
    qkv_out,
    out_out,
    up_out,
    down_out,
    gain_out,
    x_buf,
    d_buf,
    y_buf,
    n1_buf,
    z_buf,
    p_buf,
    o_buf,
    n2_buf,
    act_buf,
    der_buf,
    da_buf,
    rs_buf,
    do_buf,
    dz_buf,
    lhs_t,
    grads,
    sib,
    gain_acc,
    gain_own,
    gain_sib,
    gain_all,
    in_sem,
    send_sem,
    recv_sem,
    yo_sem,
    xo_sem,
    sib_send,
    sib_recv,
    ring_send,
    rs_recv,
    ag_recv,
    fwd_send,
    fwd_recv,
    gain_send,
    gain_recv,
    gsib_sem,
    go_sem,
    ready,
    freed,
):
    section = lax.axis_index("section")
    batch = lax.axis_index("batch")
    first = section == 0
    second = section == 1
    partner = (1 - section, batch)
    core = lax.rem(batch, 2)
    chip = batch // 2
    half_ring = chips // 2
    place = jnp.where(chip % 2 == 0, chip // 2, chips - 1 - chip // 2)

    def at_place(p):
        c = jnp.where(p < half_ring, 2 * p, 2 * (chips - 1 - p) + 1)
        return (section, 2 * c + core)

    right = at_place(lax.rem(place + 1, chips))
    left = at_place(lax.rem(place + chips - 1, chips))
    ahead = (right, left)
    sibling = (section, batch + 1 - 2 * core)
    segments = grads.shape[0]
    prow = grads.shape[3]
    d = x_buf.shape[1]
    ff = act_buf.shape[1]
    rows = CHUNK * SLOTS
    chunks = seqs // CHUNK
    total = seqs * SLOTS

    load_x = pltpu.make_async_copy(tok_ref, x_buf, in_sem)
    load_d = pltpu.make_async_copy(cot_ref, d_buf, in_sem)

    @pl.when(first)
    def _():
        load_x.start()

    @pl.when(second)
    def _():
        load_d.start()

    barrier = pltpu.get_barrier_semaphore()
    for other in (partner, sibling, left, right):
        pl.semaphore_signal(barrier, inc=1, device_id=other, device_id_type=MESH)

    gain_acc[...] = jnp.zeros_like(gain_acc)

    @pl.when(first)
    def _():
        load_x.wait()

    @pl.when(second)
    def _():
        load_d.wait()

    pl.semaphore_wait(barrier, 4)

    lane = lax.broadcasted_iota(jnp.int32, (1, PAIR), 1)
    low = jnp.where(lane < HEAD_DIM, 1.0, 0.0).astype(BF)
    high = jnp.where(lane < HEAD_DIM, 0.0, 1.0).astype(BF)
    head_row = lax.broadcasted_iota(jnp.int32, (2 * SLOTS, PAIR), 0) < SLOTS
    head_lane = lax.broadcasted_iota(jnp.int32, (2 * SLOTS, PAIR), 1) < HEAD_DIM
    minus = jnp.where(head_row == head_lane, -1.0, 0.0).astype(BF)
    scale = jnp.asarray(SCALE, BF)
    key_id = lax.broadcasted_iota(jnp.int32, (SLOTS, SLOTS), 1)
    row_id = lax.broadcasted_iota(jnp.int32, (SLOTS, SLOTS), 0)
    key_step = (key_id * 43) >> 8
    row_step = (row_id * 43) >> 8
    causal = key_step <= row_step
    diagonal = key_id == row_id
    gain0 = gain_ref[0:1, :]
    gain1 = gain_ref[1:2, :]

    def chunk_rows(i):
        return pl.ds(pl.multiple_of(i * rows, rows), rows)

    def to_second(i):
        r = chunk_rows(i)
        return pltpu.make_async_remote_copy(
            src_ref=y_buf.at[r],
            dst_ref=x_buf.at[r],
            send_sem=send_sem.at[i],
            recv_sem=recv_sem.at[i],
            device_id=partner,
            device_id_type=MESH,
        )

    def to_first(i):
        r = chunk_rows(i)
        return pltpu.make_async_remote_copy(
            src_ref=x_buf.at[r],
            dst_ref=d_buf.at[r],
            send_sem=send_sem.at[i],
            recv_sem=recv_sem.at[i],
            device_id=partner,
            device_id_type=MESH,
        )

    def store_y(i):
        r = chunk_rows(i)
        return pltpu.make_async_copy(y_buf.at[r], y_out.at[r], yo_sem.at[i])

    def store_dx(i):
        r = chunk_rows(i)
        return pltpu.make_async_copy(x_buf.at[r], dx_out.at[r], xo_sem.at[i])

    def norm(v, gain):
        mean = jnp.mean(v, axis=-1, keepdims=True)
        c = v - mean
        var = jnp.mean(c * c, axis=-1, keepdims=True)
        rs = lax.rsqrt(var + EPS)
        return (c * rs * gain).astype(BF), rs

    def norm_back(dn, n, gain, rs):
        xhat = n.astype(F32) * (1.0 / gain)
        w = dn * gain
        dgain = jnp.sum((dn * xhat).reshape(rows // 8, 8, d), axis=0)
        m1 = jnp.mean(w, axis=-1, keepdims=True)
        m2 = jnp.mean(w * xhat, axis=-1, keepdims=True)
        return rs * (w - m1 - xhat * m2), dgain

    def halves(v):
        return jnp.concatenate([v * low, v * high], axis=0)

    def turned(v):
        return jnp.concatenate([v[:, :SLOTS].T, v[:, SLOTS:].T], axis=1)

    def forward(i):
        r = chunk_rows(i)
        x = x_buf[r, :].astype(F32)
        n1, rs1 = norm(x, gain0)
        n1_buf[r, :] = n1
        rs_buf[r, 0:1] = rs1
        for c in range(3):
            z_buf[r, c * d : (c + 1) * d] = dot(n1, qkv_w[:, c * d : (c + 1) * d]).astype(BF)
        for s in range(CHUNK):
            seq = i * CHUNK + s
            rs = pl.ds(pl.multiple_of(seq * SLOTS, SLOTS), SLOTS)
            live = key_id < valid_ref[seq] * STEP_TOKENS
            recent = key_step >= start_ref[seq] - cond_ref[seq]
            allowed = (causal & live & recent) | diagonal
            for p in range(HEADS // 2):
                cq = pl.ds(p * PAIR, PAIR)
                ck = pl.ds(d + p * PAIR, PAIR)
                cv = pl.ds(2 * d + p * PAIR, PAIR)
                q = z_buf[rs, cq] * scale
                sc = dot_t(q, halves(z_buf[rs, ck]))
                parts = []
                for h in range(2):
                    sh = jnp.where(allowed, sc[:, h * SLOTS : (h + 1) * SLOTS], NEGATIVE)
                    e = jnp.exp(sh - jnp.max(sh, axis=-1, keepdims=True))
                    parts.append((e / jnp.sum(e, axis=-1, keepdims=True)).astype(BF))
                pr = jnp.concatenate(parts, axis=1)
                p_buf[seq * (HEADS // 2) + p] = pr
                o_buf[rs, cq] = dot(pr, halves(z_buf[rs, cv])).astype(BF)
        h = x + dot(o_buf[r, :], out_w[...])
        n2, rs2 = norm(h, gain1)
        n2_buf[r, :] = n2
        rs_buf[r, 1:2] = rs2
        for f in range(0, ff, d):
            u = dot(n2, up_w[:, f : f + d])
            sq = u * u
            t = jnp.tanh(u * (GELU_A + GELU_B * sq))
            hs = (0.5 + 0.5 * t).astype(BF)
            g = u.astype(BF) * hs
            e = sq.astype(BF) * (6.0 * GELU_B) + (2.0 * GELU_A)
            act_buf[r, f : f + d] = g
            der_buf[r, f : f + d] = hs + e * (g - g * hs)
        y_buf[r, :] = (h + dot(act_buf[r, :], down_w[...])).astype(BF)

    def backward(i):
        r = chunk_rows(i)
        dm = d_buf[r, :]
        for f in range(0, ff, d):
            dg = dot_t(dm, down_w[f : f + d, :])
            der_buf[r, f : f + d] = (der_buf[r, f : f + d].astype(F32) * dg).astype(BF)
        dn2 = dot_t(der_buf[r, :], up_w[...])
        dh_norm, dgain1 = norm_back(dn2, n2_buf[r, :], gain1, rs_buf[r, 1:2])
        gain_acc[1] += dgain1
        dh = dm.astype(F32) + dh_norm
        da = dh.astype(BF)
        da_buf[r, :] = da
        do_buf[...] = dot_t(da, out_w[...]).astype(BF)
        for s in range(CHUNK):
            seq = i * CHUNK + s
            rs = pl.ds(pl.multiple_of(seq * SLOTS, SLOTS), SLOTS)
            rc = pl.ds(s * SLOTS, SLOTS)
            state = []
            for p in range(HEADS // 2):
                cq = pl.ds(p * PAIR, PAIR)
                do = do_buf[rc, cq]
                pr = p_buf[seq * (HEADS // 2) + p]
                q = z_buf[rs, cq] * scale
                k = z_buf[rs, pl.ds(d + p * PAIR, PAIR)] * scale
                v = z_buf[rs, pl.ds(2 * d + p * PAIR, PAIR)]
                both = jnp.concatenate([do, do * o_buf[rs, cq]], axis=1)
                against = jnp.concatenate([halves(v), minus], axis=1)
                ds = (pr.astype(F32) * dot_t(both, against)).astype(BF)
                state.append((ds, k, turned(ds), q, turned(pr), do))
            for p in range(0, HEADS // 2, 2):
                one, two = state[p], state[p + 1]
                for c in range(3):
                    left_side = jnp.concatenate([one[2 * c], two[2 * c]], axis=0)
                    right_side = jnp.concatenate(
                        [halves(one[2 * c + 1]), halves(two[2 * c + 1])], axis=1
                    )
                    res = dot(left_side, right_side).astype(BF)
                    at = c * d + p * PAIR
                    dz_buf[rc, at : at + PAIR] = res[:SLOTS, :PAIR]
                    dz_buf[rc, at + PAIR : at + 2 * PAIR] = res[SLOTS:, PAIR:]
        dz = dz_buf[...]
        z_buf[r, :] = dz
        dn1 = dot_t(dz, qkv_w[...])
        dx_norm, dgain0 = norm_back(dn1, n1_buf[r, :], gain0, rs_buf[r, 0:1])
        gain_acc[0] += dgain0
        x_buf[r, :] = (dh + dx_norm).astype(BF)

    half = total // 2
    blocks = ff // d
    per = d // (2 * prow)

    def put(seg, c, value, h):
        where = pl.ds(c * per, per)
        value = value.reshape(per, 2, prow, d)
        if h is not None:
            value = value + jnp.where(h == 0, 0.0, 1.0) * grads[seg, where].astype(F32)
        grads[seg, where] = value.astype(BF)

    def weight_grads(h, r, between):
        for c in range(blocks):
            lhs_t[...] = act_buf[r, c * d : (c + 1) * d].T
            put(0, c, dot(lhs_t[...], d_buf[r, :]), h)
            between(0, c)
        lhs_t[...] = n2_buf[r, :].T
        for c in range(blocks):
            put(1, c, dot(lhs_t[...], der_buf[r, c * d : (c + 1) * d]), h)
            between(1, c)
        lhs_t[...] = n1_buf[r, :].T
        for c in range(3):
            put(2, c, dot(lhs_t[...], z_buf[r, c * d : (c + 1) * d]), h)
            between(2, c)
        lhs_t[...] = o_buf[r, :].T
        put(2, 3, dot(lhs_t[...], da_buf[r, :]), h)
        between(2, 3)

    def step(t, carry):
        mid = chunks + chunks // 2
        kind0 = jnp.where(t < chunks, 0, jnp.where((t == mid) | (t == 2 * chunks + 1), 2, 1))
        i0 = jnp.where(t < chunks, t, jnp.where(t < mid, t - chunks, t - chunks - 1))
        kind1 = jnp.where(t < 2 * chunks, t % 2, 2)
        kind = jnp.where(first, kind0, kind1)
        i = jnp.where(first, i0, t // 2)
        h = jnp.where(t == 2 * chunks + 1, 1, 0)

        @pl.when(kind == 0)
        def _():
            @pl.when(second)
            def _():
                to_second(i).wait_recv()

            forward(i)

            @pl.when(first)
            def _():
                to_second(i).start()

            store_y(i).start()

        @pl.when(kind == 1)
        def _():
            @pl.when(first)
            def _():
                to_first(i).wait_recv()
                to_second(i).wait_send()

            backward(i)

            @pl.when(second)
            def _():
                to_first(i).start()

            store_dx(i).start()

        @pl.when(kind == 2)
        def _():
            r = pl.ds(pl.multiple_of(h * half, half), half)
            weight_grads(h, r, lambda seg, c: None)

        return carry

    lax.fori_loop(0, 2 * chunks + 2, step, 0)
    for other in (left, right):
        pl.semaphore_signal(ready, inc=1, device_id=other, device_id_type=MESH)

    width = d // 2
    per_block = SLOTS // prow

    def columns(way):
        return pl.ds(way * width, width)

    def exchange(seg):
        return pltpu.make_async_remote_copy(
            src_ref=grads.at[seg, :, 1 - core],
            dst_ref=sib.at[seg],
            send_sem=sib_send.at[seg],
            recv_sem=sib_recv.at[seg],
            device_id=sibling,
            device_id_type=MESH,
        )

    def landing(seg, way, s):
        q = (seg * 2 + way) * (chips - 1) + s
        row = pl.multiple_of((q % per_block) * prow, prow)
        return p_buf.at[q // per_block, pl.ds(row, prow)]

    def ring(src, dst, seg, way, recv):
        return pltpu.make_async_remote_copy(
            src_ref=src,
            dst_ref=dst,
            send_sem=ring_send.at[seg, way],
            recv_sem=recv,
            device_id=ahead[way],
            device_id_type=MESH,
        )

    def gather_copy(seg, way, k, s):
        spot = grads.at[seg, k, core, :, columns(way)]
        return ring(spot, spot, seg, way, ag_recv.at[seg, way, s])

    def forward_copy(seg, way, k, f):
        spot = grads.at[seg, k, core, :, columns(way)]
        return pltpu.make_async_remote_copy(
            src_ref=spot,
            dst_ref=spot,
            send_sem=fwd_send.at[seg, way],
            recv_sem=fwd_recv.at[seg, way, f],
            device_id=sibling,
            device_id_type=MESH,
        )

    def first_copy(seg, way):
        return ring(
            sib.at[seg, place, :, columns(way)],
            landing(seg, way, 0),
            seg,
            way,
            rs_recv.at[seg, way, 0],
        )

    def ring_start(seg):
        exchange(seg).wait()
        mine = grads[seg, place, core].astype(F32) + sib[seg, place].astype(F32)
        sib[seg, place] = mine.astype(BF)
        for way in range(2):
            first_copy(seg, way).start()

    def reduce_tick(seg, s, last):
        for way in range(2):
            if way == 0:
                k = lax.rem(place + 2 * chips - 1 - s, chips)
            else:
                k = lax.rem(place + 1 + s, chips)
            here = landing(seg, way, s)
            ring(here, here, seg, way, rs_recv.at[seg, way, s]).wait()
            value = (
                here[...].astype(F32)
                + grads[seg, k, core, :, columns(way)].astype(F32)
                + sib[seg, k, :, columns(way)].astype(F32)
            ).astype(BF)
            if last:
                grads[seg, k, core, :, columns(way)] = value
                gather_copy(seg, way, k, 0).start()
                forward_copy(seg, way, k, 0).start()
            else:
                here[...] = value
                ring(
                    here, landing(seg, way, s + 1), seg, way, rs_recv.at[seg, way, s + 1]
                ).start()

    def gather_tick(seg, s, last):
        for way in range(2):
            k = lax.rem(place + chips - s, chips) if way == 0 else lax.rem(place + s, chips)
            gather_copy(seg, way, k, s).wait()
            if not last:
                gather_copy(seg, way, k, s + 1).start()
            forward_copy(seg, way, k, 0).wait_send()
            forward_copy(seg, way, k, s + 1).start()

    def gain_copy(s):
        spot = gain_all.at[lax.rem(place + chips - s, chips)]
        return pltpu.make_async_remote_copy(
            src_ref=spot,
            dst_ref=spot,
            send_sem=gain_send,
            recv_sem=gain_recv.at[s],
            device_id=right,
            device_id_type=MESH,
        )

    gain_swap = pltpu.make_async_remote_copy(
        src_ref=gain_own,
        dst_ref=gain_sib,
        send_sem=gsib_sem.at[0],
        recv_sem=gsib_sem.at[1],
        device_id=sibling,
        device_id_type=MESH,
    )
    gain_own[...] = jnp.zeros_like(gain_own)
    gain_own[0:2, :] = jnp.sum(gain_acc[...], axis=1)
    gain_swap.start()
    for seg in range(segments):
        exchange(seg).start()
    gain_swap.wait()
    gain_all[place] = gain_own[...] + gain_sib[...]
    pl.semaphore_wait(ready, 2)
    gain_copy(0).start()
    for seg in range(segments):
        ring_start(seg)
    pl.semaphore_signal(freed, inc=1, device_id=sibling, device_id_type=MESH)

    def reduce_step(s, carry):
        for seg in range(segments):
            reduce_tick(seg, s, False)
        gain_copy(s).wait()
        gain_copy(s + 1).start()
        return carry

    lax.fori_loop(0, chips - 2, reduce_step, 0)
    pl.semaphore_wait(freed, 1)
    for seg in range(segments):
        reduce_tick(seg, chips - 2, True)
    gain_copy(chips - 2).wait()

    def gather_step(s, carry):
        for seg in range(segments):
            gather_tick(seg, s, False)
        return carry

    lax.fori_loop(0, chips - 2, gather_step, 0)
    for seg in range(segments):
        gather_tick(seg, chips - 2, True)

    gains = gain_all[0]
    for k in range(1, chips):
        gains = gains + gain_all[k]
    gain_out[...] = gains[0:2, :]

    def results(seg):
        if seg == 0:
            return [pltpu.make_async_copy(grads.at[0], down_out, go_sem.at[0])]
        copies = []
        for c in range(blocks):
            if seg == 1:
                dst = up_out.at[:, :, :, c * d : (c + 1) * d]
            elif c < 3:
                dst = qkv_out.at[:, :, :, c * d : (c + 1) * d]
            else:
                dst = out_out
            src = grads.at[seg, pl.ds(c * per, per)]
            copies.append(pltpu.make_async_copy(src, dst, go_sem.at[blocks * seg + c]))
        return copies

    for seg in range(segments):
        for way in range(2):
            forward_copy(seg, way, 0, 0).wait_send()

        def arrived(f, carry, seg=seg):
            for way in range(2):
                forward_copy(seg, way, 0, f).wait_recv()
            return carry

        lax.fori_loop(0, chips, arrived, 0)
        for copy in results(seg):
            copy.start()
    for seg in range(segments):
        for copy in results(seg):
            copy.wait()

    def finish(i, carry):
        @pl.when(second)
        def _():
            to_first(i).wait_send()

        store_y(i).wait()
        store_dx(i).wait()
        return carry

    lax.fori_loop(0, chunks, finish, 0)


def local(
    tokens,
    start_steps,
    cond_counts,
    valid_steps,
    qkv_weight,
    out_weight,
    up_weight,
    down_weight,
    norm_gains,
    cotangent,
):
    seqs, slots, d = tokens.shape
    ff = up_weight.shape[2]
    rows = seqs * slots
    chunks = seqs // CHUNK
    chips = lax.axis_size("batch") // 2
    segments = 3
    prow = ff // (2 * chips)
    per = d // (2 * prow)
    vmem = pl.BlockSpec(memory_space=pltpu.VMEM)
    smem = pl.BlockSpec(memory_space=pltpu.SMEM)
    hbm = pl.BlockSpec(memory_space=pl.ANY)
    y, dx, qkv_grad, out_grad, up_grad, down_grad, gains = pl.pallas_call(
        functools.partial(layer_kernel, seqs, chips),
        out_shape=(
            jax.ShapeDtypeStruct((rows, d), BF),
            jax.ShapeDtypeStruct((rows, d), BF),
            jax.ShapeDtypeStruct((per, 2, prow, 3 * d), BF),
            jax.ShapeDtypeStruct((per, 2, prow, d), BF),
            jax.ShapeDtypeStruct((per, 2, prow, ff), BF),
            jax.ShapeDtypeStruct((chips, 2, prow, d), BF),
            jax.ShapeDtypeStruct((2, d), F32),
        ),
        in_specs=[smem] * 3 + [hbm] * 2 + [vmem] * 5,
        out_specs=(hbm, hbm, hbm, hbm, hbm, hbm, vmem),
        scratch_shapes=[
            pltpu.VMEM((rows, d), BF),
            pltpu.VMEM((rows, d), BF),
            pltpu.VMEM((rows, d), BF),
            pltpu.VMEM((rows, d), BF),
            pltpu.VMEM((rows, 3 * d), BF),
            pltpu.VMEM((seqs * HEADS // 2, SLOTS, 2 * SLOTS), BF),
            pltpu.VMEM((rows, d), BF),
            pltpu.VMEM((rows, d), BF),
            pltpu.VMEM((rows, ff), BF),
            pltpu.VMEM((rows, ff), BF),
            pltpu.VMEM((rows, d), BF),
            pltpu.VMEM((rows, 2), F32),
            pltpu.VMEM((CHUNK * SLOTS, d), BF),
            pltpu.VMEM((CHUNK * SLOTS, 3 * d), BF),
            pltpu.VMEM((d, rows // 2), BF),
            pltpu.VMEM((segments, chips, 2, prow, d), BF),
            pltpu.VMEM((segments, chips, prow, d), BF),
            pltpu.VMEM((2, 8, d), F32),
            pltpu.VMEM((8, d), F32),
            pltpu.VMEM((8, d), F32),
            pltpu.VMEM((chips, 8, d), F32),
            pltpu.SemaphoreType.DMA,
            pltpu.SemaphoreType.DMA((chunks,)),
            pltpu.SemaphoreType.DMA((chunks,)),
            pltpu.SemaphoreType.DMA((chunks,)),
            pltpu.SemaphoreType.DMA((chunks,)),
            pltpu.SemaphoreType.DMA((segments,)),
            pltpu.SemaphoreType.DMA((segments,)),
            pltpu.SemaphoreType.DMA((segments, 2)),
            pltpu.SemaphoreType.DMA((segments, 2, chips - 1)),
            pltpu.SemaphoreType.DMA((segments, 2, chips - 1)),
            pltpu.SemaphoreType.DMA((segments, 2)),
            pltpu.SemaphoreType.DMA((segments, 2, chips)),
            pltpu.SemaphoreType.DMA,
            pltpu.SemaphoreType.DMA((chips - 1,)),
            pltpu.SemaphoreType.DMA((2,)),
            pltpu.SemaphoreType.DMA((segments * ff // d,)),
            pltpu.SemaphoreType.REGULAR,
            pltpu.SemaphoreType.REGULAR,
        ],
        compiler_params=pltpu.CompilerParams(
            collective_id=0, has_side_effects=True, vmem_limit_bytes=63 * 2**20
        ),
        name="layer",
    )(
        start_steps,
        cond_counts,
        valid_steps,
        tokens.reshape(rows, d),
        cotangent.reshape(rows, d),
        qkv_weight[0],
        out_weight[0],
        up_weight[0],
        down_weight[0],
        norm_gains[0],
    )
    shape = (1, seqs, slots, d)
    return (
        y.reshape(shape),
        dx.reshape(shape),
        qkv_grad.reshape(qkv_weight.shape).astype(F32),
        out_grad.reshape(out_weight.shape).astype(F32),
        up_grad.reshape(up_weight.shape).astype(F32),
        down_grad.reshape(down_weight.shape).astype(F32),
        gains[None],
    )


def solution(mesh):
    rows = P("batch", None, None)
    flat = P("batch")
    layer = P("section", None, None)
    in_specs = (rows, flat, flat, flat, layer, layer, layer, layer, layer, rows)
    both = P("section", "batch", None, None)
    out_specs = (both, both, layer, layer, layer, layer, layer)
    return jax.shard_map(local, mesh=mesh, in_specs=in_specs, out_specs=out_specs, check_vma=False)
```

```python
import functools

import jax
import jax.numpy as jnp
from jax import lax
from jax.experimental import pallas as pl
from jax.experimental.pallas import tpu as pltpu
from jax.sharding import PartitionSpec as P

HEADS = 8
HEAD_DIM = 64
SLOTS = 128
STEP_TOKENS = 6
PAIR = 2 * HEAD_DIM
NEGATIVE = -1e30
EPS = 1e-05
SCALE = HEAD_DIM ** (-0.5)
GELU_A = 0.7978845608028654
GELU_B = 0.7978845608028654 * 0.044715
CHUNK = 2
MESH = pl.DeviceIdType.MESH
BF = jnp.bfloat16
F32 = jnp.float32


def dot(a, b):
    return jnp.dot(a, b, preferred_element_type=F32)


def dot_t(a, b):
    return lax.dot_general(a, b, (((1,), (1,)), ((), ())), preferred_element_type=F32)


def t_dot(a, b):
    return lax.dot_general(a, b, (((0,), (0,)), ((), ())), preferred_element_type=F32)


def layer_kernel(
    seqs,
    chips,
    start_ref,
    cond_ref,
    valid_ref,
    tok_ref,
    cot_ref,
    qkv_in,
    out_in,
    up_in,
    down_in,
    gain_ref,
    y_out,
    dx_out,
    qkv_out,
    out_out,
    up_out,
    down_out,
    gain_out,
    qkv_w,
    out_w,
    up_w,
    down_w,
    x_buf,
    d_buf,
    y_buf,
    n1_buf,
    z_buf,
    p_buf,
    o_buf,
    n2_buf,
    act_buf,
    der_buf,
    da_buf,
    rs_buf,
    dh_buf,
    do_buf,
    dz_buf,
    lhs_t,
    grads,
    sib,
    gain_acc,
    gain_own,
    gain_sib,
    gain_all,
    in_sem,
    w_sem,
    send_sem,
    recv_sem,
    yo_sem,
    xo_sem,
    sib_send,
    sib_recv,
    ring_send,
    rs_recv,
    ag_recv,
    fwd_send,
    fwd_recv,
    gain_send,
    gain_recv,
    gsib_sem,
    go_sem,
    ready,
    freed,
):
    section = lax.axis_index("section")
    batch = lax.axis_index("batch")
    first = section == 0
    second = section == 1
    partner = (1 - section, batch)
    core = lax.rem(batch, 2)
    chip = batch // 2
    half_ring = chips // 2
    place = jnp.where(chip % 2 == 0, chip // 2, chips - 1 - chip // 2)

    def at_place(p):
        c = jnp.where(p < half_ring, 2 * p, 2 * (chips - 1 - p) + 1)
        return (section, 2 * c + core)

    right = at_place(lax.rem(place + 1, chips))
    left = at_place(lax.rem(place + chips - 1, chips))
    ahead = (right, left)
    sibling = (section, batch + 1 - 2 * core)
    segments = grads.shape[0]
    prow = grads.shape[3]
    d = x_buf.shape[1]
    ff = act_buf.shape[1]
    rows = CHUNK * SLOTS
    chunks = seqs // CHUNK
    total = seqs * SLOTS

    weights = [
        pltpu.make_async_copy(src, dst, w_sem.at[i])
        for i, (src, dst) in enumerate(
            ((qkv_in, qkv_w), (out_in, out_w), (up_in, up_w), (down_in, down_w))
        )
    ]
    load_x = pltpu.make_async_copy(tok_ref, x_buf, in_sem)
    load_d = pltpu.make_async_copy(cot_ref, d_buf, in_sem)

    @pl.when(first)
    def _():
        load_x.start()

    @pl.when(second)
    def _():
        load_d.start()

    for copy in weights:
        copy.start()

    barrier = pltpu.get_barrier_semaphore()
    for other in (partner, sibling, left, right):
        pl.semaphore_signal(barrier, inc=1, device_id=other, device_id_type=MESH)

    gain_acc[...] = jnp.zeros_like(gain_acc)
    grads[...] = jnp.zeros_like(grads)

    @pl.when(first)
    def _():
        load_x.wait()

    @pl.when(second)
    def _():
        load_d.wait()

    pl.semaphore_wait(barrier, 4)
    for copy in weights:
        copy.wait()

    lane = lax.broadcasted_iota(jnp.int32, (1, PAIR), 1)
    low = jnp.where(lane < HEAD_DIM, 1.0, 0.0).astype(BF)
    high = jnp.where(lane < HEAD_DIM, 0.0, 1.0).astype(BF)
    head_row = lax.broadcasted_iota(jnp.int32, (2 * SLOTS, PAIR), 0) < SLOTS
    head_lane = lax.broadcasted_iota(jnp.int32, (2 * SLOTS, PAIR), 1) < HEAD_DIM
    minus = jnp.where(head_row == head_lane, -1.0, 0.0).astype(BF)
    scale = jnp.asarray(SCALE, BF)
    key_id = lax.broadcasted_iota(jnp.int32, (SLOTS, SLOTS), 1)
    row_id = lax.broadcasted_iota(jnp.int32, (SLOTS, SLOTS), 0)
    key_step = (key_id * 43) >> 8
    row_step = (row_id * 43) >> 8
    causal = key_step <= row_step
    diagonal = key_id == row_id
    gain0 = gain_ref[0:1, :]
    gain1 = gain_ref[1:2, :]

    def chunk_rows(i):
        return pl.ds(pl.multiple_of(i * rows, rows), rows)

    def to_second(i):
        r = chunk_rows(i)
        return pltpu.make_async_remote_copy(
            src_ref=y_buf.at[r],
            dst_ref=x_buf.at[r],
            send_sem=send_sem.at[i],
            recv_sem=recv_sem.at[i],
            device_id=partner,
            device_id_type=MESH,
        )

    def to_first(i):
        r = chunk_rows(i)
        return pltpu.make_async_remote_copy(
            src_ref=x_buf.at[r],
            dst_ref=d_buf.at[r],
            send_sem=send_sem.at[i],
            recv_sem=recv_sem.at[i],
            device_id=partner,
            device_id_type=MESH,
        )

    def store_y(i):
        r = chunk_rows(i)
        return pltpu.make_async_copy(y_buf.at[r], y_out.at[r], yo_sem.at[i])

    def store_dx(i):
        r = chunk_rows(i)
        return pltpu.make_async_copy(x_buf.at[r], dx_out.at[r], xo_sem.at[i])

    def norm(v, gain):
        mean = jnp.mean(v, axis=-1, keepdims=True)
        c = v - mean
        var = jnp.mean(c * c, axis=-1, keepdims=True)
        rs = lax.rsqrt(var + EPS)
        return (c * rs * gain).astype(BF), rs

    def norm_back(dn, n, gain, rs):
        xhat = n.astype(F32) * (1.0 / gain)
        w = dn * gain
        dgain = jnp.sum((dn * xhat).reshape(rows // 8, 8, d), axis=0)
        m1 = jnp.mean(w, axis=-1, keepdims=True)
        m2 = jnp.mean(w * xhat, axis=-1, keepdims=True)
        return rs * (w - m1 - xhat * m2), dgain

    def halves(v):
        return jnp.concatenate([v * low, v * high], axis=0)

    def turned(v):
        return jnp.concatenate([v[:, :SLOTS].T, v[:, SLOTS:].T], axis=1)

    def forward_attention(i):
        r = chunk_rows(i)
        x = x_buf[r, :].astype(F32)
        n1, rs1 = norm(x, gain0)
        n1_buf[r, :] = n1
        rs_buf[r, 0:1] = rs1
        for c in range(3):
            z_buf[r, c * d : (c + 1) * d] = dot(n1, qkv_w[:, c * d : (c + 1) * d]).astype(BF)
        for s in range(CHUNK):
            seq = i * CHUNK + s
            rs = pl.ds(pl.multiple_of(seq * SLOTS, SLOTS), SLOTS)
            live = key_id < valid_ref[seq] * STEP_TOKENS
            recent = key_step >= start_ref[seq] - cond_ref[seq]
            allowed = (causal & live & recent) | diagonal
            for p in range(HEADS // 2):
                cq = pl.ds(p * PAIR, PAIR)
                ck = pl.ds(d + p * PAIR, PAIR)
                cv = pl.ds(2 * d + p * PAIR, PAIR)
                q = z_buf[rs, cq] * scale
                sc = dot_t(q, halves(z_buf[rs, ck]))
                parts = []
                for h in range(2):
                    sh = jnp.where(allowed, sc[:, h * SLOTS : (h + 1) * SLOTS], NEGATIVE)
                    e = jnp.exp(sh - jnp.max(sh, axis=-1, keepdims=True))
                    parts.append((e / jnp.sum(e, axis=-1, keepdims=True)).astype(BF))
                pr = jnp.concatenate(parts, axis=1)
                p_buf[seq * (HEADS // 2) + p] = pr
                o_buf[rs, cq] = dot(pr, halves(z_buf[rs, cv])).astype(BF)

    def forward_mlp(i):
        r = chunk_rows(i)
        h = x_buf[r, :].astype(F32) + dot(o_buf[r, :], out_w[...])
        n2, rs2 = norm(h, gain1)
        n2_buf[r, :] = n2
        rs_buf[r, 1:2] = rs2
        for f in range(0, ff, d):
            u = dot(n2, up_w[:, f : f + d])
            sq = u * u
            t = jnp.tanh(u * (GELU_A + GELU_B * sq))
            hs = 0.5 + 0.5 * t
            g = u * hs
            act_buf[r, f : f + d] = g.astype(BF)
            slope = 2.0 * GELU_A + 6.0 * GELU_B * sq
            der_buf[r, f : f + d] = (hs + slope * (g - g * hs)).astype(BF)
        y_buf[r, :] = (h + dot(act_buf[r, :], down_w[...])).astype(BF)

    def backward_mlp(i):
        r = chunk_rows(i)
        dm = d_buf[r, :]
        for f in range(0, ff, d):
            dg = dot_t(dm, down_w[f : f + d, :])
            der_buf[r, f : f + d] = (der_buf[r, f : f + d].astype(F32) * dg).astype(BF)
        dn2 = dot_t(der_buf[r, :], up_w[...])
        dh_norm, dgain1 = norm_back(dn2, n2_buf[r, :], gain1, rs_buf[r, 1:2])
        gain_acc[1] += dgain1
        dh = dm.astype(F32) + dh_norm
        da = dh.astype(BF)
        da_buf[r, :] = da
        dh_buf[...] = dh
        do_buf[...] = dot_t(da, out_w[...]).astype(BF)

    def backward_attention(i):
        r = chunk_rows(i)
        for s in range(CHUNK):
            seq = i * CHUNK + s
            rs = pl.ds(pl.multiple_of(seq * SLOTS, SLOTS), SLOTS)
            rc = pl.ds(s * SLOTS, SLOTS)
            state = []
            for p in range(HEADS // 2):
                cq = pl.ds(p * PAIR, PAIR)
                do = do_buf[rc, cq]
                pr = p_buf[seq * (HEADS // 2) + p]
                q = z_buf[rs, cq] * scale
                k = z_buf[rs, pl.ds(d + p * PAIR, PAIR)] * scale
                v = z_buf[rs, pl.ds(2 * d + p * PAIR, PAIR)]
                both = jnp.concatenate([do, do * o_buf[rs, cq]], axis=1)
                against = jnp.concatenate([halves(v), minus], axis=1)
                ds = (pr.astype(F32) * dot_t(both, against)).astype(BF)
                state.append((ds, k, turned(ds), q, turned(pr), do))
            for p in range(0, HEADS // 2, 2):
                one, two = state[p], state[p + 1]
                for c in range(3):
                    left_side = jnp.concatenate([one[2 * c], two[2 * c]], axis=0)
                    right_side = jnp.concatenate(
                        [halves(one[2 * c + 1]), halves(two[2 * c + 1])], axis=1
                    )
                    res = dot(left_side, right_side).astype(BF)
                    at = c * d + p * PAIR
                    dz_buf[rc, at : at + PAIR] = res[:SLOTS, :PAIR]
                    dz_buf[rc, at + PAIR : at + 2 * PAIR] = res[SLOTS:, PAIR:]
        dz = dz_buf[...]
        z_buf[r, :] = dz
        dn1 = dot_t(dz, qkv_w[...])
        dx_norm, dgain0 = norm_back(dn1, n1_buf[r, :], gain0, rs_buf[r, 0:1])
        gain_acc[0] += dgain0
        x_buf[r, :] = (dh_buf[...] + dx_norm).astype(BF)

    def forward(i):
        forward_attention(i)
        forward_mlp(i)

    def backward(i):
        backward_mlp(i)
        backward_attention(i)

    part = total // 4
    blocks = ff // d
    per = d // (2 * prow)

    def put(seg, c, value):
        where = pl.ds(c * per, per)
        value = value.reshape(per, 2, prow, d) + grads[seg, where].astype(F32)
        grads[seg, where] = value.astype(BF)

    def weight_grads(quarter, done):
        r = pl.ds(pl.multiple_of(quarter * part, part), part)
        for c in range(blocks):
            lhs_t[...] = act_buf[r, c * d : (c + 1) * d].T
            put(0, c, dot(lhs_t[...], d_buf[r, :]))
        done(0)
        lhs_t[...] = n2_buf[r, :].T
        for c in range(blocks):
            put(1, c, dot(lhs_t[...], der_buf[r, c * d : (c + 1) * d]))
        done(1)
        lhs_t[...] = n1_buf[r, :].T
        for c in range(3):
            put(2, c, dot(lhs_t[...], z_buf[r, c * d : (c + 1) * d]))
        lhs_t[...] = o_buf[r, :].T
        put(2, 3, dot(lhs_t[...], da_buf[r, :]))
        done(2)

    per_part = chunks // 4

    def step(t, carry):
        u = t - chunks
        turn = lax.rem(u, per_part + 1)
        kind0 = jnp.where(t < chunks, 0, jnp.where(turn < per_part, 1, 2))
        quarter0 = u // (per_part + 1)
        i0 = jnp.where(t < chunks, t, quarter0 * per_part + turn)
        kind1 = jnp.where(t < 2 * chunks, t % 2, 2)
        kind = jnp.where(first, kind0, kind1)
        i = jnp.where(first, i0, t // 2)
        quarter = jnp.where(first, quarter0, t - 2 * chunks)

        @pl.when(kind == 0)
        def _():
            @pl.when(second)
            def _():
                to_second(i).wait_recv()

            forward(i)

            @pl.when(first)
            def _():
                to_second(i).start()

            store_y(i).start()

        @pl.when(kind == 1)
        def _():
            @pl.when(first)
            def _():
                to_first(i).wait_recv()
                to_second(i).wait_send()

            backward(i)

            @pl.when(second)
            def _():
                to_first(i).start()

            store_dx(i).start()

        @pl.when(kind == 2)
        def _():
            weight_grads(quarter, lambda seg: None)

        return carry

    lax.fori_loop(0, 2 * chunks + 3, step, 0)
    for other in (left, right):
        pl.semaphore_signal(ready, inc=1, device_id=other, device_id_type=MESH)

    width = d // 2
    per_block = SLOTS // prow

    def columns(way):
        return pl.ds(way * width, width)

    def exchange(seg):
        return pltpu.make_async_remote_copy(
            src_ref=grads.at[seg, :, 1 - core],
            dst_ref=sib.at[seg],
            send_sem=sib_send.at[seg],
            recv_sem=sib_recv.at[seg],
            device_id=sibling,
            device_id_type=MESH,
        )

    def landing(seg, way, s):
        q = (seg * 2 + way) * (chips - 1) + s
        row = pl.multiple_of((q % per_block) * prow, prow)
        return p_buf.at[q // per_block, pl.ds(row, prow)]

    def ring(src, dst, seg, way, recv):
        return pltpu.make_async_remote_copy(
            src_ref=src,
            dst_ref=dst,
            send_sem=ring_send.at[seg, way],
            recv_sem=recv,
            device_id=ahead[way],
            device_id_type=MESH,
        )

    def gather_copy(seg, way, k, s):
        spot = grads.at[seg, k, core, :, columns(way)]
        return ring(spot, spot, seg, way, ag_recv.at[seg, way, s])

    def forward_copy(seg, way, k, f):
        spot = grads.at[seg, k, core, :, columns(way)]
        return pltpu.make_async_remote_copy(
            src_ref=spot,
            dst_ref=spot,
            send_sem=fwd_send.at[seg, way],
            recv_sem=fwd_recv.at[seg, way, f],
            device_id=sibling,
            device_id_type=MESH,
        )

    def first_copy(seg, way):
        return ring(
            sib.at[seg, place, :, columns(way)],
            landing(seg, way, 0),
            seg,
            way,
            rs_recv.at[seg, way, 0],
        )

    def ring_start(seg):
        exchange(seg).wait()
        mine = grads[seg, place, core].astype(F32) + sib[seg, place].astype(F32)
        sib[seg, place] = mine.astype(BF)
        for way in range(2):
            first_copy(seg, way).start()

    def reduce_tick(seg, s, last):
        for way in range(2):
            if way == 0:
                k = lax.rem(place + 2 * chips - 1 - s, chips)
            else:
                k = lax.rem(place + 1 + s, chips)
            here = landing(seg, way, s)
            ring(here, here, seg, way, rs_recv.at[seg, way, s]).wait()
            value = (
                here[...].astype(F32)
                + grads[seg, k, core, :, columns(way)].astype(F32)
                + sib[seg, k, :, columns(way)].astype(F32)
            ).astype(BF)
            if last:
                grads[seg, k, core, :, columns(way)] = value
                gather_copy(seg, way, k, 0).start()
                forward_copy(seg, way, k, 0).start()
            else:
                here[...] = value
                ring(
                    here, landing(seg, way, s + 1), seg, way, rs_recv.at[seg, way, s + 1]
                ).start()

    def gather_tick(seg, s, last):
        for way in range(2):
            k = lax.rem(place + chips - s, chips) if way == 0 else lax.rem(place + s, chips)
            gather_copy(seg, way, k, s).wait()
            if not last:
                gather_copy(seg, way, k, s + 1).start()
            forward_copy(seg, way, k, 0).wait_send()
            forward_copy(seg, way, k, s + 1).start()

    def gain_copy(s):
        spot = gain_all.at[lax.rem(place + chips - s, chips)]
        return pltpu.make_async_remote_copy(
            src_ref=spot,
            dst_ref=spot,
            send_sem=gain_send,
            recv_sem=gain_recv.at[s],
            device_id=right,
            device_id_type=MESH,
        )

    gain_swap = pltpu.make_async_remote_copy(
        src_ref=gain_own,
        dst_ref=gain_sib,
        send_sem=gsib_sem.at[0],
        recv_sem=gsib_sem.at[1],
        device_id=sibling,
        device_id_type=MESH,
    )
    gain_own[...] = jnp.zeros_like(gain_own)
    gain_own[0:2, :] = jnp.sum(gain_acc[...], axis=1)
    gain_swap.start()

    def ring_begin(seg):
        if seg == 0:
            pl.semaphore_wait(ready, 2)
            gain_swap.wait()
            gain_all[place] = gain_own[...] + gain_sib[...]
            gain_copy(0).start()
        ring_start(seg)

    def done(seg):
        exchange(seg).start()
        if seg > 0:
            ring_begin(seg - 1)

    weight_grads(3, done)
    ring_begin(segments - 1)
    pl.semaphore_signal(freed, inc=1, device_id=sibling, device_id_type=MESH)

    def reduce_step(s, carry):
        for seg in range(segments):
            reduce_tick(seg, s, False)
        gain_copy(s).wait()
        gain_copy(s + 1).start()
        return carry

    lax.fori_loop(0, chips - 2, reduce_step, 0)
    pl.semaphore_wait(freed, 1)
    for seg in range(segments):
        reduce_tick(seg, chips - 2, True)
    gain_copy(chips - 2).wait()

    def gather_step(s, carry):
        for seg in range(segments):
            gather_tick(seg, s, False)
        return carry

    lax.fori_loop(0, chips - 2, gather_step, 0)
    for seg in range(segments):
        gather_tick(seg, chips - 2, True)

    gains = gain_all[0]
    for k in range(1, chips):
        gains = gains + gain_all[k]
    gain_out[...] = gains[0:2, :]

    def results(seg):
        if seg == 0:
            return [pltpu.make_async_copy(grads.at[0], down_out, go_sem.at[0])]
        copies = []
        for c in range(blocks):
            if seg == 1:
                dst = up_out.at[:, :, :, c * d : (c + 1) * d]
            elif c < 3:
                dst = qkv_out.at[:, :, :, c * d : (c + 1) * d]
            else:
                dst = out_out
            src = grads.at[seg, pl.ds(c * per, per)]
            copies.append(pltpu.make_async_copy(src, dst, go_sem.at[blocks * seg + c]))
        return copies

    for seg in range(segments):
        for way in range(2):
            forward_copy(seg, way, 0, 0).wait_send()

        def arrived(f, carry, seg=seg):
            for way in range(2):
                forward_copy(seg, way, 0, f).wait_recv()
            return carry

        lax.fori_loop(0, chips, arrived, 0)
        for copy in results(seg):
            copy.start()
    for seg in range(segments):
        for copy in results(seg):
            copy.wait()

    def finish(i, carry):
        @pl.when(second)
        def _():
            to_first(i).wait_send()

        store_y(i).wait()
        store_dx(i).wait()
        return carry

    lax.fori_loop(0, chunks, finish, 0)


def finish_kernel(parts, *refs):
    count = len(parts)
    sources, results = refs[:count], refs[count : 2 * count]
    lows, wides = refs[2 * count : 3 * count], list(refs[3 * count : -2])
    load_sem, store_sem = refs[-2:]
    pieces = []
    for src, dst, low, steps in zip(sources, results, lows, parts, strict=True):
        wide = low if dst.dtype == low.dtype else wides.pop(0)
        tall = src.shape[0] // steps
        for t in range(0, src.shape[0], tall):
            r = pl.ds(t, tall)
            n = len(pieces)
            load = pltpu.make_async_copy(src.at[r], low.at[r], load_sem.at[n])
            store = pltpu.make_async_copy(wide.at[r], dst.at[r], store_sem.at[n])
            pieces.append((load, store, low, wide, r))
    for load, _, _, _, _ in pieces:
        load.start()
    for load, store, low, wide, r in pieces:
        load.wait()
        if wide is not low:
            wide[r, :] = low[r, :].astype(F32)
        store.start()
    for _, store, _, _, _ in pieces:
        store.wait()


def finish(rows, grads):
    hbm = pl.BlockSpec(memory_space=pl.ANY)
    arrays = (*grads, *rows)
    types = [F32] * len(grads) + [a.dtype for a in rows]
    parts = [4] * len(grads) + [2 if a.shape[0] > 2 else 1 for a in rows]
    return pl.pallas_call(
        functools.partial(finish_kernel, parts),
        in_specs=[hbm] * len(arrays),
        out_specs=[hbm] * len(arrays),
        out_shape=[jax.ShapeDtypeStruct(a.shape, t) for a, t in zip(arrays, types, strict=True)],
        scratch_shapes=[pltpu.VMEM(a.shape, a.dtype) for a in arrays]
        + [pltpu.VMEM(g.shape, F32) for g in grads]
        + [pltpu.SemaphoreType.DMA((sum(parts),))] * 2,
        compiler_params=pltpu.CompilerParams(vmem_limit_bytes=60 * 2**20),
        name="finish",
    )(*arrays)


def local(
    tokens,
    start_steps,
    cond_counts,
    valid_steps,
    qkv_weight,
    out_weight,
    up_weight,
    down_weight,
    norm_gains,
    cotangent,
):
    seqs, slots, d = tokens.shape
    ff = up_weight.shape[2]
    rows = seqs * slots
    chunks = seqs // CHUNK
    chips = lax.axis_size("batch") // 2
    segments = 3
    prow = ff // (2 * chips)
    per = d // (2 * prow)
    vmem = pl.BlockSpec(memory_space=pltpu.VMEM)
    smem = pl.BlockSpec(memory_space=pltpu.SMEM)
    hbm = pl.BlockSpec(memory_space=pl.ANY)
    y, dx, qkv_grad, out_grad, up_grad, down_grad, gains = pl.pallas_call(
        functools.partial(layer_kernel, seqs, chips),
        out_shape=(
            jax.ShapeDtypeStruct((rows, d), BF),
            jax.ShapeDtypeStruct((rows, d), BF),
            jax.ShapeDtypeStruct((per, 2, prow, 3 * d), BF),
            jax.ShapeDtypeStruct((per, 2, prow, d), BF),
            jax.ShapeDtypeStruct((per, 2, prow, ff), BF),
            jax.ShapeDtypeStruct((chips, 2, prow, d), BF),
            jax.ShapeDtypeStruct((2, d), F32),
        ),
        in_specs=[smem] * 3 + [hbm] * 6 + [vmem],
        out_specs=(hbm, hbm, hbm, hbm, hbm, hbm, vmem),
        scratch_shapes=[
            pltpu.VMEM((d, 3 * d), BF),
            pltpu.VMEM((d, d), BF),
            pltpu.VMEM((d, ff), BF),
            pltpu.VMEM((ff, d), BF),
            pltpu.VMEM((rows, d), BF),
            pltpu.VMEM((rows, d), BF),
            pltpu.VMEM((rows, d), BF),
            pltpu.VMEM((rows, d), BF),
            pltpu.VMEM((rows, 3 * d), BF),
            pltpu.VMEM((seqs * HEADS // 2, SLOTS, 2 * SLOTS), BF),
            pltpu.VMEM((rows, d), BF),
            pltpu.VMEM((rows, d), BF),
            pltpu.VMEM((rows, ff), BF),
            pltpu.VMEM((rows, ff), BF),
            pltpu.VMEM((rows, d), BF),
            pltpu.VMEM((rows, 2), F32),
            pltpu.VMEM((CHUNK * SLOTS, d), F32),
            pltpu.VMEM((CHUNK * SLOTS, d), BF),
            pltpu.VMEM((CHUNK * SLOTS, 3 * d), BF),
            pltpu.VMEM((d, rows // 4), BF),
            pltpu.VMEM((segments, chips, 2, prow, d), BF),
            pltpu.VMEM((segments, chips, prow, d), BF),
            pltpu.VMEM((2, 8, d), F32),
            pltpu.VMEM((8, d), F32),
            pltpu.VMEM((8, d), F32),
            pltpu.VMEM((chips, 8, d), F32),
            pltpu.SemaphoreType.DMA,
            pltpu.SemaphoreType.DMA((4,)),
            pltpu.SemaphoreType.DMA((chunks,)),
            pltpu.SemaphoreType.DMA((chunks,)),
            pltpu.SemaphoreType.DMA((chunks,)),
            pltpu.SemaphoreType.DMA((chunks,)),
            pltpu.SemaphoreType.DMA((segments,)),
            pltpu.SemaphoreType.DMA((segments,)),
            pltpu.SemaphoreType.DMA((segments, 2)),
            pltpu.SemaphoreType.DMA((segments, 2, chips - 1)),
            pltpu.SemaphoreType.DMA((segments, 2, chips - 1)),
            pltpu.SemaphoreType.DMA((segments, 2)),
            pltpu.SemaphoreType.DMA((segments, 2, chips)),
            pltpu.SemaphoreType.DMA,
            pltpu.SemaphoreType.DMA((chips - 1,)),
            pltpu.SemaphoreType.DMA((2,)),
            pltpu.SemaphoreType.DMA((segments * ff // d,)),
            pltpu.SemaphoreType.REGULAR,
            pltpu.SemaphoreType.REGULAR,
        ],
        compiler_params=pltpu.CompilerParams(
            collective_id=0, has_side_effects=True, vmem_limit_bytes=63 * 2**20
        ),
        name="layer",
    )(
        start_steps,
        cond_counts,
        valid_steps,
        tokens.reshape(rows, d),
        cotangent.reshape(rows, d),
        qkv_weight[0],
        out_weight[0],
        up_weight[0],
        down_weight[0],
        norm_gains[0],
    )
    grads = (
        down_grad.reshape(ff, d),
        up_grad.reshape(d, ff),
        qkv_grad.reshape(d, 3 * d),
        out_grad.reshape(d, d),
    )
    down_grad, up_grad, qkv_grad, out_grad, y, dx, gains = finish((y, dx, gains), grads)
    shape = (1, seqs, slots, d)
    return (
        y.reshape(shape),
        dx.reshape(shape),
        qkv_grad[None],
        out_grad[None],
        up_grad[None],
        down_grad[None],
        gains[None],
    )


def solution(mesh):
    rows = P("batch", None, None)
    flat = P("batch")
    layer = P("section", None, None)
    in_specs = (rows, flat, flat, flat, layer, layer, layer, layer, layer, rows)
    both = P("section", "batch", None, None)
    out_specs = (both, both, layer, layer, layer, layer, layer)
    return jax.shard_map(local, mesh=mesh, in_specs=in_specs, out_specs=out_specs, check_vma=False)
```

```python
import functools

import jax
import jax.numpy as jnp
from jax import lax
from jax.experimental import pallas as pl
from jax.experimental.pallas import tpu as pltpu
from jax.sharding import PartitionSpec as P

HEADS = 8
HEAD_DIM = 64
SLOTS = 128
STEP_TOKENS = 6
PAIR = 2 * HEAD_DIM
NEGATIVE = -1e30
EPS = 1e-05
SCALE = HEAD_DIM ** (-0.5)
GELU_A = 0.7978845608028654
GELU_B = 0.7978845608028654 * 0.044715
CHUNK = 2
MESH = pl.DeviceIdType.MESH
BF = jnp.bfloat16
F32 = jnp.float32


def dot(a, b):
    return jnp.dot(a, b, preferred_element_type=F32)


def dot_t(a, b):
    return lax.dot_general(a, b, (((1,), (1,)), ((), ())), preferred_element_type=F32)


def t_dot(a, b):
    return lax.dot_general(a, b, (((0,), (0,)), ((), ())), preferred_element_type=F32)


def layer_kernel(
    seqs,
    chips,
    start_ref,
    cond_ref,
    valid_ref,
    tok_ref,
    cot_ref,
    qkv_in,
    out_in,
    up_in,
    down_in,
    gain_ref,
    y_out,
    dx_out,
    qkv_out,
    out_out,
    up_out,
    down_out,
    gain_out,
    qkv_w,
    out_w,
    up_w,
    down_w,
    x_buf,
    d_buf,
    y_buf,
    n1_buf,
    z_buf,
    p_buf,
    o_buf,
    n2_buf,
    act_buf,
    der_buf,
    da_buf,
    rs_buf,
    rs2_buf,
    dh_buf,
    do_buf,
    dz_buf,
    lhs_t,
    grads,
    sib,
    gain_acc,
    gain_own,
    gain_sib,
    gain_all,
    in_sem,
    w_sem,
    send_sem,
    recv_sem,
    yo_sem,
    xo_sem,
    sib_send,
    sib_recv,
    ring_send,
    rs_recv,
    ag_recv,
    fwd_send,
    fwd_recv,
    gain_send,
    gain_recv,
    gsib_sem,
    go_sem,
    ready,
    freed,
):
    section = lax.axis_index("section")
    batch = lax.axis_index("batch")
    first = section == 0
    second = section == 1
    partner = (1 - section, batch)
    core = lax.rem(batch, 2)
    chip = batch // 2
    half_ring = chips // 2
    place = jnp.where(chip % 2 == 0, chip // 2, chips - 1 - chip // 2)

    def at_place(p):
        c = jnp.where(p < half_ring, 2 * p, 2 * (chips - 1 - p) + 1)
        return (section, 2 * c + core)

    right = at_place(lax.rem(place + 1, chips))
    left = at_place(lax.rem(place + chips - 1, chips))
    ahead = (right, left)
    sibling = (section, batch + 1 - 2 * core)
    segments = grads.shape[0]
    prow = grads.shape[3]
    d = x_buf.shape[1]
    ff = act_buf.shape[1]
    rows = CHUNK * SLOTS
    tile = d
    chunks = seqs // CHUNK
    total = seqs * SLOTS

    weights = [
        pltpu.make_async_copy(src, dst, w_sem.at[i])
        for i, (src, dst) in enumerate(
            ((qkv_in, qkv_w), (out_in, out_w), (up_in, up_w), (down_in, down_w))
        )
    ]
    early, late = pl.ds(0, rows), pl.ds(rows, total - rows)
    load_x = pltpu.make_async_copy(tok_ref.at[early], x_buf.at[early], in_sem.at[0])
    load_rest = pltpu.make_async_copy(tok_ref.at[late], x_buf.at[late], in_sem.at[1])
    load_d = pltpu.make_async_copy(cot_ref, d_buf, in_sem.at[0])

    @pl.when(first)
    def _():
        load_x.start()

    for copy in weights:
        copy.start()

    @pl.when(first)
    def _():
        load_rest.start()

    @pl.when(second)
    def _():
        load_d.start()

    barrier = pltpu.get_barrier_semaphore()
    for other in (partner, sibling, left, right):
        pl.semaphore_signal(barrier, inc=1, device_id=other, device_id_type=MESH)

    gain_acc[...] = jnp.zeros_like(gain_acc)
    grads[...] = jnp.zeros_like(grads)

    @pl.when(first)
    def _():
        load_x.wait()

    @pl.when(second)
    def _():
        load_d.wait()

    weights[0].wait()
    pl.semaphore_wait(barrier, 4)

    lane = lax.broadcasted_iota(jnp.int32, (1, PAIR), 1)
    low = jnp.where(lane < HEAD_DIM, 1.0, 0.0).astype(BF)
    high = jnp.where(lane < HEAD_DIM, 0.0, 1.0).astype(BF)
    head_row = lax.broadcasted_iota(jnp.int32, (2 * SLOTS, PAIR), 0) < SLOTS
    head_lane = lax.broadcasted_iota(jnp.int32, (2 * SLOTS, PAIR), 1) < HEAD_DIM
    minus = jnp.where(head_row == head_lane, -1.0, 0.0).astype(BF)
    scale = jnp.asarray(SCALE, BF)
    key_id = lax.broadcasted_iota(jnp.int32, (SLOTS, SLOTS), 1)
    row_id = lax.broadcasted_iota(jnp.int32, (SLOTS, SLOTS), 0)
    key_step = (key_id * 43) >> 8
    row_step = (row_id * 43) >> 8
    causal = key_step <= row_step
    diagonal = key_id == row_id
    gain0 = gain_ref[0:1, :]
    gain1 = gain_ref[1:2, :]

    def seq_rows(q, n):
        return pl.ds(pl.multiple_of(q * SLOTS, SLOTS), n * SLOTS)

    def to_second(q, n):
        r = seq_rows(q, n)
        return pltpu.make_async_remote_copy(
            src_ref=y_buf.at[r],
            dst_ref=x_buf.at[r],
            send_sem=send_sem.at[q],
            recv_sem=recv_sem.at[q],
            device_id=partner,
            device_id_type=MESH,
        )

    def to_first(q, n):
        r = seq_rows(q, n)
        return pltpu.make_async_remote_copy(
            src_ref=x_buf.at[r],
            dst_ref=d_buf.at[r],
            send_sem=send_sem.at[q],
            recv_sem=recv_sem.at[q],
            device_id=partner,
            device_id_type=MESH,
        )

    def store_y(q, n):
        r = seq_rows(q, n)
        return pltpu.make_async_copy(y_buf.at[r], y_out.at[r], yo_sem.at[q])

    def store_dx(q, n):
        r = seq_rows(q, n)
        return pltpu.make_async_copy(x_buf.at[r], dx_out.at[r], xo_sem.at[q])

    def norm(v, gain):
        mean = jnp.mean(v, axis=-1, keepdims=True)
        c = v - mean
        var = jnp.mean(c * c, axis=-1, keepdims=True)
        rs = lax.rsqrt(var + EPS)
        return (c * rs * gain).astype(BF), rs

    def norm_back(dn, n, gain, rs):
        xhat = n.astype(F32) * (1.0 / gain)
        w = dn * gain
        dgain = jnp.sum((dn * xhat).reshape(-1, 8, d), axis=0)
        m1 = jnp.mean(w, axis=-1, keepdims=True)
        m2 = jnp.mean(w * xhat, axis=-1, keepdims=True)
        return rs * (w - m1 - xhat * m2), dgain

    def halves(v):
        return jnp.concatenate([v * low, v * high], axis=0)

    def turned(v):
        return jnp.concatenate([v[:, :SLOTS].T, v[:, SLOTS:].T], axis=1)

    def forward_attention(start, n):
        r = seq_rows(start, n)
        n1, rs1 = norm(x_buf[r, :].astype(F32), gain0)
        n1_buf[r, :] = n1
        rs_buf[r, :] = rs1
        yield
        for c in range(3):
            z_buf[r, c * d : (c + 1) * d] = dot(n1, qkv_w[:, c * d : (c + 1) * d]).astype(BF)
            yield
        for s in range(n):
            seq = start + s
            rs = pl.ds(pl.multiple_of(seq * SLOTS, SLOTS), SLOTS)
            live = key_id < valid_ref[seq] * STEP_TOKENS
            recent = key_step >= start_ref[seq] - cond_ref[seq]
            allowed = (causal & live & recent) | diagonal
            allowed = jnp.concatenate([allowed, allowed], axis=0)
            for p in range(0, HEADS // 2, 2):
                at = p * PAIR
                q = [z_buf[rs, pl.ds(at + j * PAIR, PAIR)] * scale for j in range(2)]
                k = [halves(z_buf[rs, pl.ds(d + at + j * PAIR, PAIR)]) for j in range(2)]
                v = [halves(z_buf[rs, pl.ds(2 * d + at + j * PAIR, PAIR)]) for j in range(2)]
                nil = jnp.zeros_like(q[0])
                spread = jnp.concatenate(
                    [jnp.concatenate([q[0], nil], axis=1), jnp.concatenate([nil, q[1]], axis=1)],
                    axis=0,
                )
                sc = dot_t(spread, jnp.concatenate(k, axis=1))
                parts = []
                for h in range(2):
                    sh = jnp.where(allowed, sc[:, h * SLOTS : (h + 1) * SLOTS], NEGATIVE)
                    e = jnp.exp(sh - jnp.max(sh, axis=-1, keepdims=True))
                    parts.append((e / jnp.sum(e, axis=-1, keepdims=True)).astype(BF))
                pr = jnp.concatenate(parts, axis=1)
                p_buf[seq * (HEADS // 2) + p] = pr[:SLOTS]
                p_buf[seq * (HEADS // 2) + p + 1] = pr[SLOTS:]
                mixed = dot(pr, jnp.concatenate(v, axis=1)).astype(BF)
                o_buf[rs, at : at + PAIR] = mixed[:SLOTS, :PAIR]
                o_buf[rs, at + PAIR : at + 2 * PAIR] = mixed[SLOTS:, PAIR:]
                yield

    def forward_mlp(start, n):
        r = seq_rows(start, n)
        h = x_buf[r, :].astype(F32) + dot(o_buf[r, :], out_w[...])
        yield
        n2, rs2 = norm(h, gain1)
        n2_buf[r, :] = n2
        rs2_buf[r, :] = rs2
        yield
        acc = h
        for f in range(0, ff, tile // 2):
            part = slice(f, f + tile // 2)
            u = dot(n2, up_w[:, part])
            sq = u * u
            t = jnp.tanh(u * (GELU_A + GELU_B * sq))
            hs = 0.5 + 0.5 * t
            g = u * hs
            act = g.astype(BF)
            act_buf[r, part] = act
            slope = 2.0 * GELU_A + 6.0 * GELU_B * sq
            der_buf[r, part] = (hs + slope * (g - g * hs)).astype(BF)
            acc = acc + dot(act, down_w[part, :])
            yield
        y_buf[r, :] = acc.astype(BF)
        yield

    def backward_mlp(start):
        r = seq_rows(start, CHUNK)
        dm = d_buf[r, :]
        for f in range(0, ff, tile):
            dg = dot_t(dm, down_w[f : f + tile, :])
            der_buf[r, f : f + tile] = (der_buf[r, f : f + tile].astype(F32) * dg).astype(BF)
            yield
        dn2 = dot_t(der_buf[r, :], up_w[...])
        yield
        dh_norm, dgain1 = norm_back(dn2, n2_buf[r, :], gain1, rs2_buf[r, :])
        gain_acc[1] += dgain1
        dh = dm.astype(F32) + dh_norm
        da = dh.astype(BF)
        da_buf[r, :] = da
        yield
        dout = dot_t(da, out_w[...]).astype(BF)
        yield
        dh_buf[...] = dh
        do_buf[...] = dout

    def backward_attention(start):
        r = seq_rows(start, CHUNK)
        for s in range(CHUNK):
            seq = start + s
            rs = pl.ds(pl.multiple_of(seq * SLOTS, SLOTS), SLOTS)
            rc = pl.ds(s * SLOTS, SLOTS)
            pairs = []
            for at in range(0, HEADS // 2, 2):
                for p in (at, at + 1):
                    cq = pl.ds(p * PAIR, PAIR)
                    do = do_buf[rc, cq]
                    pr = p_buf[seq * (HEADS // 2) + p]
                    q = z_buf[rs, cq] * scale
                    k = z_buf[rs, pl.ds(d + p * PAIR, PAIR)] * scale
                    v = z_buf[rs, pl.ds(2 * d + p * PAIR, PAIR)]
                    both = jnp.concatenate([do, do * o_buf[rs, cq]], axis=1)
                    against = jnp.concatenate([halves(v), minus], axis=1)
                    ds = (pr.astype(F32) * dot_t(both, against)).astype(BF)
                    pairs.append((ds, k, turned(ds), q, turned(pr), do))
                yield
            for at in range(0, HEADS // 2, 2):
                one, two = pairs[at], pairs[at + 1]
                for c in range(3):
                    left_side = jnp.concatenate([one[2 * c], two[2 * c]], axis=0)
                    right_side = jnp.concatenate(
                        [halves(one[2 * c + 1]), halves(two[2 * c + 1])], axis=1
                    )
                    res = dot(left_side, right_side).astype(BF)
                    col = c * d + at * PAIR
                    dz_buf[rc, col : col + PAIR] = res[:SLOTS, :PAIR]
                    dz_buf[rc, col + PAIR : col + 2 * PAIR] = res[SLOTS:, PAIR:]
                yield
        dz = dz_buf[...]
        z_buf[r, :] = dz
        dn1 = dot_t(dz, qkv_w[...])
        yield
        dx_norm, dgain0 = norm_back(dn1, n1_buf[r, :], gain0, rs_buf[r, :])
        gain_acc[0] += dgain0
        x_buf[r, :] = (dh_buf[...] + dx_norm).astype(BF)
        yield

    def together(*parts):
        parts = list(parts)
        while parts:
            parts = [part for part in parts if next(part, True) is None]

    def forward(start, n):
        @pl.when(second)
        def _():
            to_second(start, n).wait_recv()

        if n == CHUNK:

            @pl.when(first & (start == CHUNK))
            def _():
                load_rest.wait()

        together(forward_attention(start, n))
        if n == 1:

            @pl.when(start == 0)
            def _():
                for copy in weights[1:]:
                    copy.wait()

        together(forward_mlp(start, n))

        @pl.when(first)
        def _():
            to_second(start, n).start()

        store_y(start, n).start()

    def backward(start):
        @pl.when(first)
        def _():
            to_first(start, CHUNK).wait_recv()

        together(backward_mlp(start))
        together(backward_attention(start))

        @pl.when(second)
        def _():
            to_first(start, CHUNK).start()

        store_dx(start, CHUNK).start()

    part = total // 4
    blocks = ff // d
    per = d // (2 * prow)

    group = grads.shape[1] * 2 * prow // d

    def put(block, value):
        seg = block // group
        where = pl.ds((block % group) * per, per)
        value = value.reshape(per, 2, prow, d) + grads[seg, where].astype(F32)
        grads[seg, where] = value.astype(BF)

    def weight_grads(quarter, done):
        r = pl.ds(pl.multiple_of(quarter * part, part), part)
        for c in range(blocks):
            lhs_t[...] = act_buf[r, c * d : (c + 1) * d].T
            put(c, dot(lhs_t[...], d_buf[r, :]))
            done(c)
        lhs_t[...] = n2_buf[r, :].T
        for c in range(blocks):
            put(blocks + c, dot(lhs_t[...], der_buf[r, c * d : (c + 1) * d]))
            done(blocks + c)
        lhs_t[...] = n1_buf[r, :].T
        for c in range(3):
            put(2 * blocks + c, dot(lhs_t[...], z_buf[r, c * d : (c + 1) * d]))
            done(2 * blocks + c)
        lhs_t[...] = o_buf[r, :].T
        put(2 * blocks + 3, dot(lhs_t[...], da_buf[r, :]))
        done(2 * blocks + 3)

    per_part = chunks // 4

    def step(t, carry):
        u = t - (chunks + 1)
        turn = lax.rem(u, per_part + 1)
        quarter0 = u // (per_part + 1)
        forth0 = t <= chunks
        work0 = jnp.where(forth0, 0, jnp.where(turn < per_part, 1, 2))
        pair0 = jnp.where(forth0, t - 1, quarter0 * per_part + turn)
        work1 = jnp.where(t < 2, 0, jnp.where(t <= 2 * chunks, 1 - lax.rem(t, 2), 2))
        pair1 = (t - 1) // 2
        work = jnp.where(first, work0, work1)
        start = CHUNK * jnp.where(first, pair0, pair1)
        quarter = jnp.where(first, quarter0, t - (2 * chunks + 1))

        @pl.when(t < 2)
        def _():
            forward(t, 1)

        @pl.when((t >= 2) & (work == 0))
        def _():
            forward(start, CHUNK)

        @pl.when((t >= 2) & (work == 1))
        def _():
            backward(start)

        @pl.when(work == 2)
        def _():
            weight_grads(quarter, lambda block: None)

        return carry

    lax.fori_loop(0, 2 * chunks + 4, step, 0)
    for other in (left, right):
        pl.semaphore_signal(ready, inc=1, device_id=other, device_id_type=MESH)

    width = d // 2
    per_block = SLOTS // prow

    def columns(way):
        return pl.ds(way * width, width)

    def exchange(seg, j):
        off = (j + 1) // 2
        k = lax.rem(jnp.where(j % 2 == 1, place + chips - off, place + off), chips)
        return pltpu.make_async_remote_copy(
            src_ref=grads.at[seg, k, 1 - core],
            dst_ref=sib.at[seg, k],
            send_sem=sib_send.at[seg, j],
            recv_sem=sib_recv.at[seg, j],
            device_id=sibling,
            device_id_type=MESH,
        )

    def exchange_start(seg):
        lax.fori_loop(0, chips, lambda j, c: (exchange(seg, j).start(), c)[1], 0)

    def landing(seg, way, s):
        q = (seg * 2 + way) * (chips - 1) + s
        row = pl.multiple_of((q % per_block) * prow, prow)
        return p_buf.at[q // per_block, pl.ds(row, prow)]

    def ring(src, dst, seg, way, recv):
        return pltpu.make_async_remote_copy(
            src_ref=src,
            dst_ref=dst,
            send_sem=ring_send.at[seg, way],
            recv_sem=recv,
            device_id=ahead[way],
            device_id_type=MESH,
        )

    def gather_copy(seg, way, k, s):
        spot = grads.at[seg, k, core, :, columns(way)]
        return ring(spot, spot, seg, way, ag_recv.at[seg, way, s])

    def forward_copy(seg, way, k, f):
        spot = grads.at[seg, k, core, :, columns(way)]
        return pltpu.make_async_remote_copy(
            src_ref=spot,
            dst_ref=spot,
            send_sem=fwd_send.at[seg, way],
            recv_sem=fwd_recv.at[seg, way, f],
            device_id=sibling,
            device_id_type=MESH,
        )

    def first_copy(seg, way):
        return ring(
            sib.at[seg, place, :, columns(way)],
            landing(seg, way, 0),
            seg,
            way,
            rs_recv.at[seg, way, 0],
        )

    def ring_start(seg):
        exchange(seg, 0).wait()
        mine = grads[seg, place, core].astype(F32) + sib[seg, place].astype(F32)
        sib[seg, place] = mine.astype(BF)
        for way in range(2):
            first_copy(seg, way).start()

    def reduce_tick(seg, s, last):
        if not last:

            @pl.when(s < chips // 2)
            def _():
                exchange(seg, 2 * s + 1).wait()

            @pl.when(s < chips // 2 - 1)
            def _():
                exchange(seg, 2 * s + 2).wait()

        for way in range(2):
            if way == 0:
                k = lax.rem(place + 2 * chips - 1 - s, chips)
            else:
                k = lax.rem(place + 1 + s, chips)
            here = landing(seg, way, s)
            ring(here, here, seg, way, rs_recv.at[seg, way, s]).wait()
            value = (
                here[...].astype(F32)
                + grads[seg, k, core, :, columns(way)].astype(F32)
                + sib[seg, k, :, columns(way)].astype(F32)
            ).astype(BF)
            if last:
                grads[seg, k, core, :, columns(way)] = value
                gather_copy(seg, way, k, 0).start()
                forward_copy(seg, way, k, 0).start()
            else:
                here[...] = value
                ring(
                    here, landing(seg, way, s + 1), seg, way, rs_recv.at[seg, way, s + 1]
                ).start()

    def gather_tick(seg, s, last):
        for way in range(2):
            k = lax.rem(place + chips - s, chips) if way == 0 else lax.rem(place + s, chips)
            gather_copy(seg, way, k, s).wait()
            if not last:
                gather_copy(seg, way, k, s + 1).start()
            forward_copy(seg, way, k, 0).wait_send()
            forward_copy(seg, way, k, s + 1).start()

    def gain_copy(s):
        spot = gain_all.at[lax.rem(place + chips - s, chips)]
        return pltpu.make_async_remote_copy(
            src_ref=spot,
            dst_ref=spot,
            send_sem=gain_send,
            recv_sem=gain_recv.at[s],
            device_id=right,
            device_id_type=MESH,
        )

    gain_swap = pltpu.make_async_remote_copy(
        src_ref=gain_own,
        dst_ref=gain_sib,
        send_sem=gsib_sem.at[0],
        recv_sem=gsib_sem.at[1],
        device_id=sibling,
        device_id_type=MESH,
    )
    gain_own[...] = jnp.zeros_like(gain_own)
    gain_own[0:2, :] = jnp.sum(gain_acc[...], axis=1)
    gain_swap.start()

    def ring_begin(seg):
        if seg == 0:
            pl.semaphore_wait(ready, 2)
            gain_swap.wait()
            gain_all[place] = gain_own[...] + gain_sib[...]
            gain_copy(0).start()
        ring_start(seg)

    def done(block):
        seg, rest = divmod(block + 1, group)
        seg -= 1
        if rest:
            return
        exchange_start(seg)
        if seg > 0:
            ring_begin(seg - 1)

    weight_grads(3, done)
    ring_begin(segments - 1)

    def reduce_step(s, carry):
        for seg in range(segments):
            reduce_tick(seg, s, False)
        @pl.when(s == chips // 2 - 1)
        def _():
            pl.semaphore_signal(freed, inc=1, device_id=sibling, device_id_type=MESH)

        gain_copy(s).wait()
        gain_copy(s + 1).start()
        return carry

    lax.fori_loop(0, chips - 2, reduce_step, 0)
    pl.semaphore_wait(freed, 1)
    for seg in range(segments):
        reduce_tick(seg, chips - 2, True)
    gain_copy(chips - 2).wait()

    def gather_step(s, carry):
        for seg in range(segments):
            gather_tick(seg, s, False)
        return carry

    lax.fori_loop(0, chips - 2, gather_step, 0)
    for seg in range(segments):
        gather_tick(seg, chips - 2, True)

    gains = gain_all[0]
    for k in range(1, chips):
        gains = gains + gain_all[k]
    gain_out[...] = gains[0:2, :]

    def results(seg):
        copies = []
        for block in range(seg * group, (seg + 1) * group):
            kind, c = divmod(block, blocks)
            if kind == 0:
                dst = down_out.at[pl.ds(c * per, per)]
            elif kind == 1:
                dst = up_out.at[:, :, :, c * d : (c + 1) * d]
            elif c < 3:
                dst = qkv_out.at[:, :, :, c * d : (c + 1) * d]
            else:
                dst = out_out
            src = grads.at[seg, pl.ds((block % group) * per, per)]
            copies.append(pltpu.make_async_copy(src, dst, go_sem.at[block]))
        return copies

    for seg in range(segments):
        for way in range(2):
            forward_copy(seg, way, 0, 0).wait_send()

        def arrived(f, carry, seg=seg):
            for way in range(2):
                forward_copy(seg, way, 0, f).wait_recv()
            return carry

        lax.fori_loop(0, chips, arrived, 0)
        for copy in results(seg):
            copy.start()
    for seg in range(segments):
        for copy in results(seg):
            copy.wait()

    def finish(i, carry):
        start = i * CHUNK

        @pl.when(first & (i > 0))
        def _():
            to_second(start, CHUNK).wait_send()

        @pl.when(second)
        def _():
            to_first(start, CHUNK).wait_send()

        @pl.when(i > 0)
        def _():
            store_y(start, CHUNK).wait()

        store_dx(start, CHUNK).wait()
        return carry

    lax.fori_loop(0, chunks, finish, 0)
    for q in range(CHUNK):

        @pl.when(first)
        def _(q=q):
            to_second(q, 1).wait_send()

        store_y(q, 1).wait()


def finish_kernel(parts, *refs):
    count = len(parts)
    sources, results = refs[:count], refs[count : 2 * count]
    lows, wides = refs[2 * count : 3 * count], list(refs[3 * count : -2])
    load_sem, store_sem = refs[-2:]
    pieces = []
    for src, dst, low, steps in zip(sources, results, lows, parts, strict=True):
        wide = low if dst.dtype == low.dtype else wides.pop(0)
        tall = src.shape[0] // steps
        for t in range(0, src.shape[0], tall):
            r = pl.ds(t, tall)
            n = len(pieces)
            load = pltpu.make_async_copy(src.at[r], low.at[r], load_sem.at[n])
            store = pltpu.make_async_copy(wide.at[r], dst.at[r], store_sem.at[n])
            pieces.append((load, store, low, wide, r))
    for load, _, _, _, _ in pieces:
        load.start()
    for load, store, low, wide, r in pieces:
        load.wait()
        if wide is not low:
            wide[r, :] = low[r, :].astype(F32)
        store.start()
    for _, store, _, _, _ in pieces:
        store.wait()


def finish(rows, grads):
    hbm = pl.BlockSpec(memory_space=pl.ANY)
    arrays = (*grads, *rows)
    types = [F32] * len(grads) + [a.dtype for a in rows]
    parts = [4] * len(grads) + [2 if a.shape[0] > 2 else 1 for a in rows]
    return pl.pallas_call(
        functools.partial(finish_kernel, parts),
        in_specs=[hbm] * len(arrays),
        out_specs=[hbm] * len(arrays),
        out_shape=[jax.ShapeDtypeStruct(a.shape, t) for a, t in zip(arrays, types, strict=True)],
        scratch_shapes=[pltpu.VMEM(a.shape, a.dtype) for a in arrays]
        + [pltpu.VMEM(g.shape, F32) for g in grads]
        + [pltpu.SemaphoreType.DMA((sum(parts),))] * 2,
        compiler_params=pltpu.CompilerParams(vmem_limit_bytes=60 * 2**20),
        name="finish",
    )(*arrays)


def local(
    tokens,
    start_steps,
    cond_counts,
    valid_steps,
    qkv_weight,
    out_weight,
    up_weight,
    down_weight,
    norm_gains,
    cotangent,
):
    seqs, slots, d = tokens.shape
    ff = up_weight.shape[2]
    rows = seqs * slots
    chips = lax.axis_size("batch") // 2
    group = 4
    segments = (2 * ff // d + 4) // group
    prow = group * d // (2 * chips)
    per = d // (2 * prow)
    vmem = pl.BlockSpec(memory_space=pltpu.VMEM)
    smem = pl.BlockSpec(memory_space=pltpu.SMEM)
    hbm = pl.BlockSpec(memory_space=pl.ANY)
    y, dx, qkv_grad, out_grad, up_grad, down_grad, gains = pl.pallas_call(
        functools.partial(layer_kernel, seqs, chips),
        out_shape=(
            jax.ShapeDtypeStruct((rows, d), BF),
            jax.ShapeDtypeStruct((rows, d), BF),
            jax.ShapeDtypeStruct((per, 2, prow, 3 * d), BF),
            jax.ShapeDtypeStruct((per, 2, prow, d), BF),
            jax.ShapeDtypeStruct((per, 2, prow, ff), BF),
            jax.ShapeDtypeStruct((ff // (2 * prow), 2, prow, d), BF),
            jax.ShapeDtypeStruct((2, d), F32),
        ),
        in_specs=[smem] * 3 + [hbm] * 6 + [vmem],
        out_specs=(hbm, hbm, hbm, hbm, hbm, hbm, vmem),
        scratch_shapes=[
            pltpu.VMEM((d, 3 * d), BF),
            pltpu.VMEM((d, d), BF),
            pltpu.VMEM((d, ff), BF),
            pltpu.VMEM((ff, d), BF),
            pltpu.VMEM((rows, d), BF),
            pltpu.VMEM((rows, d), BF),
            pltpu.VMEM((rows, d), BF),
            pltpu.VMEM((rows, d), BF),
            pltpu.VMEM((rows, 3 * d), BF),
            pltpu.VMEM((seqs * HEADS // 2, SLOTS, 2 * SLOTS), BF),
            pltpu.VMEM((rows, d), BF),
            pltpu.VMEM((rows, d), BF),
            pltpu.VMEM((rows, ff), BF),
            pltpu.VMEM((rows, ff), BF),
            pltpu.VMEM((rows, d), BF),
            pltpu.VMEM((rows, 1), F32),
            pltpu.VMEM((rows, 1), F32),
            pltpu.VMEM((CHUNK * SLOTS, d), F32),
            pltpu.VMEM((CHUNK * SLOTS, d), BF),
            pltpu.VMEM((CHUNK * SLOTS, 3 * d), BF),
            pltpu.VMEM((d, rows // 4), BF),
            pltpu.VMEM((segments, chips, 2, prow, d), BF),
            pltpu.VMEM((segments, chips, prow, d), BF),
            pltpu.VMEM((2, 8, d), F32),
            pltpu.VMEM((8, d), F32),
            pltpu.VMEM((8, d), F32),
            pltpu.VMEM((chips, 8, d), F32),
            pltpu.SemaphoreType.DMA((2,)),
            pltpu.SemaphoreType.DMA((4,)),
            pltpu.SemaphoreType.DMA((seqs,)),
            pltpu.SemaphoreType.DMA((seqs,)),
            pltpu.SemaphoreType.DMA((seqs,)),
            pltpu.SemaphoreType.DMA((seqs,)),
            pltpu.SemaphoreType.DMA((segments, chips)),
            pltpu.SemaphoreType.DMA((segments, chips)),
            pltpu.SemaphoreType.DMA((segments, 2)),
            pltpu.SemaphoreType.DMA((segments, 2, chips - 1)),
            pltpu.SemaphoreType.DMA((segments, 2, chips - 1)),
            pltpu.SemaphoreType.DMA((segments, 2)),
            pltpu.SemaphoreType.DMA((segments, 2, chips)),
            pltpu.SemaphoreType.DMA,
            pltpu.SemaphoreType.DMA((chips - 1,)),
            pltpu.SemaphoreType.DMA((2,)),
            pltpu.SemaphoreType.DMA((segments * group,)),
            pltpu.SemaphoreType.REGULAR,
            pltpu.SemaphoreType.REGULAR,
        ],
        compiler_params=pltpu.CompilerParams(
            collective_id=0, has_side_effects=True, vmem_limit_bytes=63 * 2**20
        ),
        name="layer",
    )(
        start_steps,
        cond_counts,
        valid_steps,
        tokens.reshape(rows, d),
        cotangent.reshape(rows, d),
        qkv_weight[0],
        out_weight[0],
        up_weight[0],
        down_weight[0],
        norm_gains[0],
    )
    grads = (
        down_grad.reshape(ff, d),
        up_grad.reshape(d, ff),
        qkv_grad.reshape(d, 3 * d),
        out_grad.reshape(d, d),
    )
    down_grad, up_grad, qkv_grad, out_grad, y, dx, gains = finish((y, dx, gains), grads)
    shape = (1, seqs, slots, d)
    return (
        y.reshape(shape),
        dx.reshape(shape),
        qkv_grad[None],
        out_grad[None],
        up_grad[None],
        down_grad[None],
        gains[None],
    )


def solution(mesh):
    rows = P("batch", None, None)
    flat = P("batch")
    layer = P("section", None, None)
    in_specs = (rows, flat, flat, flat, layer, layer, layer, layer, layer, rows)
    both = P("section", "batch", None, None)
    out_specs = (both, both, layer, layer, layer, layer, layer)
    return jax.shard_map(local, mesh=mesh, in_specs=in_specs, out_specs=out_specs, check_vma=False)
```

```python
import functools

import jax
import jax.numpy as jnp
from jax import lax
from jax.experimental import pallas as pl
from jax.experimental.pallas import tpu as pltpu
from jax.sharding import PartitionSpec as P

HEADS = 8
HEAD_DIM = 64
SLOTS = 128
STEP_TOKENS = 6
PAIR = 2 * HEAD_DIM
NEGATIVE = -1e30
EPS = 1e-05
SCALE = HEAD_DIM ** (-0.5)
GELU_A = 0.7978845608028654
GELU_B = 0.7978845608028654 * 0.044715
CHUNK = 2
MESH = pl.DeviceIdType.MESH
BF = jnp.bfloat16
F32 = jnp.float32


def dot(a, b):
    return jnp.dot(a, b, preferred_element_type=F32)


def dot_t(a, b):
    return lax.dot_general(a, b, (((1,), (1,)), ((), ())), preferred_element_type=F32)


def t_dot(a, b):
    return lax.dot_general(a, b, (((0,), (0,)), ((), ())), preferred_element_type=F32)


def layer_kernel(
    seqs,
    chips,
    start_ref,
    cond_ref,
    valid_ref,
    tok_ref,
    cot_ref,
    qkv_in,
    out_in,
    up_in,
    down_in,
    gain_ref,
    y_out,
    dx_out,
    qkv_out,
    out_out,
    up_out,
    down_out,
    gain_out,
    qkv_w,
    out_w,
    up_w,
    down_w,
    x_buf,
    d_buf,
    y_buf,
    n1_buf,
    z_buf,
    p_buf,
    o_buf,
    n2_buf,
    act_buf,
    der_buf,
    da_buf,
    rs_buf,
    rs2_buf,
    dh_buf,
    do_buf,
    dz_buf,
    lhs_t,
    grads,
    sib,
    gain_acc,
    gain_own,
    gain_sib,
    gain_all,
    in_sem,
    w_sem,
    send_sem,
    recv_sem,
    yo_sem,
    xo_sem,
    sib_send,
    sib_recv,
    ring_send,
    rs_recv,
    ag_recv,
    fwd_send,
    fwd_recv,
    gain_send,
    gain_recv,
    gsib_sem,
    go_sem,
    ready,
    freed,
):
    section = lax.axis_index("section")
    batch = lax.axis_index("batch")
    first = section == 0
    second = section == 1
    partner = (1 - section, batch)
    core = lax.rem(batch, 2)
    chip = batch // 2
    half_ring = chips // 2
    place = jnp.where(chip % 2 == 0, chip // 2, chips - 1 - chip // 2)

    def at_place(p):
        c = jnp.where(p < half_ring, 2 * p, 2 * (chips - 1 - p) + 1)
        return (section, 2 * c + core)

    right = at_place(lax.rem(place + 1, chips))
    left = at_place(lax.rem(place + chips - 1, chips))
    ahead = (right, left)
    sibling = (section, batch + 1 - 2 * core)
    segments = grads.shape[0]
    prow = grads.shape[3]
    d = x_buf.shape[1]
    ff = act_buf.shape[1]
    rows = CHUNK * SLOTS
    tile = d
    chunks = seqs // CHUNK
    total = seqs * SLOTS

    weights = [
        pltpu.make_async_copy(src, dst, w_sem.at[i])
        for i, (src, dst) in enumerate(
            ((qkv_in, qkv_w), (out_in, out_w), (up_in, up_w), (down_in, down_w))
        )
    ]
    early, late = pl.ds(0, rows), pl.ds(rows, total - rows)
    load_x = pltpu.make_async_copy(tok_ref.at[early], x_buf.at[early], in_sem.at[0])
    load_rest = pltpu.make_async_copy(tok_ref.at[late], x_buf.at[late], in_sem.at[1])
    load_d = pltpu.make_async_copy(cot_ref, d_buf, in_sem.at[0])

    @pl.when(first)
    def _():
        load_x.start()

    for copy in weights:
        copy.start()

    @pl.when(first)
    def _():
        load_rest.start()

    @pl.when(second)
    def _():
        load_d.start()

    barrier = pltpu.get_barrier_semaphore()
    for other in (partner, sibling, left, right):
        pl.semaphore_signal(barrier, inc=1, device_id=other, device_id_type=MESH)

    gain_acc[...] = jnp.zeros_like(gain_acc)
    grads[...] = jnp.zeros_like(grads)

    @pl.when(first)
    def _():
        load_x.wait()

    @pl.when(second)
    def _():
        load_d.wait()

    weights[0].wait()
    pl.semaphore_wait(barrier, 4)

    lane = lax.broadcasted_iota(jnp.int32, (1, PAIR), 1)
    low = jnp.where(lane < HEAD_DIM, 1.0, 0.0).astype(BF)
    high = jnp.where(lane < HEAD_DIM, 0.0, 1.0).astype(BF)
    head_row = lax.broadcasted_iota(jnp.int32, (2 * SLOTS, PAIR), 0) < SLOTS
    head_lane = lax.broadcasted_iota(jnp.int32, (2 * SLOTS, PAIR), 1) < HEAD_DIM
    minus = jnp.where(head_row == head_lane, -1.0, 0.0).astype(BF)
    scale = jnp.asarray(SCALE, BF)
    key_id = lax.broadcasted_iota(jnp.int32, (SLOTS, SLOTS), 1)
    row_id = lax.broadcasted_iota(jnp.int32, (SLOTS, SLOTS), 0)
    key_step = (key_id * 43) >> 8
    row_step = (row_id * 43) >> 8
    causal = key_step <= row_step
    diagonal = key_id == row_id
    gain0 = gain_ref[0:1, :]
    gain1 = gain_ref[1:2, :]

    def seq_rows(q, n):
        return pl.ds(pl.multiple_of(q * SLOTS, SLOTS), n * SLOTS)

    def to_second(q, n):
        r = seq_rows(q, n)
        return pltpu.make_async_remote_copy(
            src_ref=y_buf.at[r],
            dst_ref=x_buf.at[r],
            send_sem=send_sem.at[q],
            recv_sem=recv_sem.at[q],
            device_id=partner,
            device_id_type=MESH,
        )

    def to_first(q, n):
        r = seq_rows(q, n)
        return pltpu.make_async_remote_copy(
            src_ref=x_buf.at[r],
            dst_ref=d_buf.at[r],
            send_sem=send_sem.at[q],
            recv_sem=recv_sem.at[q],
            device_id=partner,
            device_id_type=MESH,
        )

    def store_y(q, n):
        r = seq_rows(q, n)
        return pltpu.make_async_copy(y_buf.at[r], y_out.at[r], yo_sem.at[q])

    def store_dx(q, n):
        r = seq_rows(q, n)
        return pltpu.make_async_copy(x_buf.at[r], dx_out.at[r], xo_sem.at[q])

    def norm(v, gain):
        mean = jnp.mean(v, axis=-1, keepdims=True)
        c = v - mean
        var = jnp.mean(c * c, axis=-1, keepdims=True)
        rs = lax.rsqrt(var + EPS)
        return (c * rs * gain).astype(BF), rs

    def norm_back(dn, n, gain, rs):
        xhat = n.astype(F32) * (1.0 / gain)
        w = dn * gain
        dgain = jnp.sum((dn * xhat).reshape(-1, 8, d), axis=0)
        m1 = jnp.mean(w, axis=-1, keepdims=True)
        m2 = jnp.mean(w * xhat, axis=-1, keepdims=True)
        return rs * (w - m1 - xhat * m2), dgain

    def halves(v):
        return jnp.concatenate([v * low, v * high], axis=0)

    def turned(v):
        return jnp.concatenate([v[:, :SLOTS].T, v[:, SLOTS:].T], axis=1)

    def forward_attention(start, n):
        r = seq_rows(start, n)
        n1, rs1 = norm(x_buf[r, :].astype(F32), gain0)
        n1_buf[r, :] = n1
        rs_buf[r, :] = rs1
        yield
        for c in range(3):
            z_buf[r, c * d : (c + 1) * d] = dot(n1, qkv_w[:, c * d : (c + 1) * d]).astype(BF)
            yield
        for s in range(n):
            seq = start + s
            rs = pl.ds(pl.multiple_of(seq * SLOTS, SLOTS), SLOTS)
            live = key_id < valid_ref[seq] * STEP_TOKENS
            recent = key_step >= start_ref[seq] - cond_ref[seq]
            allowed = (causal & live & recent) | diagonal
            allowed = jnp.concatenate([allowed, allowed], axis=0)
            for p in range(0, HEADS // 2, 2):
                at = p * PAIR
                q = [z_buf[rs, pl.ds(at + j * PAIR, PAIR)] * scale for j in range(2)]
                k = [halves(z_buf[rs, pl.ds(d + at + j * PAIR, PAIR)]) for j in range(2)]
                v = [halves(z_buf[rs, pl.ds(2 * d + at + j * PAIR, PAIR)]) for j in range(2)]
                nil = jnp.zeros_like(q[0])
                spread = jnp.concatenate(
                    [jnp.concatenate([q[0], nil], axis=1), jnp.concatenate([nil, q[1]], axis=1)],
                    axis=0,
                )
                sc = dot_t(spread, jnp.concatenate(k, axis=1))
                parts = []
                for h in range(2):
                    sh = jnp.where(allowed, sc[:, h * SLOTS : (h + 1) * SLOTS], NEGATIVE)
                    e = jnp.exp(sh - jnp.max(sh, axis=-1, keepdims=True))
                    parts.append((e / jnp.sum(e, axis=-1, keepdims=True)).astype(BF))
                pr = jnp.concatenate(parts, axis=1)
                p_buf[seq * (HEADS // 2) + p] = pr[:SLOTS]
                p_buf[seq * (HEADS // 2) + p + 1] = pr[SLOTS:]
                mixed = dot(pr, jnp.concatenate(v, axis=1)).astype(BF)
                o_buf[rs, at : at + PAIR] = mixed[:SLOTS, :PAIR]
                o_buf[rs, at + PAIR : at + 2 * PAIR] = mixed[SLOTS:, PAIR:]
                yield

    def forward_mlp(start, n, whole):
        r = seq_rows(start, n)
        h = x_buf[r, :].astype(F32) + dot(o_buf[r, :], out_w[...])
        yield
        n2, rs2 = norm(h, gain1)
        n2_buf[r, :] = n2
        rs2_buf[r, :] = rs2
        yield
        acc = h
        if not whole:
            y_buf[r, :] = h.astype(BF)
        for f in range(0, ff, tile // 2):
            part = slice(f, f + tile // 2)
            u = dot(n2, up_w[:, part])
            sq = u * u
            t = jnp.tanh(u * (GELU_A + GELU_B * sq))
            hs = 0.5 + 0.5 * t
            g = u * hs
            act = g.astype(BF)
            act_buf[r, part] = act
            slope = 2.0 * GELU_A + 6.0 * GELU_B * sq
            der_buf[r, part] = (hs + slope * (g - g * hs)).astype(BF)
            if whole:
                acc = acc + dot(act, down_w[part, :])
            yield
        if whole:
            y_buf[r, :] = acc.astype(BF)
        yield

    def backward_mlp(start):
        r = seq_rows(start, CHUNK)
        dm = d_buf[r, :]
        for f in range(0, ff, tile):
            dg = dot_t(dm, down_w[f : f + tile, :])
            der_buf[r, f : f + tile] = (der_buf[r, f : f + tile].astype(F32) * dg).astype(BF)
            yield
        dn2 = dot_t(der_buf[r, :], up_w[...])
        yield
        dh_norm, dgain1 = norm_back(dn2, n2_buf[r, :], gain1, rs2_buf[r, :])
        gain_acc[1] += dgain1
        dh = dm.astype(F32) + dh_norm
        da = dh.astype(BF)
        da_buf[r, :] = da
        yield
        dout = dot_t(da, out_w[...]).astype(BF)
        yield
        dh_buf[...] = dh
        do_buf[...] = dout

    def backward_attention(start):
        r = seq_rows(start, CHUNK)
        for s in range(CHUNK):
            seq = start + s
            rs = pl.ds(pl.multiple_of(seq * SLOTS, SLOTS), SLOTS)
            rc = pl.ds(s * SLOTS, SLOTS)
            pairs = []
            for at in range(0, HEADS // 2, 2):
                for p in (at, at + 1):
                    cq = pl.ds(p * PAIR, PAIR)
                    do = do_buf[rc, cq]
                    pr = p_buf[seq * (HEADS // 2) + p]
                    q = z_buf[rs, cq] * scale
                    k = z_buf[rs, pl.ds(d + p * PAIR, PAIR)] * scale
                    v = z_buf[rs, pl.ds(2 * d + p * PAIR, PAIR)]
                    both = jnp.concatenate([do, do * o_buf[rs, cq]], axis=1)
                    against = jnp.concatenate([halves(v), minus], axis=1)
                    ds = (pr.astype(F32) * dot_t(both, against)).astype(BF)
                    pairs.append((ds, k, turned(ds), q, turned(pr), do))
                yield
            for at in range(0, HEADS // 2, 2):
                one, two = pairs[at], pairs[at + 1]
                for c in range(3):
                    left_side = jnp.concatenate([one[2 * c], two[2 * c]], axis=0)
                    right_side = jnp.concatenate(
                        [halves(one[2 * c + 1]), halves(two[2 * c + 1])], axis=1
                    )
                    res = dot(left_side, right_side).astype(BF)
                    col = c * d + at * PAIR
                    dz_buf[rc, col : col + PAIR] = res[:SLOTS, :PAIR]
                    dz_buf[rc, col + PAIR : col + 2 * PAIR] = res[SLOTS:, PAIR:]
                yield
        dz = dz_buf[...]
        z_buf[r, :] = dz
        dn1 = dot_t(dz, qkv_w[...])
        yield
        dx_norm, dgain0 = norm_back(dn1, n1_buf[r, :], gain0, rs_buf[r, :])
        gain_acc[0] += dgain0
        x_buf[r, :] = (dh_buf[...] + dx_norm).astype(BF)
        yield

    def together(*parts):
        parts = list(parts)
        while parts:
            parts = [part for part in parts if next(part, True) is None]

    def forward(start, n, to_next):
        if not to_next:
            to_second(start, n).wait_recv()
        together(forward_attention(start, n))
        if n == 1:

            @pl.when(start == 0)
            def _():
                for copy in weights[1:]:
                    copy.wait()

        together(forward_mlp(start, n, to_next))
        if to_next:
            to_second(start, n).start()
            store_y(start, n).start()

    def late_rows(i):
        @pl.when(second & (i < chunks))
        def _():
            r = seq_rows(i * CHUNK, CHUNK)
            y_buf[r, :] = (y_buf[r, :].astype(F32) + dot(act_buf[r, :], down_w[...])).astype(BF)
            store_y(i * CHUNK, CHUNK).start()

    def backward(start, from_next):
        if from_next:
            to_first(start, CHUNK).wait_recv()
        together(backward_mlp(start))
        together(backward_attention(start))
        if not from_next:
            to_first(start, CHUNK).start()
        store_dx(start, CHUNK).start()

    part = total // 4
    blocks = ff // d
    per = d // (2 * prow)

    group = grads.shape[1] * 2 * prow // d

    def put(block, value):
        seg = block // group
        where = pl.ds((block % group) * per, per)
        value = value.reshape(per, 2, prow, d) + grads[seg, where].astype(F32)
        grads[seg, where] = value.astype(BF)

    def weight_grads(quarter, done):
        r = pl.ds(pl.multiple_of(quarter * part, part), part)
        for c in range(blocks):
            lhs_t[...] = act_buf[r, c * d : (c + 1) * d].T
            put(c, dot(lhs_t[...], d_buf[r, :]))
            done(c)
        lhs_t[...] = n2_buf[r, :].T
        for c in range(blocks):
            put(blocks + c, dot(lhs_t[...], der_buf[r, c * d : (c + 1) * d]))
            done(blocks + c)
        lhs_t[...] = n1_buf[r, :].T
        for c in range(3):
            put(2 * blocks + c, dot(lhs_t[...], z_buf[r, c * d : (c + 1) * d]))
            done(2 * blocks + c)
        lhs_t[...] = o_buf[r, :].T
        put(2 * blocks + 3, dot(lhs_t[...], da_buf[r, :]))
        done(2 * blocks + 3)

    per_part = chunks // 4

    def times(low, high, act):
        def body(i, carry):
            act(i)
            return carry

        lax.fori_loop(low, high, body, 0)

    def early_quarter(q):
        weight_grads(q, lambda block: None)

    @pl.when(first)
    def _():
        times(0, CHUNK, lambda q: forward(q, 1, True))
        load_rest.wait()
        times(1, chunks, lambda i: forward(i * CHUNK, CHUNK, True))

        def quarter(q):
            times(0, per_part, lambda j: backward((q * per_part + j) * CHUNK, True))

            @pl.when(q < 3)
            def _():
                early_quarter(q)

        times(0, 4, quarter)

    @pl.when(second)
    def _():
        times(0, CHUNK, lambda q: forward(q, 1, False))

        def pair(i):
            @pl.when(i > 0)
            def _():
                forward(i * CHUNK, CHUNK, False)

            backward(i * CHUNK, False)

        times(0, chunks, pair)
        times(0, 3, early_quarter)

    for other in (left, right):
        pl.semaphore_signal(ready, inc=1, device_id=other, device_id_type=MESH)

    width = d // 2
    per_block = SLOTS // prow

    def columns(way):
        return pl.ds(way * width, width)

    def exchange(seg, j):
        off = (j + 1) // 2
        k = lax.rem(jnp.where(j % 2 == 1, place + chips - off, place + off), chips)
        return pltpu.make_async_remote_copy(
            src_ref=grads.at[seg, k, 1 - core],
            dst_ref=sib.at[seg, k],
            send_sem=sib_send.at[seg, j],
            recv_sem=sib_recv.at[seg, j],
            device_id=sibling,
            device_id_type=MESH,
        )

    def exchange_start(seg):
        lax.fori_loop(0, chips, lambda j, c: (exchange(seg, j).start(), c)[1], 0)

    def landing(seg, way, s):
        q = (seg * 2 + way) * (chips - 1) + s
        row = pl.multiple_of((q % per_block) * prow, prow)
        return p_buf.at[q // per_block, pl.ds(row, prow)]

    def ring(src, dst, seg, way, recv):
        return pltpu.make_async_remote_copy(
            src_ref=src,
            dst_ref=dst,
            send_sem=ring_send.at[seg, way],
            recv_sem=recv,
            device_id=ahead[way],
            device_id_type=MESH,
        )

    def gather_copy(seg, way, k, s):
        spot = grads.at[seg, k, core, :, columns(way)]
        return ring(spot, spot, seg, way, ag_recv.at[seg, way, s])

    def forward_copy(seg, way, k, f):
        spot = grads.at[seg, k, core, :, columns(way)]
        return pltpu.make_async_remote_copy(
            src_ref=spot,
            dst_ref=spot,
            send_sem=fwd_send.at[seg, way],
            recv_sem=fwd_recv.at[seg, way, f],
            device_id=sibling,
            device_id_type=MESH,
        )

    def first_copy(seg, way):
        return ring(
            sib.at[seg, place, :, columns(way)],
            landing(seg, way, 0),
            seg,
            way,
            rs_recv.at[seg, way, 0],
        )

    def ring_start(seg):
        exchange(seg, 0).wait()
        mine = grads[seg, place, core].astype(F32) + sib[seg, place].astype(F32)
        sib[seg, place] = mine.astype(BF)
        for way in range(2):
            first_copy(seg, way).start()

    def reduce_tick(seg, s, last):
        if not last:

            @pl.when(s < chips // 2)
            def _():
                exchange(seg, 2 * s + 1).wait()

            @pl.when(s < chips // 2 - 1)
            def _():
                exchange(seg, 2 * s + 2).wait()

        for way in range(2):
            if way == 0:
                k = lax.rem(place + 2 * chips - 1 - s, chips)
            else:
                k = lax.rem(place + 1 + s, chips)
            here = landing(seg, way, s)
            ring(here, here, seg, way, rs_recv.at[seg, way, s]).wait()
            value = (
                here[...].astype(F32)
                + grads[seg, k, core, :, columns(way)].astype(F32)
                + sib[seg, k, :, columns(way)].astype(F32)
            ).astype(BF)
            if last:
                grads[seg, k, core, :, columns(way)] = value
                gather_copy(seg, way, k, 0).start()
                forward_copy(seg, way, k, 0).start()
            else:
                here[...] = value
                ring(
                    here, landing(seg, way, s + 1), seg, way, rs_recv.at[seg, way, s + 1]
                ).start()

    def gather_tick(seg, s, last):
        for way in range(2):
            k = lax.rem(place + chips - s, chips) if way == 0 else lax.rem(place + s, chips)
            gather_copy(seg, way, k, s).wait()
            if not last:
                gather_copy(seg, way, k, s + 1).start()
            forward_copy(seg, way, k, 0).wait_send()
            forward_copy(seg, way, k, s + 1).start()

    def gain_copy(s):
        spot = gain_all.at[lax.rem(place + chips - s, chips)]
        return pltpu.make_async_remote_copy(
            src_ref=spot,
            dst_ref=spot,
            send_sem=gain_send,
            recv_sem=gain_recv.at[s],
            device_id=right,
            device_id_type=MESH,
        )

    gain_swap = pltpu.make_async_remote_copy(
        src_ref=gain_own,
        dst_ref=gain_sib,
        send_sem=gsib_sem.at[0],
        recv_sem=gsib_sem.at[1],
        device_id=sibling,
        device_id_type=MESH,
    )
    gain_own[...] = jnp.zeros_like(gain_own)
    gain_own[0:2, :] = jnp.sum(gain_acc[...], axis=1)
    gain_swap.start()

    def ring_begin(seg):
        if seg == 0:
            pl.semaphore_wait(ready, 2)
            gain_swap.wait()
            gain_all[place] = gain_own[...] + gain_sib[...]
            gain_copy(0).start()
        ring_start(seg)

    def done(block):
        seg, rest = divmod(block + 1, group)
        seg -= 1
        if rest:
            return
        exchange_start(seg)
        if seg > 0:
            ring_begin(seg - 1)

    weight_grads(3, done)
    ring_begin(segments - 1)

    def reduce_step(s, carry):
        for seg in range(segments):
            reduce_tick(seg, s, False)
        @pl.when(s == chips // 2 - 1)
        def _():
            pl.semaphore_signal(freed, inc=1, device_id=sibling, device_id_type=MESH)

        gain_copy(s).wait()
        gain_copy(s + 1).start()
        late_rows(s)
        return carry

    lax.fori_loop(0, chips - 2, reduce_step, 0)
    pl.semaphore_wait(freed, 1)
    for seg in range(segments):
        reduce_tick(seg, chips - 2, True)
    gain_copy(chips - 2).wait()

    def gather_step(s, carry):
        for seg in range(segments):
            gather_tick(seg, s, False)
        late_rows(s + chips - 2)
        return carry

    lax.fori_loop(0, chips - 2, gather_step, 0)
    for seg in range(segments):
        gather_tick(seg, chips - 2, True)

    for i in range(2 * (chips - 2), chunks):
        late_rows(i)

    gains = gain_all[0]
    for k in range(1, chips):
        gains = gains + gain_all[k]
    gain_out[...] = gains[0:2, :]

    def results(seg):
        copies = []
        for block in range(seg * group, (seg + 1) * group):
            kind, c = divmod(block, blocks)
            if kind == 0:
                dst = down_out.at[pl.ds(c * per, per)]
            elif kind == 1:
                dst = up_out.at[:, :, :, c * d : (c + 1) * d]
            elif c < 3:
                dst = qkv_out.at[:, :, :, c * d : (c + 1) * d]
            else:
                dst = out_out
            src = grads.at[seg, pl.ds((block % group) * per, per)]
            copies.append(pltpu.make_async_copy(src, dst, go_sem.at[block]))
        return copies

    for seg in range(segments):
        for way in range(2):
            forward_copy(seg, way, 0, 0).wait_send()

        def arrived(f, carry, seg=seg):
            for way in range(2):
                forward_copy(seg, way, 0, f).wait_recv()
            return carry

        lax.fori_loop(0, chips, arrived, 0)
        for copy in results(seg):
            copy.start()
    for seg in range(segments):
        for copy in results(seg):
            copy.wait()

    def finish(i, carry):
        start = i * CHUNK

        @pl.when(first & (i > 0))
        def _():
            to_second(start, CHUNK).wait_send()

        @pl.when(second)
        def _():
            to_first(start, CHUNK).wait_send()

        @pl.when(second | (i > 0))
        def _():
            store_y(start, CHUNK).wait()

        store_dx(start, CHUNK).wait()
        return carry

    lax.fori_loop(0, chunks, finish, 0)
    for q in range(CHUNK):

        @pl.when(first)
        def _(q=q):
            to_second(q, 1).wait_send()
            store_y(q, 1).wait()


def finish_kernel(parts, *refs):
    count = len(parts)
    sources, results = refs[:count], refs[count : 2 * count]
    lows, wides = refs[2 * count : 3 * count], list(refs[3 * count : -2])
    load_sem, store_sem = refs[-2:]
    pieces = []
    for src, dst, low, steps in zip(sources, results, lows, parts, strict=True):
        wide = low if dst.dtype == low.dtype else wides.pop(0)
        tall = src.shape[0] // steps
        for t in range(0, src.shape[0], tall):
            r = pl.ds(t, tall)
            n = len(pieces)
            load = pltpu.make_async_copy(src.at[r], low.at[r], load_sem.at[n])
            store = pltpu.make_async_copy(wide.at[r], dst.at[r], store_sem.at[n])
            pieces.append((load, store, low, wide, r))
    for load, _, _, _, _ in pieces:
        load.start()
    for load, store, low, wide, r in pieces:
        load.wait()
        if wide is not low:
            wide[r, :] = low[r, :].astype(F32)
        store.start()
    for _, store, _, _, _ in pieces:
        store.wait()


def finish(rows, grads):
    hbm = pl.BlockSpec(memory_space=pl.ANY)
    arrays = (*grads, *rows)
    types = [F32] * len(grads) + [a.dtype for a in rows]
    parts = [4] * len(grads) + [2 if a.shape[0] > 2 else 1 for a in rows]
    return pl.pallas_call(
        functools.partial(finish_kernel, parts),
        in_specs=[hbm] * len(arrays),
        out_specs=[hbm] * len(arrays),
        out_shape=[jax.ShapeDtypeStruct(a.shape, t) for a, t in zip(arrays, types, strict=True)],
        scratch_shapes=[pltpu.VMEM(a.shape, a.dtype) for a in arrays]
        + [pltpu.VMEM(g.shape, F32) for g in grads]
        + [pltpu.SemaphoreType.DMA((sum(parts),))] * 2,
        compiler_params=pltpu.CompilerParams(vmem_limit_bytes=60 * 2**20),
        name="finish",
    )(*arrays)


def local(
    tokens,
    start_steps,
    cond_counts,
    valid_steps,
    qkv_weight,
    out_weight,
    up_weight,
    down_weight,
    norm_gains,
    cotangent,
):
    seqs, slots, d = tokens.shape
    ff = up_weight.shape[2]
    rows = seqs * slots
    chips = lax.axis_size("batch") // 2
    group = 4
    segments = (2 * ff // d + 4) // group
    prow = group * d // (2 * chips)
    per = d // (2 * prow)
    vmem = pl.BlockSpec(memory_space=pltpu.VMEM)
    smem = pl.BlockSpec(memory_space=pltpu.SMEM)
    hbm = pl.BlockSpec(memory_space=pl.ANY)
    y, dx, qkv_grad, out_grad, up_grad, down_grad, gains = pl.pallas_call(
        functools.partial(layer_kernel, seqs, chips),
        out_shape=(
            jax.ShapeDtypeStruct((rows, d), BF),
            jax.ShapeDtypeStruct((rows, d), BF),
            jax.ShapeDtypeStruct((per, 2, prow, 3 * d), BF),
            jax.ShapeDtypeStruct((per, 2, prow, d), BF),
            jax.ShapeDtypeStruct((per, 2, prow, ff), BF),
            jax.ShapeDtypeStruct((ff // (2 * prow), 2, prow, d), BF),
            jax.ShapeDtypeStruct((2, d), F32),
        ),
        in_specs=[smem] * 3 + [hbm] * 6 + [vmem],
        out_specs=(hbm, hbm, hbm, hbm, hbm, hbm, vmem),
        scratch_shapes=[
            pltpu.VMEM((d, 3 * d), BF),
            pltpu.VMEM((d, d), BF),
            pltpu.VMEM((d, ff), BF),
            pltpu.VMEM((ff, d), BF),
            pltpu.VMEM((rows, d), BF),
            pltpu.VMEM((rows, d), BF),
            pltpu.VMEM((rows, d), BF),
            pltpu.VMEM((rows, d), BF),
            pltpu.VMEM((rows, 3 * d), BF),
            pltpu.VMEM((seqs * HEADS // 2, SLOTS, 2 * SLOTS), BF),
            pltpu.VMEM((rows, d), BF),
            pltpu.VMEM((rows, d), BF),
            pltpu.VMEM((rows, ff), BF),
            pltpu.VMEM((rows, ff), BF),
            pltpu.VMEM((rows, d), BF),
            pltpu.VMEM((rows, 1), F32),
            pltpu.VMEM((rows, 1), F32),
            pltpu.VMEM((CHUNK * SLOTS, d), F32),
            pltpu.VMEM((CHUNK * SLOTS, d), BF),
            pltpu.VMEM((CHUNK * SLOTS, 3 * d), BF),
            pltpu.VMEM((d, rows // 4), BF),
            pltpu.VMEM((segments, chips, 2, prow, d), BF),
            pltpu.VMEM((segments, chips, prow, d), BF),
            pltpu.VMEM((2, 8, d), F32),
            pltpu.VMEM((8, d), F32),
            pltpu.VMEM((8, d), F32),
            pltpu.VMEM((chips, 8, d), F32),
            pltpu.SemaphoreType.DMA((2,)),
            pltpu.SemaphoreType.DMA((4,)),
            pltpu.SemaphoreType.DMA((seqs,)),
            pltpu.SemaphoreType.DMA((seqs,)),
            pltpu.SemaphoreType.DMA((seqs,)),
            pltpu.SemaphoreType.DMA((seqs,)),
            pltpu.SemaphoreType.DMA((segments, chips)),
            pltpu.SemaphoreType.DMA((segments, chips)),
            pltpu.SemaphoreType.DMA((segments, 2)),
            pltpu.SemaphoreType.DMA((segments, 2, chips - 1)),
            pltpu.SemaphoreType.DMA((segments, 2, chips - 1)),
            pltpu.SemaphoreType.DMA((segments, 2)),
            pltpu.SemaphoreType.DMA((segments, 2, chips)),
            pltpu.SemaphoreType.DMA,
            pltpu.SemaphoreType.DMA((chips - 1,)),
            pltpu.SemaphoreType.DMA((2,)),
            pltpu.SemaphoreType.DMA((segments * group,)),
            pltpu.SemaphoreType.REGULAR,
            pltpu.SemaphoreType.REGULAR,
        ],
        compiler_params=pltpu.CompilerParams(
            collective_id=0, has_side_effects=True, vmem_limit_bytes=63 * 2**20
        ),
        name="layer",
    )(
        start_steps,
        cond_counts,
        valid_steps,
        tokens.reshape(rows, d),
        cotangent.reshape(rows, d),
        qkv_weight[0],
        out_weight[0],
        up_weight[0],
        down_weight[0],
        norm_gains[0],
    )
    grads = (
        down_grad.reshape(ff, d),
        up_grad.reshape(d, ff),
        qkv_grad.reshape(d, 3 * d),
        out_grad.reshape(d, d),
    )
    down_grad, up_grad, qkv_grad, out_grad, y, dx, gains = finish((y, dx, gains), grads)
    shape = (1, seqs, slots, d)
    return (
        y.reshape(shape),
        dx.reshape(shape),
        qkv_grad[None],
        out_grad[None],
        up_grad[None],
        down_grad[None],
        gains[None],
    )


def solution(mesh):
    rows = P("batch", None, None)
    flat = P("batch")
    layer = P("section", None, None)
    in_specs = (rows, flat, flat, flat, layer, layer, layer, layer, layer, rows)
    both = P("section", "batch", None, None)
    out_specs = (both, both, layer, layer, layer, layer, layer)
    return jax.shard_map(local, mesh=mesh, in_specs=in_specs, out_specs=out_specs, check_vma=False)
```

```python
import functools

import jax
import jax.numpy as jnp
from jax import lax
from jax.experimental import pallas as pl
from jax.experimental.pallas import tpu as pltpu
from jax.sharding import PartitionSpec as P

HEADS = 8
HEAD_DIM = 64
SLOTS = 128
STEP_TOKENS = 6
PAIR = 2 * HEAD_DIM
NEGATIVE = -1e30
EPS = 1e-05
SCALE = HEAD_DIM ** (-0.5)
GELU_A = 0.7978845608028654
GELU_B = 0.7978845608028654 * 0.044715
CHUNK = 2
MESH = pl.DeviceIdType.MESH
BF = jnp.bfloat16
F32 = jnp.float32


def dot(a, b):
    return jnp.dot(a, b, preferred_element_type=F32)


def dot_t(a, b):
    return lax.dot_general(a, b, (((1,), (1,)), ((), ())), preferred_element_type=F32)


def t_dot(a, b):
    return lax.dot_general(a, b, (((0,), (0,)), ((), ())), preferred_element_type=F32)


def layer_kernel(
    seqs,
    chips,
    start_ref,
    cond_ref,
    valid_ref,
    tok_ref,
    cot_ref,
    qkv_in,
    out_in,
    up_in,
    down_in,
    gain_ref,
    y_out,
    dx_out,
    sum_out,
    gain_out,
    qkv_w,
    out_w,
    up_w,
    down_w,
    x_buf,
    d_buf,
    y_buf,
    n1_buf,
    z_buf,
    p_buf,
    o_buf,
    n2_buf,
    act_buf,
    der_buf,
    da_buf,
    rs_buf,
    rs2_buf,
    dh_buf,
    do_buf,
    dz_buf,
    lhs_t,
    grads,
    sib,
    gain_acc,
    gain_own,
    gain_sib,
    gain_all,
    in_sem,
    w_sem,
    send_sem,
    recv_sem,
    yo_sem,
    xo_sem,
    sib_send,
    sib_recv,
    ring_send,
    rs_recv,
    ag_recv,
    fwd_send,
    fwd_recv,
    gain_send,
    gain_recv,
    gsib_sem,
    go_sem,
    ready,
    freed,
):
    section = lax.axis_index("section")
    batch = lax.axis_index("batch")
    first = section == 0
    second = section == 1
    partner = (1 - section, batch)
    core = lax.rem(batch, 2)
    chip = batch // 2
    half_ring = chips // 2
    place = jnp.where(chip % 2 == 0, chip // 2, chips - 1 - chip // 2)

    def at_place(p):
        c = jnp.where(p < half_ring, 2 * p, 2 * (chips - 1 - p) + 1)
        return (section, 2 * c + core)

    right = at_place(lax.rem(place + 1, chips))
    left = at_place(lax.rem(place + chips - 1, chips))
    ahead = (right, left)
    sibling = (section, batch + 1 - 2 * core)
    segments = grads.shape[0]
    prow = grads.shape[3]
    d = x_buf.shape[1]
    ff = act_buf.shape[1]
    rows = CHUNK * SLOTS
    tile = d
    chunks = seqs // CHUNK
    total = seqs * SLOTS

    weights = [
        pltpu.make_async_copy(src, dst, w_sem.at[i])
        for i, (src, dst) in enumerate(
            ((qkv_in, qkv_w), (out_in, out_w), (up_in, up_w), (down_in, down_w))
        )
    ]
    early, late = pl.ds(0, rows), pl.ds(rows, total - rows)
    load_x = pltpu.make_async_copy(tok_ref.at[early], x_buf.at[early], in_sem.at[0])
    load_rest = pltpu.make_async_copy(tok_ref.at[late], x_buf.at[late], in_sem.at[1])
    load_d = pltpu.make_async_copy(cot_ref, d_buf, in_sem.at[0])

    @pl.when(first)
    def _():
        load_x.start()

    for copy in weights:
        copy.start()

    @pl.when(first)
    def _():
        load_rest.start()

    @pl.when(second)
    def _():
        load_d.start()

    barrier = pltpu.get_barrier_semaphore()
    for other in (partner, sibling, left, right):
        pl.semaphore_signal(barrier, inc=1, device_id=other, device_id_type=MESH)

    gain_acc[...] = jnp.zeros_like(gain_acc)
    grads[...] = jnp.zeros_like(grads)

    @pl.when(first)
    def _():
        load_x.wait()

    @pl.when(second)
    def _():
        load_d.wait()

    weights[0].wait()

    lane = lax.broadcasted_iota(jnp.int32, (1, PAIR), 1)
    low = jnp.where(lane < HEAD_DIM, 1.0, 0.0).astype(BF)
    high = jnp.where(lane < HEAD_DIM, 0.0, 1.0).astype(BF)
    head_row = lax.broadcasted_iota(jnp.int32, (2 * SLOTS, PAIR), 0) < SLOTS
    head_lane = lax.broadcasted_iota(jnp.int32, (2 * SLOTS, PAIR), 1) < HEAD_DIM
    minus = jnp.where(head_row == head_lane, -1.0, 0.0).astype(BF)
    scale = jnp.asarray(SCALE, BF)
    key_id = lax.broadcasted_iota(jnp.int32, (SLOTS, SLOTS), 1)
    row_id = lax.broadcasted_iota(jnp.int32, (SLOTS, SLOTS), 0)
    key_step = (key_id * 43) >> 8
    row_step = (row_id * 43) >> 8
    causal = key_step <= row_step
    diagonal = key_id == row_id
    gain0 = gain_ref[0:1, :]
    gain1 = gain_ref[1:2, :]

    def seq_rows(q, n):
        return pl.ds(pl.multiple_of(q * SLOTS, SLOTS), n * SLOTS)

    def to_second(q, n):
        r = seq_rows(q, n)
        return pltpu.make_async_remote_copy(
            src_ref=y_buf.at[r],
            dst_ref=x_buf.at[r],
            send_sem=send_sem.at[q],
            recv_sem=recv_sem.at[q],
            device_id=partner,
            device_id_type=MESH,
        )

    def to_first(q, n):
        r = seq_rows(q, n)
        return pltpu.make_async_remote_copy(
            src_ref=x_buf.at[r],
            dst_ref=d_buf.at[r],
            send_sem=send_sem.at[q],
            recv_sem=recv_sem.at[q],
            device_id=partner,
            device_id_type=MESH,
        )

    def store_y(q, n):
        r = seq_rows(q, n)
        return pltpu.make_async_copy(y_buf.at[r], y_out.at[r], yo_sem.at[q])

    def store_dx(q, n):
        r = seq_rows(q, n)
        return pltpu.make_async_copy(x_buf.at[r], dx_out.at[r], xo_sem.at[q])

    def norm(v, gain):
        mean = jnp.mean(v, axis=-1, keepdims=True)
        c = v - mean
        var = jnp.mean(c * c, axis=-1, keepdims=True)
        rs = lax.rsqrt(var + EPS)
        return (c * rs * gain).astype(BF), rs

    def norm_back(dn, n, gain, rs):
        xhat = n.astype(F32) * (1.0 / gain)
        w = dn * gain
        dgain = jnp.sum((dn * xhat).reshape(-1, 8, d), axis=0)
        m1 = jnp.mean(w, axis=-1, keepdims=True)
        m2 = jnp.mean(w * xhat, axis=-1, keepdims=True)
        return rs * (w - m1 - xhat * m2), dgain

    def halves(v):
        return jnp.concatenate([v * low, v * high], axis=0)

    def turned(v):
        return jnp.concatenate([v[:, :SLOTS].T, v[:, SLOTS:].T], axis=1)

    def forward_attention(start, n):
        r = seq_rows(start, n)
        n1, rs1 = norm(x_buf[r, :].astype(F32), gain0)
        n1_buf[r, :] = n1
        rs_buf[r, :] = rs1
        yield
        for c in range(3):
            z_buf[r, c * d : (c + 1) * d] = dot(n1, qkv_w[:, c * d : (c + 1) * d]).astype(BF)
            yield
        for s in range(n):
            seq = start + s
            rs = pl.ds(pl.multiple_of(seq * SLOTS, SLOTS), SLOTS)
            live = key_id < valid_ref[seq] * STEP_TOKENS
            recent = key_step >= start_ref[seq] - cond_ref[seq]
            allowed = (causal & live & recent) | diagonal
            allowed = jnp.concatenate([allowed, allowed], axis=0)
            for p in range(0, HEADS // 2, 2):
                at = p * PAIR
                q = [z_buf[rs, pl.ds(at + j * PAIR, PAIR)] * scale for j in range(2)]
                k = [halves(z_buf[rs, pl.ds(d + at + j * PAIR, PAIR)]) for j in range(2)]
                v = [halves(z_buf[rs, pl.ds(2 * d + at + j * PAIR, PAIR)]) for j in range(2)]
                nil = jnp.zeros_like(q[0])
                spread = jnp.concatenate(
                    [jnp.concatenate([q[0], nil], axis=1), jnp.concatenate([nil, q[1]], axis=1)],
                    axis=0,
                )
                sc = dot_t(spread, jnp.concatenate(k, axis=1))
                parts = []
                for h in range(2):
                    sh = jnp.where(allowed, sc[:, h * SLOTS : (h + 1) * SLOTS], NEGATIVE)
                    e = jnp.exp(sh - jnp.max(sh, axis=-1, keepdims=True))
                    parts.append((e / jnp.sum(e, axis=-1, keepdims=True)).astype(BF))
                pr = jnp.concatenate(parts, axis=1)
                p_buf[seq * (HEADS // 2) + p] = pr[:SLOTS]
                p_buf[seq * (HEADS // 2) + p + 1] = pr[SLOTS:]
                mixed = dot(pr, jnp.concatenate(v, axis=1)).astype(BF)
                o_buf[rs, at : at + PAIR] = mixed[:SLOTS, :PAIR]
                o_buf[rs, at + PAIR : at + 2 * PAIR] = mixed[SLOTS:, PAIR:]
                yield

    def forward_mlp(start, n, whole):
        r = seq_rows(start, n)
        h = x_buf[r, :].astype(F32) + dot(o_buf[r, :], out_w[...])
        yield
        n2, rs2 = norm(h, gain1)
        n2_buf[r, :] = n2
        rs2_buf[r, :] = rs2
        yield
        acc = h
        if not whole:
            y_buf[r, :] = h.astype(BF)
        for f in range(0, ff, tile // 2):
            part = slice(f, f + tile // 2)
            u = dot(n2, up_w[:, part])
            sq = u * u
            t = jnp.tanh(u * (GELU_A + GELU_B * sq))
            hs = 0.5 + 0.5 * t
            g = u * hs
            act = g.astype(BF)
            act_buf[r, part] = act
            slope = 2.0 * GELU_A + 6.0 * GELU_B * sq
            der_buf[r, part] = (hs + slope * (g - g * hs)).astype(BF)
            if whole:
                acc = acc + dot(act, down_w[part, :])
            yield
        if whole:
            y_buf[r, :] = acc.astype(BF)
        yield

    def backward_mlp(start):
        r = seq_rows(start, CHUNK)
        dm = d_buf[r, :]
        for f in range(0, ff, tile):
            dg = dot_t(dm, down_w[f : f + tile, :])
            der_buf[r, f : f + tile] = (der_buf[r, f : f + tile].astype(F32) * dg).astype(BF)
            yield
        dn2 = dot_t(der_buf[r, :], up_w[...])
        yield
        dh_norm, dgain1 = norm_back(dn2, n2_buf[r, :], gain1, rs2_buf[r, :])
        gain_acc[1] += dgain1
        dh = dm.astype(F32) + dh_norm
        da = dh.astype(BF)
        da_buf[r, :] = da
        yield
        dout = dot_t(da, out_w[...]).astype(BF)
        yield
        dh_buf[...] = dh
        do_buf[...] = dout

    def backward_attention(start):
        r = seq_rows(start, CHUNK)
        for s in range(CHUNK):
            seq = start + s
            rs = pl.ds(pl.multiple_of(seq * SLOTS, SLOTS), SLOTS)
            rc = pl.ds(s * SLOTS, SLOTS)
            pairs = []
            for at in range(0, HEADS // 2, 2):
                for p in (at, at + 1):
                    cq = pl.ds(p * PAIR, PAIR)
                    do = do_buf[rc, cq]
                    pr = p_buf[seq * (HEADS // 2) + p]
                    q = z_buf[rs, cq] * scale
                    k = z_buf[rs, pl.ds(d + p * PAIR, PAIR)] * scale
                    v = z_buf[rs, pl.ds(2 * d + p * PAIR, PAIR)]
                    both = jnp.concatenate([do, do * o_buf[rs, cq]], axis=1)
                    against = jnp.concatenate([halves(v), minus], axis=1)
                    ds = (pr.astype(F32) * dot_t(both, against)).astype(BF)
                    pairs.append((ds, k, turned(ds), q, turned(pr), do))
                    yield
            for at in range(0, HEADS // 2, 2):
                one, two = pairs[at], pairs[at + 1]
                for c in range(3):
                    left_side = jnp.concatenate([one[2 * c], two[2 * c]], axis=0)
                    right_side = jnp.concatenate(
                        [halves(one[2 * c + 1]), halves(two[2 * c + 1])], axis=1
                    )
                    res = dot(left_side, right_side).astype(BF)
                    col = c * d + at * PAIR
                    dz_buf[rc, col : col + PAIR] = res[:SLOTS, :PAIR]
                    dz_buf[rc, col + PAIR : col + 2 * PAIR] = res[SLOTS:, PAIR:]
                    yield
        dz = dz_buf[...]
        z_buf[r, :] = dz
        dn1 = dot_t(dz, qkv_w[...])
        yield
        dx_norm, dgain0 = norm_back(dn1, n1_buf[r, :], gain0, rs_buf[r, :])
        gain_acc[0] += dgain0
        x_buf[r, :] = (dh_buf[...] + dx_norm).astype(BF)
        yield

    def alone(part):
        for _ in part:
            pass

    def together(long, many, short, few):
        done = 0
        for n in range(many):
            next(long, None)
            while done * many < (n + 1) * few:
                next(short, None)
                done += 1
        alone(long)
        alone(short)

    def forward(start, n, to_next):
        if not to_next:
            to_second(start, n).wait_recv()
        alone(forward_attention(start, n))
        if n == 1:

            @pl.when(start == 0)
            def _():
                for copy in weights[1:]:
                    copy.wait()

        alone(forward_mlp(start, n, to_next))
        if to_next:
            if n == 1:

                @pl.when(start == 0)
                def _():
                    pl.semaphore_wait(barrier, 4)

            to_second(start, n).start()
            store_y(start, n).start()

    def late_rows(i):
        @pl.when(second & (i < chunks))
        def _():
            r = seq_rows(i * CHUNK, CHUNK)
            y_buf[r, :] = (y_buf[r, :].astype(F32) + dot(act_buf[r, :], down_w[...])).astype(BF)
            store_y(i * CHUNK, CHUNK).start()

    def backward(start, from_next):
        if from_next:
            to_first(start, CHUNK).wait_recv()
        alone(backward_mlp(start))
        alone(backward_attention(start))
        if not from_next:
            to_first(start, CHUNK).start()
        store_dx(start, CHUNK).start()

    def forward_with_back(start):
        before = start - CHUNK
        to_second(start, CHUNK).wait_recv()
        together(backward_mlp(before), 6, forward_attention(start, CHUNK), 8)
        together(forward_mlp(start, CHUNK, False), 11, backward_attention(before), 22)
        to_first(before, CHUNK).start()
        store_dx(before, CHUNK).start()

    part = total // 4
    blocks = ff // d
    per = d // (2 * prow)

    group = grads.shape[1] * 2 * prow // d

    def put(block, value):
        seg = block // group
        where = pl.ds((block % group) * per, per)
        value = value.reshape(per, 2, prow, d) + grads[seg, where].astype(F32)
        grads[seg, where] = value.astype(BF)

    def weight_grads(quarter, done):
        r = pl.ds(pl.multiple_of(quarter * part, part), part)
        for c in range(blocks):
            lhs_t[...] = act_buf[r, c * d : (c + 1) * d].T
            put(c, dot(lhs_t[...], d_buf[r, :]))
            done(c)
        lhs_t[...] = n2_buf[r, :].T
        for c in range(blocks):
            put(blocks + c, dot(lhs_t[...], der_buf[r, c * d : (c + 1) * d]))
            done(blocks + c)
        lhs_t[...] = n1_buf[r, :].T
        for c in range(3):
            put(2 * blocks + c, dot(lhs_t[...], z_buf[r, c * d : (c + 1) * d]))
            done(2 * blocks + c)
        lhs_t[...] = o_buf[r, :].T
        put(2 * blocks + 3, dot(lhs_t[...], da_buf[r, :]))
        done(2 * blocks + 3)

    per_part = chunks // 4

    def times(low, high, act):
        def body(i, carry):
            act(i)
            return carry

        lax.fori_loop(low, high, body, 0)

    def early_quarter(q):
        weight_grads(q, lambda block: None)

    @pl.when(first)
    def _():
        times(0, CHUNK, lambda q: forward(q, 1, True))
        load_rest.wait()
        times(1, chunks, lambda i: forward(i * CHUNK, CHUNK, True))

        def quarter(q):
            times(0, per_part, lambda j: backward((q * per_part + j) * CHUNK, True))

            @pl.when(q < 3)
            def _():
                early_quarter(q)

        times(0, 4, quarter)

    @pl.when(second)
    def _():
        pl.semaphore_wait(barrier, 4)
        times(0, CHUNK, lambda q: forward(q, 1, False))

        def with_back(i):
            return (i >= 2) & (i < chunks)

        def pair(i):
            @pl.when((i > 0) & jnp.logical_not(with_back(i)))
            def _():
                forward(i * CHUNK, CHUNK, False)

            @pl.when(with_back(i))
            def _():
                forward_with_back(i * CHUNK)

            @pl.when(jnp.logical_not(with_back(i + 1)))
            def _():
                backward(i * CHUNK, False)

        times(0, chunks, pair)
        times(0, 3, early_quarter)

    for other in (left, right):
        pl.semaphore_signal(ready, inc=1, device_id=other, device_id_type=MESH)

    width = d // 2
    per_block = SLOTS // prow

    def columns(way):
        return pl.ds(way * width, width)

    def exchange(seg, j):
        off = (j + 1) // 2
        k = lax.rem(jnp.where(j % 2 == 1, place + chips - off, place + off), chips)
        return pltpu.make_async_remote_copy(
            src_ref=grads.at[seg, k, 1 - core],
            dst_ref=sib.at[seg, k],
            send_sem=sib_send.at[seg, j],
            recv_sem=sib_recv.at[seg, j],
            device_id=sibling,
            device_id_type=MESH,
        )

    def exchange_start(seg):
        lax.fori_loop(0, chips, lambda j, c: (exchange(seg, j).start(), c)[1], 0)

    def landing(seg, way, s):
        q = (seg * 2 + way) * (chips - 1) + s
        row = pl.multiple_of((q % per_block) * prow, prow)
        return p_buf.at[q // per_block, pl.ds(row, prow)]

    def ring(src, dst, seg, way, recv):
        return pltpu.make_async_remote_copy(
            src_ref=src,
            dst_ref=dst,
            send_sem=ring_send.at[seg, way],
            recv_sem=recv,
            device_id=ahead[way],
            device_id_type=MESH,
        )

    def gather_copy(seg, way, k, s):
        spot = grads.at[seg, k, core, :, columns(way)]
        return ring(spot, spot, seg, way, ag_recv.at[seg, way, s])

    def forward_copy(seg, way, k, f):
        spot = grads.at[seg, k, core, :, columns(way)]
        return pltpu.make_async_remote_copy(
            src_ref=spot,
            dst_ref=spot,
            send_sem=fwd_send.at[seg, way],
            recv_sem=fwd_recv.at[seg, way, f],
            device_id=sibling,
            device_id_type=MESH,
        )

    def first_copy(seg, way):
        return ring(
            sib.at[seg, place, :, columns(way)],
            landing(seg, way, 0),
            seg,
            way,
            rs_recv.at[seg, way, 0],
        )

    def ring_start(seg):
        exchange(seg, 0).wait()
        mine = grads[seg, place, core].astype(F32) + sib[seg, place].astype(F32)
        sib[seg, place] = mine.astype(BF)
        for way in range(2):
            first_copy(seg, way).start()

    def reduce_tick(seg, s, last):
        if not last:

            @pl.when(s < chips // 2)
            def _():
                exchange(seg, 2 * s + 1).wait()

            @pl.when(s < chips // 2 - 1)
            def _():
                exchange(seg, 2 * s + 2).wait()

        for way in range(2):
            if way == 0:
                k = lax.rem(place + 2 * chips - 1 - s, chips)
            else:
                k = lax.rem(place + 1 + s, chips)
            here = landing(seg, way, s)
            ring(here, here, seg, way, rs_recv.at[seg, way, s]).wait_recv()
            value = (
                here[...].astype(F32)
                + grads[seg, k, core, :, columns(way)].astype(F32)
                + sib[seg, k, :, columns(way)].astype(F32)
            ).astype(BF)
            ring(here, here, seg, way, rs_recv.at[seg, way, s]).wait_send()
            if last:
                grads[seg, k, core, :, columns(way)] = value
                gather_copy(seg, way, k, 0).start()
                forward_copy(seg, way, k, 0).start()
            else:
                here[...] = value
                ring(
                    here, landing(seg, way, s + 1), seg, way, rs_recv.at[seg, way, s + 1]
                ).start()

    def gather_tick(seg, s, last):
        for way in range(2):
            k = lax.rem(place + chips - s, chips) if way == 0 else lax.rem(place + s, chips)
            gather_copy(seg, way, k, s).wait()
            if not last:
                gather_copy(seg, way, k, s + 1).start()
            forward_copy(seg, way, k, 0).wait_send()
            forward_copy(seg, way, k, s + 1).start()

    def gain_copy(s):
        spot = gain_all.at[lax.rem(place + chips - s, chips)]
        return pltpu.make_async_remote_copy(
            src_ref=spot,
            dst_ref=spot,
            send_sem=gain_send,
            recv_sem=gain_recv.at[s],
            device_id=right,
            device_id_type=MESH,
        )

    gain_swap = pltpu.make_async_remote_copy(
        src_ref=gain_own,
        dst_ref=gain_sib,
        send_sem=gsib_sem.at[0],
        recv_sem=gsib_sem.at[1],
        device_id=sibling,
        device_id_type=MESH,
    )
    gain_own[...] = jnp.zeros_like(gain_own)
    gain_own[0:2, :] = jnp.sum(gain_acc[...], axis=1)
    gain_swap.start()

    def ring_begin(seg):
        if seg == 0:
            pl.semaphore_wait(ready, 2)
            gain_swap.wait()
            gain_all[place] = gain_own[...] + gain_sib[...]
            gain_copy(0).start()
        ring_start(seg)

    def done(block):
        seg, rest = divmod(block + 1, group)
        seg -= 1
        if rest:
            return
        exchange_start(seg)
        if seg > 0:
            ring_begin(seg - 1)

    weight_grads(3, done)
    ring_begin(segments - 1)

    def reduce_step(s, carry):
        for seg in range(segments):
            reduce_tick(seg, s, False)
        @pl.when(s == chips // 2 - 1)
        def _():
            pl.semaphore_signal(freed, inc=1, device_id=sibling, device_id_type=MESH)

        gain_copy(s).wait()
        gain_copy(s + 1).start()
        late_rows(s)
        return carry

    lax.fori_loop(0, chips - 2, reduce_step, 0)
    pl.semaphore_wait(freed, 1)
    for seg in range(segments):
        reduce_tick(seg, chips - 2, True)
    gain_copy(chips - 2).wait()

    def result(seg, k):
        return pltpu.make_async_copy(grads.at[seg, k], sum_out.at[seg, k], go_sem.at[seg, k])

    def keep(j):
        k = lax.rem(place + j, chips)
        on = lax.rem(chips + 1 - j, chips)
        back = lax.rem(j + 1, chips)
        for seg in range(segments):
            forward_copy(seg, 0, k, on).wait_recv()
            forward_copy(seg, 1, k, back).wait_recv()
            result(seg, k).start()

    def gather_step(s, carry):
        for seg in range(segments):
            gather_tick(seg, s, False)
        late_rows(s + chips - 2)

        @pl.when(s == 1)
        def _():
            keep(0)

        @pl.when(s == 2)
        def _():
            keep(1)
            keep(chips - 1)

        @pl.when(s > chips // 2)
        def _():
            keep(s - 1)

        @pl.when(s > chips // 2 + 1)
        def _():
            keep(chips + 1 - s)

        return carry

    lax.fori_loop(0, chips - 2, gather_step, 0)
    for seg in range(segments):
        gather_tick(seg, chips - 2, True)
        forward_copy(seg, 0, 0, 0).wait_send()
        forward_copy(seg, 1, 0, 0).wait_send()
    for c in (chips - 3, chips - 2):
        for j in sorted({c, chips - c}):
            keep(j)
    for i in range(2 * (chips - 2), chunks):
        late_rows(i)

    gains = gain_all[0]
    for k in range(1, chips):
        gains = gains + gain_all[k]
    gain_out[...] = gains[0:2, :]

    for seg in range(segments):
        times(0, chips, lambda k, seg=seg: result(seg, k).wait())

    def finish(i, carry):
        start = i * CHUNK

        @pl.when(first & (i > 0))
        def _():
            to_second(start, CHUNK).wait_send()

        @pl.when(second)
        def _():
            to_first(start, CHUNK).wait_send()

        @pl.when(second | (i > 0))
        def _():
            store_y(start, CHUNK).wait()

        store_dx(start, CHUNK).wait()
        return carry

    lax.fori_loop(0, chunks, finish, 0)
    for q in range(CHUNK):

        @pl.when(first)
        def _(q=q):
            to_second(q, 1).wait_send()
            store_y(q, 1).wait()


def finish_kernel(ff, sums, y, dx, gains, *refs):
    down_out, up_out, qkv_out, out_out, y_out, dx_out, gain_out = refs[:7]
    low, wide, y_buf, dx_buf, gain_buf, load_sem, store_sem = refs[7:]
    segments, chips, _, prow, d = low.shape
    per = d // (2 * prow)
    count = ff // d
    moves = []
    for block in range(wide.shape[0]):
        seg, c = divmod(block, chips // per)
        here = pl.ds(c * per, per)
        kind, c = divmod(block, count)
        if kind == 0:
            dst = down_out.at[pl.ds(c * d, d)]
        elif kind == 1:
            dst = up_out.at[:, pl.ds(c * d, d)]
        elif c < 3:
            dst = qkv_out.at[:, pl.ds(c * d, d)]
        else:
            dst = out_out
        moves.append((sums.at[seg, here], low.at[seg, here], wide.at[block], dst))
    for src, buf, dst in ((y, y_buf, y_out), (dx, dx_buf, dx_out), (gains, gain_buf, gain_out)):
        moves.append((src, buf, buf, dst))
    loads, stores = [], []
    for n, (src, buf, ready, dst) in enumerate(moves):
        loads.append(pltpu.make_async_copy(src, buf, load_sem.at[n]))
        stores.append(pltpu.make_async_copy(ready, dst, store_sem.at[n]))
    for copy in loads:
        copy.start()
    for n, (_, buf, ready, _) in enumerate(moves):
        loads[n].wait()
        if ready is not buf:
            ready[...] = buf[...].reshape(d, d).astype(F32)
        stores[n].start()
    for copy in stores:
        copy.wait()


def finish(sums, y, dx, gains, ff):
    segments, chips, _, prow, d = sums.shape
    hbm = pl.BlockSpec(memory_space=pl.ANY)
    blocks = segments * chips * 2 * prow // d
    shapes = [(ff, d), (d, ff), (d, 3 * d), (d, d)]
    return pl.pallas_call(
        functools.partial(finish_kernel, ff),
        in_specs=[hbm] * 4,
        out_specs=[hbm] * 7,
        out_shape=[jax.ShapeDtypeStruct(shape, F32) for shape in shapes]
        + [jax.ShapeDtypeStruct(a.shape, a.dtype) for a in (y, dx, gains)],
        scratch_shapes=[
            pltpu.VMEM(sums.shape, BF),
            pltpu.VMEM((blocks, d, d), F32),
            pltpu.VMEM(y.shape, y.dtype),
            pltpu.VMEM(dx.shape, dx.dtype),
            pltpu.VMEM(gains.shape, gains.dtype),
            pltpu.SemaphoreType.DMA((blocks + 3,)),
            pltpu.SemaphoreType.DMA((blocks + 3,)),
        ],
        compiler_params=pltpu.CompilerParams(vmem_limit_bytes=60 * 2**20),
        name="finish",
    )(sums, y, dx, gains)


def local(
    tokens,
    start_steps,
    cond_counts,
    valid_steps,
    qkv_weight,
    out_weight,
    up_weight,
    down_weight,
    norm_gains,
    cotangent,
):
    seqs, slots, d = tokens.shape
    ff = up_weight.shape[2]
    rows = seqs * slots
    chips = lax.axis_size("batch") // 2
    group = 4
    segments = (2 * ff // d + 4) // group
    prow = group * d // (2 * chips)
    vmem = pl.BlockSpec(memory_space=pltpu.VMEM)
    smem = pl.BlockSpec(memory_space=pltpu.SMEM)
    hbm = pl.BlockSpec(memory_space=pl.ANY)
    y, dx, sums, gains = pl.pallas_call(
        functools.partial(layer_kernel, seqs, chips),
        out_shape=(
            jax.ShapeDtypeStruct((rows, d), BF),
            jax.ShapeDtypeStruct((rows, d), BF),
            jax.ShapeDtypeStruct((segments, chips, 2, prow, d), BF),
            jax.ShapeDtypeStruct((2, d), F32),
        ),
        in_specs=[smem] * 3 + [hbm] * 6 + [vmem],
        out_specs=(hbm, hbm, hbm, vmem),
        scratch_shapes=[
            pltpu.VMEM((d, 3 * d), BF),
            pltpu.VMEM((d, d), BF),
            pltpu.VMEM((d, ff), BF),
            pltpu.VMEM((ff, d), BF),
            pltpu.VMEM((rows, d), BF),
            pltpu.VMEM((rows, d), BF),
            pltpu.VMEM((rows, d), BF),
            pltpu.VMEM((rows, d), BF),
            pltpu.VMEM((rows, 3 * d), BF),
            pltpu.VMEM((seqs * HEADS // 2, SLOTS, 2 * SLOTS), BF),
            pltpu.VMEM((rows, d), BF),
            pltpu.VMEM((rows, d), BF),
            pltpu.VMEM((rows, ff), BF),
            pltpu.VMEM((rows, ff), BF),
            pltpu.VMEM((rows, d), BF),
            pltpu.VMEM((rows, 1), F32),
            pltpu.VMEM((rows, 1), F32),
            pltpu.VMEM((CHUNK * SLOTS, d), F32),
            pltpu.VMEM((CHUNK * SLOTS, d), BF),
            pltpu.VMEM((CHUNK * SLOTS, 3 * d), BF),
            pltpu.VMEM((d, rows // 4), BF),
            pltpu.VMEM((segments, chips, 2, prow, d), BF),
            pltpu.VMEM((segments, chips, prow, d), BF),
            pltpu.VMEM((2, 8, d), F32),
            pltpu.VMEM((8, d), F32),
            pltpu.VMEM((8, d), F32),
            pltpu.VMEM((chips, 8, d), F32),
            pltpu.SemaphoreType.DMA((2,)),
            pltpu.SemaphoreType.DMA((4,)),
            pltpu.SemaphoreType.DMA((seqs,)),
            pltpu.SemaphoreType.DMA((seqs,)),
            pltpu.SemaphoreType.DMA((seqs,)),
            pltpu.SemaphoreType.DMA((seqs,)),
            pltpu.SemaphoreType.DMA((segments, chips)),
            pltpu.SemaphoreType.DMA((segments, chips)),
            pltpu.SemaphoreType.DMA((segments, 2)),
            pltpu.SemaphoreType.DMA((segments, 2, chips - 1)),
            pltpu.SemaphoreType.DMA((segments, 2, chips - 1)),
            pltpu.SemaphoreType.DMA((segments, 2)),
            pltpu.SemaphoreType.DMA((segments, 2, chips)),
            pltpu.SemaphoreType.DMA,
            pltpu.SemaphoreType.DMA((chips - 1,)),
            pltpu.SemaphoreType.DMA((2,)),
            pltpu.SemaphoreType.DMA((segments, chips)),
            pltpu.SemaphoreType.REGULAR,
            pltpu.SemaphoreType.REGULAR,
        ],
        compiler_params=pltpu.CompilerParams(
            collective_id=0, has_side_effects=True, vmem_limit_bytes=63 * 2**20
        ),
        name="layer",
    )(
        start_steps,
        cond_counts,
        valid_steps,
        tokens.reshape(rows, d),
        cotangent.reshape(rows, d),
        qkv_weight[0],
        out_weight[0],
        up_weight[0],
        down_weight[0],
        norm_gains[0],
    )
    down_grad, up_grad, qkv_grad, out_grad, y, dx, gains = finish(sums, y, dx, gains, ff)
    shape = (1, seqs, slots, d)
    return (
        y.reshape(shape),
        dx.reshape(shape),
        qkv_grad[None],
        out_grad[None],
        up_grad[None],
        down_grad[None],
        gains[None],
    )


def solution(mesh):
    rows = P("batch", None, None)
    flat = P("batch")
    layer = P("section", None, None)
    in_specs = (rows, flat, flat, flat, layer, layer, layer, layer, layer, rows)
    both = P("section", "batch", None, None)
    out_specs = (both, both, layer, layer, layer, layer, layer)
    return jax.shard_map(local, mesh=mesh, in_specs=in_specs, out_specs=out_specs, check_vma=False)
```

```python
import functools

import jax
import jax.numpy as jnp
from jax import lax
from jax.experimental import pallas as pl
from jax.experimental.pallas import tpu as pltpu
from jax.sharding import PartitionSpec as P

HEADS = 8
HEAD_DIM = 64
SLOTS = 128
STEP_TOKENS = 6
PAIR = 2 * HEAD_DIM
NEGATIVE = -1e30
EPS = 1e-05
SCALE = HEAD_DIM ** (-0.5)
GELU_A = 0.7978845608028654
GELU_B = 0.7978845608028654 * 0.044715
CHUNK = 2
MESH = pl.DeviceIdType.MESH
BF = jnp.bfloat16
F32 = jnp.float32


def dot(a, b):
    return jnp.dot(a, b, preferred_element_type=F32)


def dot_t(a, b):
    return lax.dot_general(a, b, (((1,), (1,)), ((), ())), preferred_element_type=F32)


def t_dot(a, b):
    return lax.dot_general(a, b, (((0,), (0,)), ((), ())), preferred_element_type=F32)


def layer_kernel(
    seqs,
    chips,
    start_ref,
    cond_ref,
    valid_ref,
    tok_ref,
    cot_ref,
    qkv_in,
    out_in,
    up_in,
    down_in,
    gain_ref,
    y_out,
    dx_out,
    sum_out,
    gain_out,
    qkv_w,
    out_w,
    up_w,
    down_w,
    x_buf,
    d_buf,
    y_buf,
    n1_buf,
    z_buf,
    p_buf,
    o_buf,
    n2_buf,
    act_buf,
    der_buf,
    da_buf,
    rs_buf,
    rs2_buf,
    dh_buf,
    do_buf,
    dz_buf,
    lhs_t,
    grads,
    sib,
    gain_acc,
    gain_own,
    gain_sib,
    gain_all,
    in_sem,
    w_sem,
    send_sem,
    recv_sem,
    yo_sem,
    xo_sem,
    sib_send,
    sib_recv,
    ring_send,
    rs_recv,
    ag_recv,
    fwd_send,
    fwd_recv,
    gain_send,
    gain_recv,
    gsib_sem,
    go_sem,
    ready,
    freed,
):
    section = lax.axis_index("section")
    batch = lax.axis_index("batch")
    first = section == 0
    second = section == 1
    partner = (1 - section, batch)
    core = lax.rem(batch, 2)
    chip = batch // 2
    half_ring = chips // 2
    place = jnp.where(chip % 2 == 0, chip // 2, chips - 1 - chip // 2)

    def at_place(p):
        c = jnp.where(p < half_ring, 2 * p, 2 * (chips - 1 - p) + 1)
        return (section, 2 * c + core)

    right = at_place(lax.rem(place + 1, chips))
    left = at_place(lax.rem(place + chips - 1, chips))
    ahead = (right, left)
    sibling = (section, batch + 1 - 2 * core)
    segments = grads.shape[0]
    prow = grads.shape[3]
    d = x_buf.shape[1]
    ff = act_buf.shape[1]
    rows = CHUNK * SLOTS
    tile = d
    chunks = seqs // CHUNK
    total = seqs * SLOTS

    weights = [
        pltpu.make_async_copy(src, dst, w_sem.at[i])
        for i, (src, dst) in enumerate(
            ((qkv_in, qkv_w), (out_in, out_w), (up_in, up_w), (down_in, down_w))
        )
    ]
    early, late = pl.ds(0, rows), pl.ds(rows, total - rows)
    load_x = pltpu.make_async_copy(tok_ref.at[early], x_buf.at[early], in_sem.at[0])
    load_rest = pltpu.make_async_copy(tok_ref.at[late], x_buf.at[late], in_sem.at[1])
    load_d = pltpu.make_async_copy(cot_ref, d_buf, in_sem.at[0])

    @pl.when(first)
    def _():
        load_x.start()

    for copy in weights:
        copy.start()

    @pl.when(first)
    def _():
        load_rest.start()

    @pl.when(second)
    def _():
        load_d.start()

    barrier = pltpu.get_barrier_semaphore()
    for other in (partner, sibling, left, right):
        pl.semaphore_signal(barrier, inc=1, device_id=other, device_id_type=MESH)

    gain_acc[...] = jnp.zeros_like(gain_acc)

    @pl.when(first)
    def _():
        load_x.wait()

    @pl.when(second)
    def _():
        load_d.wait()

    weights[0].wait()

    lane = lax.broadcasted_iota(jnp.int32, (1, PAIR), 1)
    low = jnp.where(lane < HEAD_DIM, 1.0, 0.0).astype(BF)
    high = jnp.where(lane < HEAD_DIM, 0.0, 1.0).astype(BF)
    head_row = lax.broadcasted_iota(jnp.int32, (2 * SLOTS, PAIR), 0) < SLOTS
    head_lane = lax.broadcasted_iota(jnp.int32, (2 * SLOTS, PAIR), 1) < HEAD_DIM
    minus = jnp.where(head_row == head_lane, -1.0, 0.0).astype(BF)
    scale = jnp.asarray(SCALE, BF)
    key_id = lax.broadcasted_iota(jnp.int32, (SLOTS, SLOTS), 1)
    row_id = lax.broadcasted_iota(jnp.int32, (SLOTS, SLOTS), 0)
    key_step = (key_id * 43) >> 8
    row_step = (row_id * 43) >> 8
    causal = key_step <= row_step
    diagonal = key_id == row_id
    gain0 = gain_ref[0:1, :]
    gain1 = gain_ref[1:2, :]

    def seq_rows(q, n):
        return pl.ds(pl.multiple_of(q * SLOTS, SLOTS), n * SLOTS)

    def to_second(q, n):
        r = seq_rows(q, n)
        return pltpu.make_async_remote_copy(
            src_ref=y_buf.at[r],
            dst_ref=x_buf.at[r],
            send_sem=send_sem.at[q],
            recv_sem=recv_sem.at[q],
            device_id=partner,
            device_id_type=MESH,
        )

    def to_first(q, n):
        r = seq_rows(q, n)
        return pltpu.make_async_remote_copy(
            src_ref=x_buf.at[r],
            dst_ref=d_buf.at[r],
            send_sem=send_sem.at[q],
            recv_sem=recv_sem.at[q],
            device_id=partner,
            device_id_type=MESH,
        )

    def store_y(q, n):
        r = seq_rows(q, n)
        return pltpu.make_async_copy(y_buf.at[r], y_out.at[r], yo_sem.at[q])

    def store_dx(q, n):
        r = seq_rows(q, n)
        return pltpu.make_async_copy(x_buf.at[r], dx_out.at[r], xo_sem.at[q])

    def norm(v, gain):
        mean = jnp.mean(v, axis=-1, keepdims=True)
        c = v - mean
        var = jnp.mean(c * c, axis=-1, keepdims=True)
        rs = lax.rsqrt(var + EPS)
        return (c * rs * gain).astype(BF), rs

    def norm_back(dn, n, gain, rs):
        xhat = n.astype(F32) * (1.0 / gain)
        w = dn * gain
        dgain = jnp.sum((dn * xhat).reshape(-1, 8, d), axis=0)
        m1 = jnp.mean(w, axis=-1, keepdims=True)
        m2 = jnp.mean(w * xhat, axis=-1, keepdims=True)
        return rs * (w - m1 - xhat * m2), dgain

    def halves(v):
        return jnp.concatenate([v * low, v * high], axis=0)

    def turned(v):
        return jnp.concatenate([v[:, :SLOTS].T, v[:, SLOTS:].T], axis=1)

    def forward_attention(start, n):
        r = seq_rows(start, n)
        n1, rs1 = norm(x_buf[r, :].astype(F32), gain0)
        n1_buf[r, :] = n1
        rs_buf[r, :] = rs1
        yield
        for c in range(3):
            z_buf[r, c * d : (c + 1) * d] = dot(n1, qkv_w[:, c * d : (c + 1) * d]).astype(BF)
            yield
        for s in range(n):
            seq = start + s
            rs = pl.ds(pl.multiple_of(seq * SLOTS, SLOTS), SLOTS)
            live = key_id < valid_ref[seq] * STEP_TOKENS
            recent = key_step >= start_ref[seq] - cond_ref[seq]
            allowed = (causal & live & recent) | diagonal
            allowed = jnp.concatenate([allowed, allowed], axis=0)
            for p in range(0, HEADS // 2, 2):
                at = p * PAIR
                q = [z_buf[rs, pl.ds(at + j * PAIR, PAIR)] * scale for j in range(2)]
                k = [halves(z_buf[rs, pl.ds(d + at + j * PAIR, PAIR)]) for j in range(2)]
                v = [halves(z_buf[rs, pl.ds(2 * d + at + j * PAIR, PAIR)]) for j in range(2)]
                nil = jnp.zeros_like(q[0])
                spread = jnp.concatenate(
                    [jnp.concatenate([q[0], nil], axis=1), jnp.concatenate([nil, q[1]], axis=1)],
                    axis=0,
                )
                sc = dot_t(spread, jnp.concatenate(k, axis=1))
                parts = []
                for h in range(2):
                    sh = jnp.where(allowed, sc[:, h * SLOTS : (h + 1) * SLOTS], NEGATIVE)
                    e = jnp.exp(sh - jnp.max(sh, axis=-1, keepdims=True))
                    parts.append((e / jnp.sum(e, axis=-1, keepdims=True)).astype(BF))
                pr = jnp.concatenate(parts, axis=1)
                p_buf[seq * (HEADS // 2) + p] = pr[:SLOTS]
                p_buf[seq * (HEADS // 2) + p + 1] = pr[SLOTS:]
                mixed = dot(pr, jnp.concatenate(v, axis=1)).astype(BF)
                o_buf[rs, at : at + PAIR] = mixed[:SLOTS, :PAIR]
                o_buf[rs, at + PAIR : at + 2 * PAIR] = mixed[SLOTS:, PAIR:]
                yield

    def forward_mlp(start, n, whole):
        r = seq_rows(start, n)
        h = x_buf[r, :].astype(F32) + dot(o_buf[r, :], out_w[...])
        yield
        n2, rs2 = norm(h, gain1)
        n2_buf[r, :] = n2
        rs2_buf[r, :] = rs2
        yield
        acc = h
        if not whole:
            y_buf[r, :] = h.astype(BF)
        for f in range(0, ff, tile // 2):
            part = slice(f, f + tile // 2)
            u = dot(n2, up_w[:, part])
            sq = u * u
            t = jnp.tanh(u * (GELU_A + GELU_B * sq))
            hs = 0.5 + 0.5 * t
            g = u * hs
            act = g.astype(BF)
            act_buf[r, part] = act
            slope = 2.0 * GELU_A + 6.0 * GELU_B * sq
            der_buf[r, part] = (hs + slope * (g - g * hs)).astype(BF)
            if whole:
                acc = acc + dot(act, down_w[part, :])
            yield
        if whole:
            y_buf[r, :] = acc.astype(BF)
        yield

    def backward_mlp(start):
        r = seq_rows(start, CHUNK)
        dm = d_buf[r, :]
        for f in range(0, ff, tile):
            dg = dot_t(dm, down_w[f : f + tile, :])
            der_buf[r, f : f + tile] = (der_buf[r, f : f + tile].astype(F32) * dg).astype(BF)
            yield
        dn2 = dot_t(der_buf[r, :], up_w[...])
        yield
        dh_norm, dgain1 = norm_back(dn2, n2_buf[r, :], gain1, rs2_buf[r, :])
        gain_acc[1] += dgain1
        dh = dm.astype(F32) + dh_norm
        da = dh.astype(BF)
        da_buf[r, :] = da
        yield
        dout = dot_t(da, out_w[...]).astype(BF)
        yield
        dh_buf[...] = dh
        do_buf[...] = dout

    def backward_attention(start):
        r = seq_rows(start, CHUNK)
        for s in range(CHUNK):
            seq = start + s
            rs = pl.ds(pl.multiple_of(seq * SLOTS, SLOTS), SLOTS)
            rc = pl.ds(s * SLOTS, SLOTS)
            pairs = []
            for at in range(0, HEADS // 2, 2):
                for p in (at, at + 1):
                    cq = pl.ds(p * PAIR, PAIR)
                    do = do_buf[rc, cq]
                    pr = p_buf[seq * (HEADS // 2) + p]
                    q = z_buf[rs, cq] * scale
                    k = z_buf[rs, pl.ds(d + p * PAIR, PAIR)] * scale
                    v = z_buf[rs, pl.ds(2 * d + p * PAIR, PAIR)]
                    both = jnp.concatenate([do, do * o_buf[rs, cq]], axis=1)
                    against = jnp.concatenate([halves(v), minus], axis=1)
                    ds = (pr.astype(F32) * dot_t(both, against)).astype(BF)
                    pairs.append((ds, k, turned(ds), q, turned(pr), do))
                    yield
            for at in range(0, HEADS // 2, 2):
                one, two = pairs[at], pairs[at + 1]
                for c in range(3):
                    left_side = jnp.concatenate([one[2 * c], two[2 * c]], axis=0)
                    right_side = jnp.concatenate(
                        [halves(one[2 * c + 1]), halves(two[2 * c + 1])], axis=1
                    )
                    res = dot(left_side, right_side).astype(BF)
                    col = c * d + at * PAIR
                    dz_buf[rc, col : col + PAIR] = res[:SLOTS, :PAIR]
                    dz_buf[rc, col + PAIR : col + 2 * PAIR] = res[SLOTS:, PAIR:]
                    yield
        dz = dz_buf[...]
        z_buf[r, :] = dz
        dn1 = dot_t(dz, qkv_w[...])
        yield
        dx_norm, dgain0 = norm_back(dn1, n1_buf[r, :], gain0, rs_buf[r, :])
        gain_acc[0] += dgain0
        x_buf[r, :] = (dh_buf[...] + dx_norm).astype(BF)
        yield

    def alone(part):
        for _ in part:
            pass

    def together(long, many, short, few):
        done = 0
        for n in range(many):
            next(long, None)
            while done * many < (n + 1) * few:
                next(short, None)
                done += 1
        alone(long)
        alone(short)

    def forward(start, n, to_next):
        if not to_next:
            to_second(start, n).wait_recv()
        alone(forward_attention(start, n))
        if n == 1:

            @pl.when(start == 0)
            def _():
                for copy in weights[1:]:
                    copy.wait()

        alone(forward_mlp(start, n, to_next))
        if to_next:
            if n == 1:

                @pl.when(start == 0)
                def _():
                    pl.semaphore_wait(barrier, 4)

            to_second(start, n).start()
            store_y(start, n).start()

    def late_rows(i):
        @pl.when(second & (i < chunks))
        def _():
            r = seq_rows(i * CHUNK, CHUNK)
            y_buf[r, :] = (y_buf[r, :].astype(F32) + dot(act_buf[r, :], down_w[...])).astype(BF)
            store_y(i * CHUNK, CHUNK).start()

    def backward(start, from_next):
        if from_next:
            to_first(start, CHUNK).wait_recv()
        alone(backward_mlp(start))
        alone(backward_attention(start))
        if not from_next:
            to_first(start, CHUNK).start()
        store_dx(start, CHUNK).start()

    def forward_with_back(start):
        before = start - CHUNK
        to_second(start, CHUNK).wait_recv()
        together(backward_mlp(before), 6, forward_attention(start, CHUNK), 8)
        together(forward_mlp(start, CHUNK, False), 11, backward_attention(before), 22)
        to_first(before, CHUNK).start()
        store_dx(before, CHUNK).start()

    part = total // 4
    blocks = ff // d
    per = d // (2 * prow)

    group = grads.shape[1] * 2 * prow // d

    def put(block, value):
        seg = block // group
        where = pl.ds((block % group) * per, per)
        value = value.reshape(per, 2, prow, d) + grads[seg, where].astype(F32)
        grads[seg, where] = value.astype(BF)

    def weight_grads(quarter, done):
        r = pl.ds(pl.multiple_of(quarter * part, part), part)
        for c in range(blocks):
            lhs_t[...] = act_buf[r, c * d : (c + 1) * d].T
            put(c, dot(lhs_t[...], d_buf[r, :]))
            done(c)
        lhs_t[...] = n2_buf[r, :].T
        for c in range(blocks):
            put(blocks + c, dot(lhs_t[...], der_buf[r, c * d : (c + 1) * d]))
            done(blocks + c)
        lhs_t[...] = n1_buf[r, :].T
        for c in range(3):
            put(2 * blocks + c, dot(lhs_t[...], z_buf[r, c * d : (c + 1) * d]))
            done(2 * blocks + c)
        lhs_t[...] = o_buf[r, :].T
        put(2 * blocks + 3, dot(lhs_t[...], da_buf[r, :]))
        done(2 * blocks + 3)

    per_part = chunks // 4

    def times(low, high, act):
        def body(i, carry):
            act(i)
            return carry

        lax.fori_loop(low, high, body, 0)

    def early_quarter(q):
        weight_grads(q, lambda block: None)

    @pl.when(first)
    def _():
        times(0, CHUNK, lambda q: forward(q, 1, True))
        load_rest.wait()
        times(1, chunks, lambda i: forward(i * CHUNK, CHUNK, True))
        grads[...] = jnp.zeros_like(grads)

        def quarter(q):
            times(0, per_part, lambda j: backward((q * per_part + j) * CHUNK, True))

            @pl.when(q < 3)
            def _():
                early_quarter(q)

        times(0, 4, quarter)

    @pl.when(second)
    def _():
        grads[...] = jnp.zeros_like(grads)
        pl.semaphore_wait(barrier, 4)
        times(0, CHUNK, lambda q: forward(q, 1, False))

        def with_back(i):
            return (i >= 2) & (i < chunks)

        def pair(i):
            @pl.when((i > 0) & jnp.logical_not(with_back(i)))
            def _():
                forward(i * CHUNK, CHUNK, False)

            @pl.when(with_back(i))
            def _():
                forward_with_back(i * CHUNK)

            @pl.when(jnp.logical_not(with_back(i + 1)))
            def _():
                backward(i * CHUNK, False)

        times(0, chunks, pair)
        times(0, 3, early_quarter)

    for other in (left, right):
        pl.semaphore_signal(ready, inc=1, device_id=other, device_id_type=MESH)

    width = d // 2
    per_block = SLOTS // prow

    def columns(way):
        return pl.ds(way * width, width)

    def exchange(seg, j):
        off = (j + 1) // 2
        k = lax.rem(jnp.where(j % 2 == 1, place + chips - off, place + off), chips)
        return pltpu.make_async_remote_copy(
            src_ref=grads.at[seg, k, 1 - core],
            dst_ref=sib.at[seg, k],
            send_sem=sib_send.at[seg, j],
            recv_sem=sib_recv.at[seg, j],
            device_id=sibling,
            device_id_type=MESH,
        )

    def exchange_start(seg):
        lax.fori_loop(0, chips, lambda j, c: (exchange(seg, j).start(), c)[1], 0)

    def landing(seg, way, s):
        q = (seg * 2 + way) * (chips - 1) + s
        row = pl.multiple_of((q % per_block) * prow, prow)
        return p_buf.at[q // per_block, pl.ds(row, prow)]

    def ring(src, dst, seg, way, recv):
        return pltpu.make_async_remote_copy(
            src_ref=src,
            dst_ref=dst,
            send_sem=ring_send.at[seg, way],
            recv_sem=recv,
            device_id=ahead[way],
            device_id_type=MESH,
        )

    def gather_copy(seg, way, k, s):
        spot = grads.at[seg, k, core, :, columns(way)]
        return ring(spot, spot, seg, way, ag_recv.at[seg, way, s])

    def forward_copy(seg, way, k, f):
        spot = grads.at[seg, k, core, :, columns(way)]
        return pltpu.make_async_remote_copy(
            src_ref=spot,
            dst_ref=spot,
            send_sem=fwd_send.at[seg, way],
            recv_sem=fwd_recv.at[seg, way, f],
            device_id=sibling,
            device_id_type=MESH,
        )

    def first_copy(seg, way):
        return ring(
            sib.at[seg, place, :, columns(way)],
            landing(seg, way, 0),
            seg,
            way,
            rs_recv.at[seg, way, 0],
        )

    def ring_start(seg):
        exchange(seg, 0).wait()
        mine = grads[seg, place, core].astype(F32) + sib[seg, place].astype(F32)
        sib[seg, place] = mine.astype(BF)
        for way in range(2):
            first_copy(seg, way).start()

    def reduce_tick(seg, s, last):
        if not last:

            @pl.when(s < chips // 2)
            def _():
                exchange(seg, 2 * s + 1).wait()

            @pl.when(s < chips // 2 - 1)
            def _():
                exchange(seg, 2 * s + 2).wait()

        for way in range(2):
            if way == 0:
                k = lax.rem(place + 2 * chips - 1 - s, chips)
            else:
                k = lax.rem(place + 1 + s, chips)
            here = landing(seg, way, s)
            ring(here, here, seg, way, rs_recv.at[seg, way, s]).wait_recv()
            value = (
                here[...].astype(F32)
                + grads[seg, k, core, :, columns(way)].astype(F32)
                + sib[seg, k, :, columns(way)].astype(F32)
            ).astype(BF)
            ring(here, here, seg, way, rs_recv.at[seg, way, s]).wait_send()
            if last:
                grads[seg, k, core, :, columns(way)] = value
                gather_copy(seg, way, k, 0).start()
                forward_copy(seg, way, k, 0).start()
            else:
                here[...] = value
                ring(
                    here, landing(seg, way, s + 1), seg, way, rs_recv.at[seg, way, s + 1]
                ).start()

    def gather_tick(seg, s, last):
        for way in range(2):
            k = lax.rem(place + chips - s, chips) if way == 0 else lax.rem(place + s, chips)
            gather_copy(seg, way, k, s).wait()
            if not last:
                gather_copy(seg, way, k, s + 1).start()
            forward_copy(seg, way, k, 0).wait_send()
            forward_copy(seg, way, k, s + 1).start()

    def gain_copy(s):
        spot = gain_all.at[lax.rem(place + chips - s, chips)]
        return pltpu.make_async_remote_copy(
            src_ref=spot,
            dst_ref=spot,
            send_sem=gain_send,
            recv_sem=gain_recv.at[s],
            device_id=right,
            device_id_type=MESH,
        )

    gain_swap = pltpu.make_async_remote_copy(
        src_ref=gain_own,
        dst_ref=gain_sib,
        send_sem=gsib_sem.at[0],
        recv_sem=gsib_sem.at[1],
        device_id=sibling,
        device_id_type=MESH,
    )
    gain_own[...] = jnp.zeros_like(gain_own)
    gain_own[0:2, :] = jnp.sum(gain_acc[...], axis=1)
    gain_swap.start()

    def ring_begin(seg):
        if seg == 0:
            pl.semaphore_wait(ready, 2)
            gain_swap.wait()
            gain_all[place] = gain_own[...] + gain_sib[...]
            gain_copy(0).start()
        ring_start(seg)

    def done(block):
        seg, rest = divmod(block + 1, group)
        seg -= 1
        if rest:
            return
        exchange_start(seg)
        if seg > 0:
            ring_begin(seg - 1)

    weight_grads(3, done)
    ring_begin(segments - 1)

    def reduce_step(s, carry):
        for seg in range(segments):
            reduce_tick(seg, s, False)
        @pl.when(s == chips // 2 - 1)
        def _():
            pl.semaphore_signal(freed, inc=1, device_id=sibling, device_id_type=MESH)

        gain_copy(s).wait()
        gain_copy(s + 1).start()
        late_rows(s)
        return carry

    lax.fori_loop(0, chips - 2, reduce_step, 0)
    pl.semaphore_wait(freed, 1)
    for seg in range(segments):
        reduce_tick(seg, chips - 2, True)
    gain_copy(chips - 2).wait()

    def result(seg, k):
        return pltpu.make_async_copy(grads.at[seg, k], sum_out.at[seg, k], go_sem.at[seg, k])

    def keep(j):
        k = lax.rem(place + j, chips)
        on = lax.rem(chips + 1 - j, chips)
        back = lax.rem(j + 1, chips)
        for seg in range(segments):
            forward_copy(seg, 0, k, on).wait_recv()
            forward_copy(seg, 1, k, back).wait_recv()
            result(seg, k).start()

    def gather_step(s, carry):
        for seg in range(segments):
            gather_tick(seg, s, False)
        late_rows(s + chips - 2)

        @pl.when(s == 1)
        def _():
            keep(0)

        @pl.when(s == 2)
        def _():
            keep(1)
            keep(chips - 1)

        @pl.when(s > chips // 2)
        def _():
            keep(s - 1)

        @pl.when(s > chips // 2 + 1)
        def _():
            keep(chips + 1 - s)

        return carry

    lax.fori_loop(0, chips - 2, gather_step, 0)
    for seg in range(segments):
        gather_tick(seg, chips - 2, True)
        forward_copy(seg, 0, 0, 0).wait_send()
        forward_copy(seg, 1, 0, 0).wait_send()
    for c in (chips - 3, chips - 2):
        for j in sorted({c, chips - c}):
            keep(j)
    for i in range(2 * (chips - 2), chunks):
        late_rows(i)

    gains = gain_all[0]
    for k in range(1, chips):
        gains = gains + gain_all[k]
    gain_out[...] = gains[0:2, :]

    for seg in range(segments):
        times(0, chips, lambda k, seg=seg: result(seg, k).wait())

    def finish(i, carry):
        start = i * CHUNK

        @pl.when(first & (i > 0))
        def _():
            to_second(start, CHUNK).wait_send()

        @pl.when(second)
        def _():
            to_first(start, CHUNK).wait_send()

        @pl.when(second | (i > 0))
        def _():
            store_y(start, CHUNK).wait()

        store_dx(start, CHUNK).wait()
        return carry

    lax.fori_loop(0, chunks, finish, 0)
    for q in range(CHUNK):

        @pl.when(first)
        def _(q=q):
            to_second(q, 1).wait_send()
            store_y(q, 1).wait()


def finish_kernel(ff, sums, y, dx, gains, *refs):
    down_out, up_out, qkv_out, out_out, y_out, dx_out, gain_out = refs[:7]
    low, wide, y_buf, dx_buf, gain_buf, load_sem, store_sem = refs[7:]
    segments, chips, _, prow, d = low.shape
    per = d // (2 * prow)
    count = ff // d
    moves = []
    for block in range(wide.shape[0]):
        seg, c = divmod(block, chips // per)
        here = pl.ds(c * per, per)
        kind, c = divmod(block, count)
        if kind == 0:
            dst = down_out.at[pl.ds(c * d, d)]
        elif kind == 1:
            dst = up_out.at[:, pl.ds(c * d, d)]
        elif c < 3:
            dst = qkv_out.at[:, pl.ds(c * d, d)]
        else:
            dst = out_out
        moves.append((sums.at[seg, here], low.at[seg, here], wide.at[block], dst))
    for src, buf, dst in ((y, y_buf, y_out), (dx, dx_buf, dx_out), (gains, gain_buf, gain_out)):
        moves.append((src, buf, buf, dst))
    loads, stores = [], []
    for n, (src, buf, ready, dst) in enumerate(moves):
        loads.append(pltpu.make_async_copy(src, buf, load_sem.at[n]))
        stores.append(pltpu.make_async_copy(ready, dst, store_sem.at[n]))
    for copy in loads:
        copy.start()
    for n, (_, buf, ready, _) in enumerate(moves):
        loads[n].wait()
        if ready is not buf:
            ready[...] = buf[...].reshape(d, d).astype(F32)
        stores[n].start()
    for copy in stores:
        copy.wait()


def finish(sums, y, dx, gains, ff):
    segments, chips, _, prow, d = sums.shape
    hbm = pl.BlockSpec(memory_space=pl.ANY)
    blocks = segments * chips * 2 * prow // d
    shapes = [(ff, d), (d, ff), (d, 3 * d), (d, d)]
    return pl.pallas_call(
        functools.partial(finish_kernel, ff),
        in_specs=[hbm] * 4,
        out_specs=[hbm] * 7,
        out_shape=[jax.ShapeDtypeStruct(shape, F32) for shape in shapes]
        + [jax.ShapeDtypeStruct(a.shape, a.dtype) for a in (y, dx, gains)],
        scratch_shapes=[
            pltpu.VMEM(sums.shape, BF),
            pltpu.VMEM((blocks, d, d), F32),
            pltpu.VMEM(y.shape, y.dtype),
            pltpu.VMEM(dx.shape, dx.dtype),
            pltpu.VMEM(gains.shape, gains.dtype),
            pltpu.SemaphoreType.DMA((blocks + 3,)),
            pltpu.SemaphoreType.DMA((blocks + 3,)),
        ],
        compiler_params=pltpu.CompilerParams(vmem_limit_bytes=60 * 2**20),
        name="finish",
    )(sums, y, dx, gains)


def local(
    tokens,
    start_steps,
    cond_counts,
    valid_steps,
    qkv_weight,
    out_weight,
    up_weight,
    down_weight,
    norm_gains,
    cotangent,
):
    seqs, slots, d = tokens.shape
    ff = up_weight.shape[2]
    rows = seqs * slots
    chips = lax.axis_size("batch") // 2
    group = 4
    segments = (2 * ff // d + 4) // group
    prow = group * d // (2 * chips)
    vmem = pl.BlockSpec(memory_space=pltpu.VMEM)
    smem = pl.BlockSpec(memory_space=pltpu.SMEM)
    hbm = pl.BlockSpec(memory_space=pl.ANY)
    y, dx, sums, gains = pl.pallas_call(
        functools.partial(layer_kernel, seqs, chips),
        out_shape=(
            jax.ShapeDtypeStruct((rows, d), BF),
            jax.ShapeDtypeStruct((rows, d), BF),
            jax.ShapeDtypeStruct((segments, chips, 2, prow, d), BF),
            jax.ShapeDtypeStruct((2, d), F32),
        ),
        in_specs=[smem] * 3 + [hbm] * 6 + [vmem],
        out_specs=(hbm, hbm, hbm, vmem),
        scratch_shapes=[
            pltpu.VMEM((d, 3 * d), BF),
            pltpu.VMEM((d, d), BF),
            pltpu.VMEM((d, ff), BF),
            pltpu.VMEM((ff, d), BF),
            pltpu.VMEM((rows, d), BF),
            pltpu.VMEM((rows, d), BF),
            pltpu.VMEM((rows, d), BF),
            pltpu.VMEM((rows, d), BF),
            pltpu.VMEM((rows, 3 * d), BF),
            pltpu.VMEM((seqs * HEADS // 2, SLOTS, 2 * SLOTS), BF),
            pltpu.VMEM((rows, d), BF),
            pltpu.VMEM((rows, d), BF),
            pltpu.VMEM((rows, ff), BF),
            pltpu.VMEM((rows, ff), BF),
            pltpu.VMEM((rows, d), BF),
            pltpu.VMEM((rows, 1), F32),
            pltpu.VMEM((rows, 1), F32),
            pltpu.VMEM((CHUNK * SLOTS, d), F32),
            pltpu.VMEM((CHUNK * SLOTS, d), BF),
            pltpu.VMEM((CHUNK * SLOTS, 3 * d), BF),
            pltpu.VMEM((d, rows // 4), BF),
            pltpu.VMEM((segments, chips, 2, prow, d), BF),
            pltpu.VMEM((segments, chips, prow, d), BF),
            pltpu.VMEM((2, 8, d), F32),
            pltpu.VMEM((8, d), F32),
            pltpu.VMEM((8, d), F32),
            pltpu.VMEM((chips, 8, d), F32),
            pltpu.SemaphoreType.DMA((2,)),
            pltpu.SemaphoreType.DMA((4,)),
            pltpu.SemaphoreType.DMA((seqs,)),
            pltpu.SemaphoreType.DMA((seqs,)),
            pltpu.SemaphoreType.DMA((seqs,)),
            pltpu.SemaphoreType.DMA((seqs,)),
            pltpu.SemaphoreType.DMA((segments, chips)),
            pltpu.SemaphoreType.DMA((segments, chips)),
            pltpu.SemaphoreType.DMA((segments, 2)),
            pltpu.SemaphoreType.DMA((segments, 2, chips - 1)),
            pltpu.SemaphoreType.DMA((segments, 2, chips - 1)),
            pltpu.SemaphoreType.DMA((segments, 2)),
            pltpu.SemaphoreType.DMA((segments, 2, chips)),
            pltpu.SemaphoreType.DMA,
            pltpu.SemaphoreType.DMA((chips - 1,)),
            pltpu.SemaphoreType.DMA((2,)),
            pltpu.SemaphoreType.DMA((segments, chips)),
            pltpu.SemaphoreType.REGULAR,
            pltpu.SemaphoreType.REGULAR,
        ],
        compiler_params=pltpu.CompilerParams(
            collective_id=0, has_side_effects=True, vmem_limit_bytes=63 * 2**20
        ),
        name="layer",
    )(
        start_steps,
        cond_counts,
        valid_steps,
        tokens.reshape(rows, d),
        cotangent.reshape(rows, d),
        qkv_weight[0],
        out_weight[0],
        up_weight[0],
        down_weight[0],
        norm_gains[0],
    )
    down_grad, up_grad, qkv_grad, out_grad, y, dx, gains = finish(sums, y, dx, gains, ff)
    shape = (1, seqs, slots, d)
    return (
        y.reshape(shape),
        dx.reshape(shape),
        qkv_grad[None],
        out_grad[None],
        up_grad[None],
        down_grad[None],
        gains[None],
    )


def solution(mesh):
    rows = P("batch", None, None)
    flat = P("batch")
    layer = P("section", None, None)
    in_specs = (rows, flat, flat, flat, layer, layer, layer, layer, layer, rows)
    both = P("section", "batch", None, None)
    out_specs = (both, both, layer, layer, layer, layer, layer)
    return jax.shard_map(local, mesh=mesh, in_specs=in_specs, out_specs=out_specs, check_vma=False)
```
